32 devices in a mesh: dp: 4 (over x, core), expert: 8 (over z, y).
Axes of the slice: x: 2, y: 2, z: 4, core: 2. Of those that a mesh axis runs over, the one named last changes fastest.
Arguments:
- inputs: bfloat16 [2, 16384, 768], P(None, ('dp', 'expert')), may hold values from -6 to 6
- gain_one: bfloat16 [768], P('dp'), may hold values from 0.5 to 1.5
- w_qkv: bfloat16 [768, 2304], P('dp'), may hold values from -0.21875 to 0.21875
- w_out: bfloat16 [768, 768], P('dp'), may hold values from -1.75 to 1.75
- rel_table: bfloat16 [32, 12], P('dp'), may hold values from -4 to 4
- second_norm_gain: bfloat16 [768], P('dp'), may hold values from 0.5 to 1.5
- w_router: bfloat16 [768, 8], P('dp'), may hold values from -0.15625 to 0.15625
- w_in: bfloat16 [8, 768, 3072], P('expert'), may hold values from -0.21875 to 0.21875
- w_back: bfloat16 [8, 3072, 768], P('expert'), may hold values from -0.109375 to 0.109375
- expert_ids: int32 [2, 16384, 2], P(None, ('dp', 'expert')), may hold values from 0 to 7, all different within a row; in each aligned block of 512 rows (0 to 511, 512 to 1023, ..., all dimensions but the last counted through in order) at most 192 rows name the same one
- block_ids: int32 [2, 32, 512], P(None, ('dp', 'expert')), may hold values from 0 to 3, never falling along the last dimension, each value on 1 to 256 neighbouring positions
- cotangent: bfloat16 [2, 16384, 768], P(None, ('dp', 'expert')), may hold values from -6 to 6
Outputs:
- out: bfloat16 [2, 16384, 768], P(None, ('dp', 'expert'))
- grad_inputs: bfloat16 [2, 16384, 768], P(None, ('dp', 'expert'))
- grad_gain_one: float32 [768], P('dp')
- grad_w_qkv: float32 [768, 2304], P('dp')
- grad_w_out: float32 [768, 768], P('dp')
- grad_rel_table: float32 [32, 12], P('dp')
- grad_gain_two: float32 [768], P('dp')
- grad_w_router: float32 [768, 8], P('dp')
- grad_w_in: float32 [8, 768, 3072], P('expert')
- grad_w_back: float32 [8, 3072, 768], P('expert')
The draws below stay inside these ranges and needn't reach their ends.
Inputs may be any that keep to these rules, and one draw needn't show every extreme that they name: `expert_ids`: each token names two different experts; among the tokens of one sequence no expert is named more than 192 times. `block_ids`: along each sequence block ids never fall; each block holds 1 to 256 tokens, one of them exactly 256.
All inputs are finite; a program needn't handle non-finite values.
Results may differ from the reference program's by a relative error of at most 0.02.
Values may be sent and summed in bfloat16 or wider, within the bound.
No kernel may reach another device: no remote copies, remote signals or barrier semaphores. Data moves between devices by JAX's collectives and lax.ppermute only.
A program may use at most 192 MiB of HBM per device.

```python
import math
import jax
import jax.numpy as jnp
import numpy as np
from jax import lax

D = 768
HEADS = 12
HEAD = 64
FF = 3072
BUCKETS = 32
BLOCK = 256
MICRO = 2
TOK_DEV = 512
EXPERTS = 8
SEQUENCES = 32
TOKENS = 16384
CAP = 192


def block_levels(rng, shape, shards, least, high):
    loudness, own = 1.0, jax.random.fold_in(rng, 6)
    for dim, parts in shards:
        draws = jnp.exp(jax.random.uniform(jax.random.fold_in(own, dim), (parts,), jnp.float32, least / len(shards), high / len(shards)))
        loudness = loudness * jnp.repeat(draws, shape[dim] // parts).reshape([-1 if axis == dim else 1 for axis in range(len(shape))])
    return loudness


def length_profile(amount, total, reach, slope):
    loads = [(1 << 20) // math.isqrt(rank ** slope) + 1 for rank in range(2, amount + 1)]
    surplus, given = total - reach - (amount - 1), [1] * (amount - 1)
    while surplus > 0:
        free = [i for i in range(amount - 1) if given[i] < reach]
        whole, left = sum([loads[i] for i in free]), surplus
        for i in free:
            more = min(reach - given[i], max(1, left * loads[i] // whole), surplus)
            given[i] = given[i] + more
            surplus = surplus - more
    return np.array([reach] + given)


def uneven(own_key, count, total, limit, skew):
    if count == 2:
        one = jax.random.randint(own_key, (), max(1, total - limit), min(limit, total - 1) + 1)
        return jnp.stack([one, total - one])
    lengths = jnp.asarray(length_profile(count, total, limit, skew), jnp.int32)
    couples = (count - 1) // 2
    giver, receiver = lengths[1:1 + 2 * couples:2], lengths[2:2 + 2 * couples:2]
    margin = jnp.minimum(giver - 1, limit - receiver)
    passed = jax.random.randint(jax.random.fold_in(own_key, 1), (couples,), 0, 1 << 20) % (margin + 1)
    lengths = lengths.at[1:1 + 2 * couples:2].set(giver - passed).at[2:2 + 2 * couples:2].set(receiver + passed)
    return lengths[jax.random.permutation(jax.random.fold_in(own_key, 2), count)]


def routed_block(key, own, number, rows, count, top, reach, slope):
    order = jax.random.permutation(key, count)
    crowded, ordinary = portions_of(count, rows * top, reach, slope, True), portions_of(count, rows * top, reach, slope, False)
    places = jnp.arange(count)

    def named(lengths, rotation):
        used = int((lengths > 0).sum())
        fixed = max(1, used // 4)
        moved = fixed + (places - fixed + rotation * (used - fixed)) % max(1, count - fixed)
        return jnp.zeros((count,), jnp.int32).at[order[jnp.where(places < fixed, places, moved)]].set(jnp.asarray(lengths, jnp.int32))

    lengths = jnp.where(number % 4 == 0, named(crowded, number // 4), named(ordinary, number - number // 4 - 1))
    mixed = jax.random.permutation(jax.random.fold_in(own, 3), count)
    giver, taker = mixed[0:count // 2 * 2:2], mixed[1:count // 2 * 2:2]
    margin = jnp.minimum(lengths[giver] - 1, reach - lengths[taker]) // 2
    margin = jnp.where((giver == order[0]) | (taker == order[0]) | (lengths[taker] == 0), 0, jnp.maximum(margin, 0))
    moved = jax.random.randint(jax.random.fold_in(own, 4), (count // 2,), 0, 1 << 20) % (margin + 1)
    lengths = lengths.at[giver].add(-moved).at[taker].add(moved)
    members = jnp.searchsorted(jnp.cumsum(lengths), jnp.arange(rows * top), side="right").astype(jnp.int32)
    grid = members.reshape(top, rows).T
    grid = grid[jax.random.permutation(jax.random.fold_in(own, 1), rows)]
    rotation = jax.random.randint(jax.random.fold_in(own, 2), (rows, 1), 0, top)
    return jnp.take_along_axis(grid, (jnp.arange(top)[None, :] + rotation) % top, axis=1)


def portions_of(number_of, total, reach, skew, full):
    loads = [(1 << 20) // math.isqrt(standing ** skew) + 1 for standing in range(1, number_of + 1)]
    largest = reach if full else min(reach, max(-(-total // number_of), total * loads[0] // sum(loads)))
    least = 1 if total - largest >= number_of - 1 else 0
    given, spare = [largest] + [least] * (number_of - 1), total - largest - least * (number_of - 1)
    while spare > 0:
        free = [i for i in range(1, number_of) if given[i] < largest] or [i for i in range(1, number_of) if given[i] < reach]
        pool, budget = sum([loads[i] for i in free]), spare
        for i in free:
            more = min(reach - given[i], max(1, budget * loads[i] // pool), spare)
            given[i] = given[i] + more
            spare = spare - more
    return np.array(given)


def noise(stream_key, shape, deviation, most, cuts=(), kind=jnp.bfloat16):
    gain = block_levels(stream_key, shape, cuts, -0.22, 0.18) if cuts else 1.0
    values = jax.random.normal(stream_key, shape, jnp.float32) * deviation * gain
    return jnp.minimum(jnp.maximum(values, -most), most).astype(kind)


def setup_inputs(seed: int = 0) -> dict:
    key_list = jax.random.split(jax.random.key(seed), 13)
    inputs = noise(key_list[0], (MICRO, TOKENS, D), 1.0, 6.0, ((1, 32),))
    gain_one = jnp.clip(1.0 + 0.1 * jax.random.normal(key_list[1], (D,), jnp.float32), 0.5, 1.5).astype(jnp.bfloat16)
    w_qkv = noise(key_list[2], (D, 3 * D), D ** -0.5, 0.21875, ((0, 4),))
    w_out = noise(key_list[3], (D, D), (D // 64) ** -0.5, 1.75, ((0, 4),))
    rel_table = noise(key_list[4], (BUCKETS, HEADS), 1.0, 4.0, ((0, 4),))
    second_norm_gain = jnp.clip(1.0 + 0.1 * jax.random.normal(key_list[5], (D,), jnp.float32), 0.5, 1.5).astype(jnp.bfloat16)
    w_router = noise(key_list[6], (D, EXPERTS), (2 * D) ** -0.5, 0.15625, ((0, 4),))
    w_in = noise(key_list[7], (EXPERTS, D, FF), D ** -0.5, 0.21875, ((0, 8),))
    w_back = noise(key_list[8], (EXPERTS, FF, D), FF ** -0.5, 0.109375, ((0, 8),))
    expert_ids_keys = jax.random.split(jax.random.fold_in(key_list[9], 1), MICRO * TOKENS // TOK_DEV)
    expert_ids_turns = jax.random.permutation(jax.random.fold_in(key_list[9], 3), MICRO * TOKENS // TOK_DEV)
    expert_ids = jax.vmap(lambda own, number: routed_block(jax.random.fold_in(key_list[9], 2), own, number, TOK_DEV, EXPERTS, 2, CAP, 1))(expert_ids_keys, expert_ids_turns).reshape((MICRO, TOKENS, 2))
    block_ids = jax.vmap(lambda own: jnp.searchsorted(jnp.cumsum(uneven(own, 2 * TOK_DEV // BLOCK, TOK_DEV, BLOCK, 1)), jnp.arange(TOK_DEV), side="right"))(jax.random.split(key_list[10], MICRO * SEQUENCES)).reshape((MICRO, SEQUENCES, TOK_DEV)).astype(jnp.int32)
    cotangent = noise(key_list[11], (MICRO, TOKENS, D), 1.0, 6.0, ((1, 32),))
    return {"inputs": inputs, "gain_one": gain_one, "w_qkv": w_qkv, "w_out": w_out, "rel_table": rel_table, "second_norm_gain": second_norm_gain, "w_router": w_router, "w_in": w_in, "w_back": w_back, "expert_ids": expert_ids, "block_ids": block_ids, "cotangent": cotangent}


epsilon = 1e-06
bucket_edges = (12, 16, 23, 32, 46, 64, 91)
largest_value = lax.Precision.HIGHEST
masked_score = -1e+30

@jax.custom_vjp
def low(v):
    return lax.optimization_barrier(v.astype(jnp.bfloat16)).astype(jnp.float32)

@jax.custom_vjp
def low_back(v):
    return v

def low_keep(v):
    return (low(v), None)

def low_pass(kept, grad):
    return (grad,)

def back_keep(v):
    return (v, None)

def back_low(kept, grad):
    return (low(grad),)
low.defvjp(low_keep, low_pass)
low_back.defvjp(back_keep, back_low)

def buckets(offset):
    distance = jnp.abs(offset)
    far_bucket = 8 + sum(((distance >= edge_value).astype(jnp.int32) for edge_value in bucket_edges))
    return jnp.where(distance < 8, distance, far_bucket) + 16 * (offset > 0).astype(jnp.int32)

def rms_norm(values, gain_vector):
    return values * lax.rsqrt(lax.optimization_barrier(jnp.mean(values * values, axis=-1, keepdims=True)) + epsilon) * gain_vector

def position_bias(first_row, row_count, length, position_bias_lookup):
    query_pos = first_row + lax.broadcasted_iota(jnp.int32, (row_count, length), 0)
    key_pos = lax.broadcasted_iota(jnp.int32, (row_count, length), 1)
    bucket_ids = buckets(key_pos - query_pos)
    levels = lax.broadcasted_iota(jnp.int32, (position_bias_lookup.shape[0], row_count, length), 0)
    expert_indicator = (bucket_ids[None] == levels).astype(position_bias_lookup.dtype)
    return (expert_indicator, jnp.einsum('mty,md->dty', expert_indicator, position_bias_lookup, precision=largest_value))

def attend_one(queries, key_rows, values, block_row, position):
    length = queries.shape[0]
    query_heads = queries.reshape(length, HEADS, HEAD)
    key_heads = key_rows.reshape(length, HEADS, HEAD)
    value_heads = values.reshape(length, HEADS, HEAD)
    products = jnp.einsum('qhd,khd->hqk', query_heads, key_heads, precision=largest_value)
    scores = low_back(products * HEAD ** (-0.5)) + position
    allowed = block_row[None, :] <= block_row[:, None]
    scores = jnp.where(allowed[None], scores, masked_score)
    weights = low(jax.nn.softmax(scores, axis=-1))
    mixed_heads = jnp.einsum('hqk,khd->qhd', weights, value_heads, precision=largest_value)
    return mixed_heads.reshape(length, HEADS * HEAD)

def attention(projected, blocks, position_bias_lookup):
    group_size = math.gcd(SEQUENCES, max(1, 4096 // TOK_DEV))
    shaped = projected.reshape(SEQUENCES // group_size, group_size, TOK_DEV, 3, HEADS * HEAD)
    expert_sorted_index = blocks.reshape(SEQUENCES // group_size, group_size, TOK_DEV)
    position = position_bias(0, TOK_DEV, TOK_DEV, position_bias_lookup)[1]

    def one_sequence(pieces, block_row):
        return attend_one(pieces[:, 0], pieces[:, 1], pieces[:, 2], block_row, position)

    def one_group(grouped):
        return jax.vmap(one_sequence)(grouped[0], grouped[1])
    mixed_rows = lax.map(jax.checkpoint(one_group), (shaped, expert_sorted_index))
    return mixed_rows.reshape(SEQUENCES * TOK_DEV, HEADS * HEAD)

def slots(routes):
    flat_ids = routes.reshape(-1)
    assign = flat_ids.shape[0]
    expert_indicator = (flat_ids[:, None] == jnp.arange(EXPERTS, dtype=jnp.int32)[None, :]).astype(jnp.int32)
    grouped = expert_indicator.reshape(SEQUENCES, 2 * TOK_DEV, EXPERTS)
    earlier = (jnp.cumsum(grouped, axis=1, dtype=jnp.int32) - grouped).reshape(assign, EXPERTS)
    slot_index = lax.optimization_barrier(jnp.sum(earlier * expert_indicator, axis=1, dtype=jnp.int32))
    source = jnp.arange(assign, dtype=jnp.int32) // (2 * TOK_DEV)
    target = (flat_ids * SEQUENCES + source) * CAP + slot_index
    owner_index = jnp.full((EXPERTS * SEQUENCES * CAP,), assign, jnp.int32).at[target].set(jnp.arange(assign, dtype=jnp.int32))
    return (owner_index < assign, jnp.minimum(owner_index, assign - 1))

def expert_block(pieces):
    expert_rows, first_weight, last_weight = pieces
    up_values = low_back(jnp.dot(expert_rows, first_weight, precision=largest_value))
    activated = low(jax.nn.gelu(up_values, approximate=True))
    return low_back(low(jnp.dot(activated, last_weight, precision=largest_value)))

def layer(values, gain_one, w_qkv, w_out, rel_table, second_norm_gain, w_router, w_in, w_back, routes, blocks):
    normed = low(rms_norm(values, gain_one))
    projected = low_back(low(jnp.dot(normed, w_qkv, precision=largest_value)))
    mixed_rows = low_back(low(attention(projected, blocks, rel_table)))
    hidden = values + low_back(jnp.dot(mixed_rows, w_out, precision=largest_value))
    second = low(rms_norm(hidden, second_norm_gain))
    logits = low_back(jnp.dot(second, w_router, precision=largest_value))
    gate_values = jax.nn.softmax(jnp.take_along_axis(logits, routes, axis=1), axis=-1)
    filled, picked = slots(routes)
    expert_rows = jnp.where(filled[:, None], low_back(second[picked // 2]), 0.0)
    produced = lax.map(jax.checkpoint(expert_block), (expert_rows.reshape(EXPERTS, SEQUENCES * CAP, D), w_in, w_back))
    weighted = jnp.where(filled[:, None], gate_values.reshape(-1)[picked][:, None] * produced.reshape(-1, D), 0.0)
    return hidden + jnp.zeros_like(hidden).at[picked // 2].add(weighted)

def reference(inputs, gain_one, w_qkv, w_out, rel_table, second_norm_gain, w_router, w_in, w_back, expert_ids, block_ids, cotangent):
    params = tuple((weight.astype(jnp.float32) for weight in (gain_one, w_qkv, w_out, rel_table, second_norm_gain, w_router, w_in, w_back)))
    totals = tuple((jnp.zeros_like(weight) for weight in params))
    results = []
    input_grads = []
    for micro_index in range(MICRO):
        routes = expert_ids[micro_index]
        blocks = block_ids[micro_index]

        def forward(values, *weight_list):
            return layer(values, *weight_list, routes, blocks)
        result, pullback = jax.vjp(forward, inputs[micro_index].astype(jnp.float32), *params)
        gradients = pullback(cotangent[micro_index].astype(jnp.float32))
        results.append(result.astype(jnp.bfloat16))
        input_grads.append(gradients[0].astype(jnp.bfloat16))
        totals = tuple((earlier_sum + addition for earlier_sum, addition in zip(totals, gradients[1:])))
    return (jnp.stack(results), jnp.stack(input_grads), totals[0], totals[1], totals[2], totals[3], totals[4], totals[5], totals[6], totals[7])
```

```python
import functools

import jax
import jax.numpy as jnp
import numpy as np
from jax import lax
from jax.experimental import pallas as pl
from jax.experimental.pallas import tpu as pltpu
from jax.sharding import PartitionSpec as P

HEAD = 64
PAIR = 2 * HEAD
STRIP = 128
LANES = 128
VMEM_BYTES = 60 * 1024 * 1024

epsilon = 1e-06
bucket_edges = (12, 16, 23, 32, 46, 64, 91)
masked_score = -1e30
gelu_a = float(np.sqrt(2.0 / np.pi))
gelu_b = 0.044715

F32 = jnp.float32
BF16 = jnp.bfloat16


def dot(a, b):
    return jnp.dot(a, b, preferred_element_type=F32)


def dot_nt(a, b):
    return lax.dot_general(a, b, (((1,), (1,)), ((), ())), preferred_element_type=F32)


def dot_tn(a, b):
    return lax.dot_general(a, b, (((0,), (0,)), ((), ())), preferred_element_type=F32)


def iota(shape, dim):
    return lax.broadcasted_iota(jnp.int32, shape, dim)


def hot(mask):
    return jnp.where(mask, 1.0, 0.0).astype(BF16)


def params(**extra):
    return pltpu.CompilerParams(vmem_limit_bytes=VMEM_BYTES, **extra)


def bucket_table(length, buckets):
    offset = np.arange(2 * length) - (length - 1)
    distance = np.abs(offset)
    far = 8 + sum((distance >= edge).astype(np.int32) for edge in bucket_edges)
    bucket = np.where(distance < 8, distance, far) + 16 * (offset > 0)
    table = (bucket[None, :] == np.arange(buckets)[:, None]) & (offset < length)[None, :]
    return table.astype(np.float32)


def strip_kernel(base_ref, out_ref):
    heads, width = base_ref.shape
    for h in range(heads):
        row = jnp.broadcast_to(base_ref[h : h + 1, :], (STRIP, width))
        rolled = pltpu.roll(row, width - (STRIP - 1), 1, stride=1, stride_axis=0)
        out_ref[h] = rolled[:, : width - STRIP].astype(BF16)


def dispatch_kernel(experts, capacity, ids_row_ref, ids_col_ref, cot_ref, row_ref, col_ref, send_ref):
    length = cot_ref.shape[0]
    padded = max(16, experts)
    before = hot(iota((length, length), 0) < iota((length, length), 1))
    level = iota((padded, length), 0)
    first, second = ids_row_ref[0:1, :], ids_row_ref[1:2, :]
    place = dot(hot((level == first) | (level == second)), before).astype(jnp.int32)
    slot = place + level * capacity
    row_first = jnp.sum(jnp.where(level == first, slot, 0), axis=0, keepdims=True)
    row_second = jnp.sum(jnp.where(level == second, slot, 0), axis=0, keepdims=True)
    row_ref[0:1, :] = row_first
    row_ref[1:2, :] = row_second

    after = hot(iota((length, length), 1) < iota((length, length), 0))
    level = iota((length, LANES), 1)
    first, second = ids_col_ref[:, 0:1], ids_col_ref[:, 1:2]
    place = dot(after, hot((level == first) | (level == second)))
    slot = place + (level * capacity).astype(F32)
    col_ref[:, 0:1] = jnp.sum(jnp.where(level == first, slot, 0.0), axis=1, keepdims=True).astype(jnp.int32)
    col_ref[:, 1:2] = jnp.sum(jnp.where(level == second, slot, 0.0), axis=1, keepdims=True).astype(jnp.int32)
    scatter_rows(row_first, row_second, cot_ref[...], send_ref)


def scatter_rows(row_first, row_second, values, send_ref):
    total, length = send_ref.shape[0], values.shape[0]
    step = 256
    for start in range(0, total, step):
        slots = iota((step, length), 0) + start
        pick = hot((slots == row_first) | (slots == row_second))
        send_ref[start : start + step, :] = dot(pick, values).astype(BF16)


def fill_pick(col_ref, pick_ref):
    length, total = pick_ref.shape
    first, second = col_ref[:, 0:1], col_ref[:, 1:2]
    step = 256
    for start in range(0, total, step):
        slots = iota((length, step), 1) + start
        pick_ref[:, start : start + step] = hot((slots == first) | (slots == second))


def head_mask(length):
    return iota((length, PAIR), 1) < HEAD


def forward_kernel(
    x_ref, gains_ref, weight_ref, strip_ref, block_row_ref, block_col_ref, row_ref,
    proj_ref, mixed_ref, total_ref, hidden_ref, send_ref,
):
    length, width = x_ref.shape
    scale = HEAD ** (-0.5)
    x = x_ref[...].astype(F32)
    r1 = lax.rsqrt(jnp.mean(x * x, axis=1, keepdims=True) + epsilon)
    normed = (x * r1 * gains_ref[0:1, :]).astype(BF16)
    proj_ref[...] = dot(normed, weight_ref[:, : 3 * width]).astype(BF16)

    def pair(p, carry):
        lanes = pl.multiple_of(p * PAIR, PAIR)
        q = proj_ref[:, pl.ds(lanes, PAIR)]
        k = proj_ref[:, pl.ds(width + lanes, PAIR)]
        v = proj_ref[:, pl.ds(2 * width + lanes, PAIR)]
        left = head_mask(length)
        zero = jnp.zeros_like(k)
        outs = [None] * (length // STRIP)
        for h in range(2):
            keep = left if h == 0 else jnp.logical_not(left)
            kh = jnp.where(keep, k, zero)
            vh = jnp.where(keep, v, zero)
            strip = strip_ref[2 * p + h].astype(F32)
            for i in range(length // STRIP):
                rows = slice(i * STRIP, (i + 1) * STRIP)
                start = length - STRIP - i * STRIP
                s = dot_nt(q[rows], kh) * scale + strip[:, start : start + length]
                s = jnp.where(block_row_ref[...] <= block_col_ref[rows, :], s, masked_score)
                top = jnp.max(s, axis=1, keepdims=True)
                e = jnp.exp(s - top)
                total = jnp.sum(e, axis=1, keepdims=True)
                weights = (e * (1.0 / total)).astype(BF16)
                total_ref[2 * p + h, rows, :] = top + jnp.log(total)
                part = dot(weights, vh)
                outs[i] = part if outs[i] is None else outs[i] + part
        for i, part in enumerate(outs):
            mixed_ref[i * STRIP : (i + 1) * STRIP, pl.ds(lanes, PAIR)] = part.astype(BF16)
        return carry

    lax.fori_loop(0, width // PAIR, pair, 0)
    hidden = x + dot(mixed_ref[...], weight_ref[:, 3 * width : 4 * width])
    hidden_ref[...] = hidden
    r2 = lax.rsqrt(jnp.mean(hidden * hidden, axis=1, keepdims=True) + epsilon)
    second = (hidden * r2 * gains_ref[1:2, :]).astype(BF16)
    scatter_rows(row_ref[0:1, :], row_ref[1:2, :], second, send_ref)


def backward_kernel(
    back_ref, col_ref, cot_ref, hidden_ref, gains_ref, weight_ref, proj_ref, total_ref, strip_ref,
    block_row_ref, block_col_ref, x_ref,
    grad_x_ref, branch_ref, grad_proj_ref, normed_ref, grad_gain_ref, diagonal_ref,
    pick_ref, grad_mixed_ref, low_ref, prob_ref, strip_sum_ref,
):
    length, width = cot_ref.shape
    scale = HEAD ** (-0.5)
    fill_pick(col_ref, pick_ref)
    grad_second = dot(pick_ref[...], back_ref[...])
    hidden = hidden_ref[...]
    r2 = lax.rsqrt(jnp.mean(hidden * hidden, axis=1, keepdims=True) + epsilon)
    scaled = grad_second * gains_ref[1:2, :]
    inner = jnp.mean(hidden * scaled, axis=1, keepdims=True)
    grad_hidden = cot_ref[...].astype(F32) + r2 * scaled - hidden * (r2 * r2 * r2 * inner)
    grad_gain_ref[1:2, :] = jnp.sum(grad_second * hidden * r2, axis=0, keepdims=True)
    branch = grad_hidden.astype(BF16)
    branch_ref[...] = branch
    grad_mixed_ref[...] = dot_nt(branch, weight_ref[:, 3 * width : 4 * width]).astype(BF16)

    def pair(p, carry):
        lanes = pl.multiple_of(p * PAIR, PAIR)
        q = proj_ref[:, pl.ds(lanes, PAIR)]
        k = proj_ref[:, pl.ds(width + lanes, PAIR)]
        v = proj_ref[:, pl.ds(2 * width + lanes, PAIR)]
        g = grad_mixed_ref[:, pl.ds(lanes, PAIR)]
        q_turned = q.astype(F32).T.astype(BF16)
        g_turned = g.astype(F32).T.astype(BF16)
        left = head_mask(length)
        zero = jnp.zeros_like(k)
        outs = [None] * (length // STRIP)
        keys, values = [], []
        for h in range(2):
            keep = left if h == 0 else jnp.logical_not(left)
            kh = jnp.where(keep, k, zero)
            vh = jnp.where(keep, v, zero)
            strip = strip_ref[2 * p + h].astype(F32)
            strip_sum_ref[...] = jnp.zeros_like(strip_sum_ref)
            for i in range(length // STRIP):
                rows = slice(i * STRIP, (i + 1) * STRIP)
                start = length - STRIP - i * STRIP
                s = dot_nt(q[rows], kh) * scale + strip[:, start : start + length]
                s = jnp.where(block_row_ref[...] <= block_col_ref[rows, :], s, masked_score)
                prob = jnp.exp(s - total_ref[2 * p + h, rows, :])
                grad_prob = dot_nt(g[rows], vh)
                row_inner = jnp.sum(prob * grad_prob, axis=1, keepdims=True)
                grad_score = prob * (grad_prob - row_inner)
                strip_sum_ref[:, start : start + length] += grad_score
                low = grad_score.astype(BF16)
                low_ref[rows, :] = low
                prob_ref[rows, :] = prob.astype(BF16)
                part = dot(low, kh)
                outs[i] = part if outs[i] is None else outs[i] + part
            half = slice(h * HEAD, (h + 1) * HEAD)
            keys.append(dot(q_turned[half], low_ref[...]))
            values.append(dot(g_turned[half], prob_ref[...]))
            gathered = jnp.zeros((8, 2 * length), F32)
            for a in range(STRIP // 8):
                piece = strip_sum_ref[8 * a : 8 * a + 8, :]
                gathered += pltpu.roll(piece, STRIP - 8 - 8 * a, 1) if a < STRIP // 8 - 1 else piece
            line = gathered[7:8]
            for b in range(7):
                line += pltpu.roll(gathered[b : b + 1], 7 - b, 1)
            diagonal_ref[pl.ds(2 * p + h, 1), :] = line
        for i, part in enumerate(outs):
            grad_proj_ref[i * STRIP : (i + 1) * STRIP, pl.ds(lanes, PAIR)] = (part * scale).astype(BF16)
        grad_key = jnp.concatenate(keys, axis=0).T
        grad_value = jnp.concatenate(values, axis=0).T
        grad_proj_ref[:, pl.ds(width + lanes, PAIR)] = (grad_key * scale).astype(BF16)
        grad_proj_ref[:, pl.ds(2 * width + lanes, PAIR)] = grad_value.astype(BF16)
        return carry

    lax.fori_loop(0, width // PAIR, pair, 0)
    x = x_ref[...].astype(F32)
    r1 = lax.rsqrt(jnp.mean(x * x, axis=1, keepdims=True) + epsilon)
    normed_ref[...] = (x * r1 * gains_ref[0:1, :]).astype(BF16)
    grad_normed = dot_nt(grad_proj_ref[...], weight_ref[:, : 3 * width])
    scaled = grad_normed * gains_ref[0:1, :]
    inner = jnp.mean(x * scaled, axis=1, keepdims=True)
    grad_gain_ref[0:1, :] = jnp.sum(grad_normed * x * r1, axis=0, keepdims=True)
    grad_x_ref[...] = (grad_hidden + r1 * scaled - x * (r1 * r1 * r1 * inner)).astype(BF16)


def expert_kernel(
    rows_ref, cot_ref, ids_ref, mine_ref, router_ref, router_turned_ref, first_ref, last_ref,
    out_ref, back_ref, act_ref, grad_up_ref, scaled_ref, grad_router_ref,
    gate_ref, other_ref, out_acc, back_acc,
):
    step = pl.program_id(0)
    total = rows_ref.shape[0]
    sources, length = ids_ref.shape[1], ids_ref.shape[2]
    capacity = total // sources
    mine = mine_ref[0, 0]
    tile = 512

    @pl.when(step == 0)
    def _():
        first, second = ids_ref[0], ids_ref[1]
        named = (first == mine) | (second == mine)
        before = hot(iota((length, length), 0) < iota((length, length), 1))
        place = dot(hot(named), before).astype(jnp.int32)
        slot = jnp.where(named, place, -1)
        partner = jnp.where(first == mine, second, first).astype(F32)
        for s in range(sources):
            here = iota((capacity, length), 0) == slot[s : s + 1, :]
            other_ref[s * capacity : (s + 1) * capacity, :] = jnp.sum(
                jnp.where(here, partner[s : s + 1, :], 0.0), axis=1, keepdims=True
            ).astype(jnp.int32)
        lane = iota((total, LANES), 1)
        logits = dot(rows_ref[...], router_ref[...])
        gap = jnp.sum(
            jnp.where(lane == mine, logits, 0.0) - jnp.where(lane == other_ref[...], logits, 0.0),
            axis=1, keepdims=True,
        )
        small = jnp.exp(-jnp.abs(gap))
        gate = jnp.where(gap >= 0, 1.0, small) / (1.0 + small)
        gate_ref[...] = gate
        scaled_ref[...] = (gate * cot_ref[...].astype(F32)).astype(BF16)

    first_weight, last_weight = first_ref[...], last_ref[...]

    def row_tile(t, carry):
        at = pl.ds(pl.multiple_of(t * tile, tile), tile)
        rows = rows_ref[at, :]
        scaled = scaled_ref[at, :]
        up = dot(rows, first_weight)
        grad_act = dot_nt(scaled, last_weight)
        square = up * up
        half = 0.5 * jnp.tanh(up * (gelu_a + (gelu_a * gelu_b) * square)) + 0.5
        act = up * half
        slope = half + (act * (1.0 - half)) * (2 * gelu_a + (6 * gelu_a * gelu_b) * square)
        act_low = act.astype(BF16)
        grad_up = (grad_act * slope).astype(BF16)
        act_ref[at, :] = act_low
        grad_up_ref[at, :] = grad_up
        out_part = dot(act_low, last_weight)
        back_part = dot_nt(grad_up, first_weight)

        @pl.when(step == 0)
        def _():
            out_acc[at, :] = out_part
            back_acc[at, :] = back_part

        @pl.when(step > 0)
        def _():
            out_acc[at, :] += out_part
            back_acc[at, :] += back_part

        return carry

    lax.fori_loop(0, total // tile, row_tile, 0)

    @pl.when(step == pl.num_programs(0) - 1)
    def _():
        grad_router = jnp.zeros(grad_router_ref.shape, F32)
        for t in range(total // tile):
            at = slice(t * tile, (t + 1) * tile)
            produced = out_acc[at, :].astype(BF16).astype(F32)
            gate = gate_ref[at, :]
            out_ref[at, :] = (gate * produced).astype(BF16)
            grad_gate = jnp.sum(cot_ref[at, :].astype(F32) * produced, axis=1, keepdims=True)
            share = gate * (1.0 - gate) * grad_gate
            lane = iota((tile, LANES), 1)
            signed = jnp.where(lane == mine, share, 0.0) - jnp.where(lane == other_ref[at, :], share, 0.0)
            high = signed.astype(BF16)
            rest = (signed - high.astype(F32)).astype(BF16)
            routed = dot(high, router_turned_ref[...]) + dot(rest, router_turned_ref[...])
            back_ref[at, :] = (back_acc[at, :] + routed).astype(BF16)
            rows = rows_ref[at, :]
            grad_router = grad_router + dot_tn(rows, high) + dot_tn(rows, rest)
        grad_router_ref[...] = grad_router


def pair_grad_kernel(a0_ref, a1_ref, b0_ref, b1_ref, out_ref):
    out_ref[...] = (dot_tn(a0_ref[...], b0_ref[...]) + dot_tn(a1_ref[...], b1_ref[...])).astype(BF16)


def dense_grad_kernel(n0, n1, g0, g1, m0, m1, b0, b1, small, out_ref):
    width = n0.shape[1]
    for start in range(0, 3 * width, width):
        cols = slice(start, start + width)
        out_ref[:, cols] = (dot_tn(n0[...], g0[:, cols]) + dot_tn(n1[...], g1[:, cols])).astype(BF16)
    out_ref[:, 3 * width : 4 * width] = (dot_tn(m0[...], b0[...]) + dot_tn(m1[...], b1[...])).astype(BF16)
    out_ref[:, 4 * width :] = small[...]


def combine_kernel(out_ref, col_ref, hidden_ref, result_ref, pick_ref):
    fill_pick(col_ref, pick_ref)
    result_ref[...] = (hidden_ref[...] + dot(pick_ref[...], out_ref[...])).astype(BF16)


def cost(flops, byte_count, transcendentals=0):
    return pl.CostEstimate(flops=int(flops), bytes_accessed=int(byte_count), transcendentals=int(transcendentals))


def shaped(shape, dtype):
    return jax.ShapeDtypeStruct(shape, dtype)


def make_strip(base):
    heads, width = base.shape
    return pl.pallas_call(
        strip_kernel,
        out_shape=shaped((heads, STRIP, width - STRIP), BF16),
        compiler_params=params(),
        cost_estimate=cost(1e8, 4e6),
    )(base)


def dispatch(ids, cot, experts, capacity):
    length, width = cot.shape
    total = experts * capacity
    return pl.pallas_call(
        functools.partial(dispatch_kernel, experts, capacity),
        out_shape=(
            shaped((2, length), jnp.int32),
            shaped((length, 2), jnp.int32),
            shaped((total, width), BF16),
        ),
        compiler_params=params(),
        cost_estimate=cost(2 * total * length * width, 4e6),
    )(ids.T, ids, cot)


def forward(x, gains, weight, strip, block_row, block_col, row_slots, total):
    length, width = x.shape
    heads = width // HEAD
    return pl.pallas_call(
        forward_kernel,
        out_shape=(
            shaped((length, 3 * width), BF16),
            shaped((length, width), BF16),
            shaped((heads, length, 1), F32),
            shaped((length, width), F32),
            shaped((total, width), BF16),
        ),
        compiler_params=params(),
        cost_estimate=cost(
            2 * length * width * 4 * width + 8 * heads * length * length * HEAD + 2 * total * length * width,
            24e6, heads * length * length,
        ),
    )(x, gains, weight, strip, block_row, block_col, row_slots)


def backward(back, col, cot, hidden, gains, weight, proj, totals, strip, block_row, block_col, x):
    length, width = x.shape
    heads = width // HEAD
    total = back.shape[0]
    return pl.pallas_call(
        backward_kernel,
        out_shape=(
            shaped((length, width), BF16),
            shaped((length, width), BF16),
            shaped((length, 3 * width), BF16),
            shaped((length, width), BF16),
            shaped((2, width), F32),
            shaped((heads, 2 * length), F32),
        ),
        scratch_shapes=[
            pltpu.VMEM((length, total), BF16),
            pltpu.VMEM((length, width), BF16),
            pltpu.VMEM((length, length), BF16),
            pltpu.VMEM((length, length), BF16),
            pltpu.VMEM((STRIP, 2 * length), F32),
        ],
        compiler_params=params(),
        cost_estimate=cost(
            2 * length * width * 4 * width + 20 * heads * length * length * HEAD + 2 * total * length * width,
            30e6, heads * length * length,
        ),
    )(back, col, cot, hidden, gains, weight, proj, totals, strip, block_row, block_col, x)


def expert(rows, cot, ids, mine, router, router_turned, first, last):
    total, width = rows.shape
    inner = first.shape[1]
    step = 512
    whole = lambda shape: pl.BlockSpec(shape, lambda f: (0,) * len(shape))
    return pl.pallas_call(
        expert_kernel,
        grid=(inner // step,),
        in_specs=[
            whole(rows.shape), whole(cot.shape), whole(ids.shape),
            pl.BlockSpec(memory_space=pltpu.SMEM),
            whole(router.shape), whole(router_turned.shape),
            pl.BlockSpec((width, step), lambda f: (0, f)),
            pl.BlockSpec((step, width), lambda f: (f, 0)),
        ],
        out_specs=(
            whole((total, width)), whole((total, width)),
            pl.BlockSpec((total, step), lambda f: (0, f)),
            pl.BlockSpec((total, step), lambda f: (0, f)),
            whole((total, width)), whole((width, LANES)),
        ),
        out_shape=(
            shaped((total, width), BF16), shaped((total, width), BF16),
            shaped((total, inner), BF16), shaped((total, inner), BF16),
            shaped((total, width), BF16), shaped((width, LANES), F32),
        ),
        scratch_shapes=[
            pltpu.VMEM((total, 1), F32),
            pltpu.VMEM((total, 1), jnp.int32),
            pltpu.VMEM((total, width), F32),
            pltpu.VMEM((total, width), F32),
        ],
        compiler_params=params(dimension_semantics=("arbitrary",)),
        cost_estimate=cost(8 * total * width * inner, 40e6, total * inner),
    )(rows, cot, ids, mine, router, router_turned, first, last)


def pair_grad(a0, a1, b0, b1, split_left):
    total, left = a0.shape
    right = b0.shape[1]
    step = 512
    if split_left:
        grid, a_spec = (left // step,), pl.BlockSpec((total, step), lambda f: (0, f))
        b_spec = pl.BlockSpec((total, right), lambda f: (0, 0))
        out_spec = pl.BlockSpec((step, right), lambda f: (f, 0))
    else:
        grid, a_spec = (right // step,), pl.BlockSpec((total, left), lambda f: (0, 0))
        b_spec = pl.BlockSpec((total, step), lambda f: (0, f))
        out_spec = pl.BlockSpec((left, step), lambda f: (0, f))
    return pl.pallas_call(
        pair_grad_kernel,
        grid=grid,
        in_specs=[a_spec, a_spec, b_spec, b_spec],
        out_specs=out_spec,
        out_shape=shaped((left, right), BF16),
        compiler_params=params(dimension_semantics=("arbitrary",)),
        cost_estimate=cost(4 * total * left * right, 30e6),
    )(a0, a1, b0, b1)


def dense_grad(*arrays):
    small = arrays[-1]
    width = arrays[0].shape[1]
    length = arrays[0].shape[0]
    return pl.pallas_call(
        dense_grad_kernel,
        out_shape=shaped((width, 4 * width + small.shape[1]), BF16),
        compiler_params=params(),
        cost_estimate=cost(4 * length * width * 4 * width, 20e6),
    )(*arrays)


def combine(out_rows, col, hidden):
    length, width = hidden.shape
    total = out_rows.shape[0]
    return pl.pallas_call(
        combine_kernel,
        out_shape=shaped((length, width), BF16),
        scratch_shapes=[pltpu.VMEM((length, total), BF16)],
        compiler_params=params(),
        cost_estimate=cost(2 * total * length * width, 6e6),
    )(out_rows, col, hidden)


def body(
    dp, inputs, gain_one, w_qkv, w_out, rel_table, second_norm_gain, w_router, w_in, w_back,
    expert_ids, block_ids, cotangent,
):
    micro, length, width = inputs.shape
    experts = w_router.shape[1]
    capacity = 3 * length // experts
    total = experts * capacity
    buckets, heads = rel_table.shape[0] * dp, rel_table.shape[1]
    shard = gain_one.shape[0]
    first_in, last_out = w_in[0], w_back[0]
    mine = lax.axis_index("expert").astype(jnp.int32).reshape(1, 1)

    def exchange(rows):
        return lax.all_to_all(
            rows.reshape(experts, capacity, width), "expert", split_axis=0, concat_axis=0, tiled=True
        ).reshape(total, width)

    table_column = jnp.pad(rel_table.reshape(-1), (0, shard - rel_table.size))
    small = jnp.concatenate([gain_one[:, None], second_norm_gain[:, None], table_column[:, None], w_router], axis=1)
    small = jnp.pad(small, ((0, 0), (0, LANES - small.shape[1])))
    packed = lax.all_gather(jnp.concatenate([w_qkv, w_out, small], axis=1), "dp", axis=0, tiled=True)
    extra = packed[:, 4 * width :]
    gains = extra[:, :2].astype(F32).T
    table = extra[:, 2].reshape(dp, shard)[:, : rel_table.size].reshape(buckets, heads)
    router = jnp.pad(extra[:, 3 : 3 + experts], ((0, 0), (0, LANES - experts)))
    router_turned = router.T
    levels = bucket_table(length, buckets)
    base = lax.dot_general(
        table, jnp.asarray(levels, BF16), (((0,), (0,)), ((), ())), preferred_element_type=F32
    )
    ids_row = jnp.transpose(expert_ids, (0, 2, 1))
    ids_all = lax.all_gather(ids_row, "expert", axis=0, tiled=False)
    ids_all = jnp.transpose(ids_all, (1, 2, 0, 3))
    strip = make_strip(base)

    slots, cot_rows = [], []
    for m in range(micro):
        row, col, send = dispatch(expert_ids[m], cotangent[m], experts, capacity)
        slots.append((row, col))
        cot_rows.append(exchange(send))

    kept, rows = [], []
    for m in range(micro):
        block_row, block_col = block_ids[m], block_ids[m].reshape(length, 1)
        proj, mixed, totals, hidden, send = forward(
            inputs[m], gains, packed, strip, block_row, block_col, slots[m][0], total
        )
        kept.append((proj, mixed, totals, hidden, block_row, block_col))
        rows.append(exchange(send))

    expert_outs = []
    for m in range(micro):
        expert_outs.append(
            expert(rows[m], cot_rows[m], ids_all[m], mine, router, router_turned, first_in, last_out)
        )
    backs = [exchange(expert_outs[m][1]) for m in range(micro)]
    weighted = [exchange(expert_outs[m][0]) for m in range(micro)]

    grad_last = pair_grad(
        expert_outs[0][2], expert_outs[1][2], expert_outs[0][4], expert_outs[1][4], True
    )
    grad_first = pair_grad(rows[0], rows[1], expert_outs[0][3], expert_outs[1][3], False)
    grad_last = lax.psum(grad_last, "dp").astype(F32)
    grad_first = lax.psum(grad_first, "dp").astype(F32)
    grad_router = lax.psum(expert_outs[0][5][:, :experts] + expert_outs[1][5][:, :experts], ("dp", "expert"))
    grad_router = lax.dynamic_slice_in_dim(grad_router, lax.axis_index("dp") * shard, shard, 0)

    back_outs = []
    for m in range(micro):
        proj, mixed, totals, hidden, block_row, block_col = kept[m]
        back_outs.append(
            backward(
                backs[m], slots[m][1], cotangent[m], hidden, gains, packed, proj, totals, strip,
                block_row, block_col, inputs[m],
            )
        )
    results = [combine(weighted[m], slots[m][1], kept[m][3]) for m in range(micro)]

    gain_grads = back_outs[0][4] + back_outs[1][4]
    diagonals = back_outs[0][5] + back_outs[1][5]
    table_grad = lax.dot_general(
        jnp.asarray(levels, F32), diagonals, (((1,), (1,)), ((), ())),
        precision=lax.Precision.HIGHEST, preferred_element_type=F32,
    )
    table_grad = jnp.pad(table_grad.reshape(dp, rel_table.size), ((0, 0), (0, shard - rel_table.size)))
    small_grad = jnp.concatenate([gain_grads.T, table_grad.reshape(width, 1)], axis=1).astype(BF16)
    small_grad = jnp.pad(small_grad, ((0, 0), (0, LANES - small_grad.shape[1])))
    dense = dense_grad(
        back_outs[0][3], back_outs[1][3], back_outs[0][2], back_outs[1][2],
        kept[0][1], kept[1][1], back_outs[0][1], back_outs[1][1], small_grad,
    )
    dense = lax.psum_scatter(dense, "dp", scatter_dimension=0, tiled=True)
    dense = lax.psum(dense, "expert").astype(F32)
    tail = dense[:, 4 * width :]
    return (
        jnp.stack(results),
        jnp.stack([out[0] for out in back_outs]),
        tail[:, 0],
        dense[:, : 3 * width],
        dense[:, 3 * width : 4 * width],
        tail[: rel_table.size, 2].reshape(rel_table.shape),
        tail[:, 1],
        grad_router,
        grad_first[None],
        grad_last[None],
    )


def solution(mesh):
    split = P(None, ("dp", "expert"), None)
    in_specs = (
        split, P("dp"), P("dp", None), P("dp", None), P("dp", None), P("dp"), P("dp", None),
        P("expert", None, None), P("expert", None, None), split, split, split,
    )
    out_specs = (
        split, split, P("dp"), P("dp", None), P("dp", None), P("dp", None), P("dp"), P("dp", None),
        P("expert", None, None), P("expert", None, None),
    )
    return jax.shard_map(
        functools.partial(body, mesh.shape["dp"]), mesh=mesh, in_specs=in_specs, out_specs=out_specs, check_vma=False
    )
```

```python
import functools

import jax
import jax.numpy as jnp
import numpy as np
from jax import lax
from jax.experimental import pallas as pl
from jax.experimental.pallas import tpu as pltpu
from jax.sharding import PartitionSpec as P

HEAD = 64
PAIR = 2 * HEAD
STRIP = 128
LANES = 128
VMEM_BYTES = 60 * 1024 * 1024
SCALE = 5
VECTOR = pl.BlockSpec(memory_space=pltpu.VMEM)
SCALAR = pl.BlockSpec(memory_space=pltpu.SMEM)
ANYWHERE = pl.BlockSpec(memory_space=pl.ANY)

epsilon = 1e-06
bucket_edges = (12, 16, 23, 32, 46, 64, 91)
masked_score = -1e30
gelu_a = float(np.sqrt(2.0 / np.pi))
gelu_b = 0.044715

F32 = jnp.float32
BF16 = jnp.bfloat16


def dot(a, b):
    return jnp.dot(a, b, preferred_element_type=F32)


def dot_nt(a, b):
    return lax.dot_general(a, b, (((1,), (1,)), ((), ())), preferred_element_type=F32)


def dot_tn(a, b):
    return lax.dot_general(a, b, (((0,), (0,)), ((), ())), preferred_element_type=F32)


def iota(shape, dim):
    return lax.broadcasted_iota(jnp.int32, shape, dim)


def hot(mask):
    return jnp.where(mask, 1.0, 0.0).astype(BF16)


def params(**extra):
    return pltpu.CompilerParams(vmem_limit_bytes=VMEM_BYTES, **extra)


def bucket_table(length, buckets):
    offset = np.arange(2 * length) - (length - 1)
    distance = np.abs(offset)
    far = 8 + sum((distance >= edge).astype(np.int32) for edge in bucket_edges)
    bucket = np.where(distance < 8, distance, far) + 16 * (offset > 0)
    table = (bucket[None, :] == np.arange(buckets)[:, None]) & (offset < length)[None, :]
    return table.astype(np.float32)


def strip_kernel(base_ref, out_ref):
    heads, width = base_ref.shape
    for h in range(heads):
        row = jnp.broadcast_to(base_ref[h : h + 1, :], (STRIP, width))
        rolled = pltpu.roll(row, width - (STRIP - 1), 1, stride=1, stride_axis=0)
        out_ref[h] = rolled[:, : width - STRIP].astype(BF16)


def slots_kernel(experts, near, capacity, ids_row_ref, ids_col_ref, far_row_ref, far_col_ref, mine_ref, row_ref, row_far_ref, col_ref, col_far_ref):
    length = ids_row_ref.shape[1]
    base = mine_ref[0, 0] // near * near
    padded = max(16, experts)
    before = hot(iota((length, length), 0) < iota((length, length), 1))
    for ids_row, row_out in ((ids_row_ref, row_ref), (far_row_ref, row_far_ref)):
        level = iota((padded, length), 0)
        first, second = ids_row[0:1, :], ids_row[1:2, :]
        place = dot(hot((level == first) | (level == second)), before).astype(jnp.int32)
        block = level - base
        slot = jnp.where((block >= 0) & (block < near), place + block * capacity, -1)
        row_out[0:1, :] = jnp.sum(jnp.where(level == first, slot, 0), axis=0, keepdims=True)
        row_out[1:2, :] = jnp.sum(jnp.where(level == second, slot, 0), axis=0, keepdims=True)

    after = hot(iota((length, length), 1) < iota((length, length), 0))
    for ids_col, col_out in ((ids_col_ref, col_ref), (far_col_ref, col_far_ref)):
        level = iota((length, LANES), 1)
        first, second = ids_col[:, 0:1], ids_col[:, 1:2]
        slot = dot(after, hot((level == first) | (level == second))) + (level * capacity).astype(F32)
        col_out[:, 0:1] = jnp.sum(jnp.where(level == first, slot, 0.0), axis=1, keepdims=True).astype(jnp.int32)
        col_out[:, 1:2] = jnp.sum(jnp.where(level == second, slot, 0.0), axis=1, keepdims=True).astype(jnp.int32)


def scatter_kernel(picks, *refs):
    count = len(picks)
    slots, refs, send_ref = refs[:count], refs[count:-1], refs[-1]
    values = []
    for part in picks:
        values.append([ref if pick is None else ref.at[pick] for pick, ref in zip(part, refs)])
        refs = refs[len(part) :]
    scatter_parts(slots, values, send_ref)


def scatter_parts(slot_refs, value_refs, send_ref):
    near, length = send_ref.shape[0], slot_refs[0].shape[1]
    count = len(slot_refs)
    capacity = send_ref.shape[1] // count
    for n in range(count):
        first, second = slot_refs[n][0:1, :], slot_refs[n][1:2, :]
        values = [ref[...] for ref in value_refs[n]]
        for d in range(near):
            slots = iota((capacity, length), 0) + d * capacity
            pick = hot((slots == first) | (slots == second))
            total, start = None, 0
            for value in values:
                part = dot(pick[:, start : start + value.shape[0]], value)
                total = part if total is None else total + part
                start += value.shape[0]
            send_ref[d, n * capacity : (n + 1) * capacity, :] = total.astype(BF16)


def fill_pick(col_ref, pick_ref, offset=0):
    length, total = pick_ref.shape
    first, second = col_ref[:, 0:1] - offset, col_ref[:, 1:2] - offset
    step = 256
    for start in range(0, total, step):
        slots = iota((length, step), 1) + start
        pick_ref[:, start : start + step] = hot((slots == first) | (slots == second))


def gather_kernel(first_ref, second_ref, mine_ref, blocks_ref, first_sum_ref, second_sum_ref, pick_ref, near_ref):
    near, pair_rows, _ = blocks_ref.shape
    capacity = pair_rows // 2
    offset = mine_ref[0, 0] // near * near * capacity
    for part, (col_ref, sum_ref) in enumerate(((first_ref, first_sum_ref), (second_ref, second_sum_ref))):
        fill_pick(col_ref, pick_ref, offset)
        for d in range(near):
            near_ref[d * capacity : (d + 1) * capacity, :] = blocks_ref[d, part * capacity : (part + 1) * capacity, :]
        sum_ref[...] = dot(pick_ref[...], near_ref[...]).astype(BF16)


def head_mask(length):
    return iota((length, PAIR), 1) < HEAD


def forward_kernel(
    m, x_ref, gains_ref, weight_ref, strip_ref, block_row_ref, block_col_ref, row_ref,
    proj_ref, mixed_ref, total_ref, hidden_ref, second_ref, send_ref,
):
    _, length, width = x_ref.shape
    scale = HEAD ** (-0.5)
    x = x_ref[m].astype(F32)
    r1 = lax.rsqrt(jnp.mean(x * x, axis=1, keepdims=True) + epsilon)
    normed = (x * r1 * gains_ref[0:1, :]).astype(BF16)
    proj_ref[...] = dot(normed, weight_ref[:, : 3 * width]).astype(BF16)

    def pair(p, carry):
        lanes = pl.multiple_of(p * PAIR, PAIR)
        q = proj_ref[:, pl.ds(lanes, PAIR)]
        k = proj_ref[:, pl.ds(width + lanes, PAIR)]
        v = proj_ref[:, pl.ds(2 * width + lanes, PAIR)]
        left = head_mask(length)
        zero = jnp.zeros_like(k)
        outs = [None] * (length // STRIP)
        for h in range(2):
            keep = left if h == 0 else jnp.logical_not(left)
            kh = jnp.where(keep, k, zero)
            vh = jnp.where(keep, v, zero)
            strip = strip_ref[2 * p + h].astype(F32)
            for i in range(length // STRIP):
                rows = slice(i * STRIP, (i + 1) * STRIP)
                start = length - STRIP - i * STRIP
                s = dot_nt(q[rows], kh) * scale + strip[:, start : start + length]
                s = jnp.where(block_row_ref[m] <= block_col_ref[rows, m : m + 1], s, masked_score)
                top = jnp.max(s, axis=1, keepdims=True)
                e = jnp.exp(s - top)
                total = jnp.sum(e, axis=1, keepdims=True)
                weights = (e * (1.0 / total)).astype(BF16)
                total_ref[2 * p + h, rows, :] = top + jnp.log(total)
                part = dot(weights, vh)
                outs[i] = part if outs[i] is None else outs[i] + part
        for i, part in enumerate(outs):
            mixed_ref[i * STRIP : (i + 1) * STRIP, pl.ds(lanes, PAIR)] = part.astype(BF16)
        return carry

    lax.fori_loop(0, width // PAIR, pair, 0)
    hidden = x + dot(mixed_ref[...], weight_ref[:, 3 * width : 4 * width])
    hidden_ref[...] = hidden
    r2 = lax.rsqrt(jnp.mean(hidden * hidden, axis=1, keepdims=True) + epsilon)
    second_ref[...] = (hidden * r2 * gains_ref[1:2, :]).astype(BF16)
    scatter_parts([row_ref], [[second_ref]], send_ref)


def backward_kernel(near, part, *refs):
    backward_main(part, refs[:near], *refs[near:])


def backward_main(
    part, far_refs, own_ref, mine_ref, col_ref, cot_ref, hidden_ref, gains_ref, weight_ref, proj_ref, total_ref, strip_ref,
    block_row_ref, block_col_ref, x_ref,
    grad_x_ref, branch_ref, grad_proj_ref, normed_ref, grad_gain_ref, diagonal_ref,
    pick_ref, back_ref, grad_mixed_ref, low_ref, prob_ref, strip_sum_ref,
):
    _, length, width = cot_ref.shape
    scale = HEAD ** (-0.5)
    near, capacity = own_ref.shape[0], own_ref.shape[1] // 2
    mine = mine_ref[0, 0]
    base = mine // near * near
    for d in range(near):
        own = own_ref[d, part * capacity : (part + 1) * capacity, :]
        back_ref[pl.ds(pl.multiple_of((base + d) * capacity, 16), capacity), :] = own
        back_ref[pl.ds(pl.multiple_of((mine ^ (near | d)) * capacity, 16), capacity), :] = far_refs[d][...]
    fill_pick(col_ref, pick_ref)
    grad_second = dot(pick_ref[...], back_ref[...])
    hidden = hidden_ref[...]
    r2 = lax.rsqrt(jnp.mean(hidden * hidden, axis=1, keepdims=True) + epsilon)
    scaled = grad_second * gains_ref[1:2, :]
    inner = jnp.mean(hidden * scaled, axis=1, keepdims=True)
    grad_hidden = cot_ref[part].astype(F32) + r2 * scaled - hidden * (r2 * r2 * r2 * inner)
    grad_gain_ref[1:2, :] = jnp.sum(grad_second * hidden * r2, axis=0, keepdims=True)
    branch = grad_hidden.astype(BF16)
    branch_ref[...] = branch
    grad_mixed_ref[...] = dot_nt(branch, weight_ref[:, 3 * width : 4 * width]).astype(BF16)

    m = part

    def pair(p, carry):
        lanes = pl.multiple_of(p * PAIR, PAIR)
        q = proj_ref[:, pl.ds(lanes, PAIR)]
        k = proj_ref[:, pl.ds(width + lanes, PAIR)]
        v = proj_ref[:, pl.ds(2 * width + lanes, PAIR)]
        g = grad_mixed_ref[:, pl.ds(lanes, PAIR)]
        q_turned = q.astype(F32).T.astype(BF16)
        g_turned = g.astype(F32).T.astype(BF16)
        left = head_mask(length)
        zero = jnp.zeros_like(k)
        outs = [None] * (length // STRIP)
        keys, values = [], []
        for h in range(2):
            keep = left if h == 0 else jnp.logical_not(left)
            kh = jnp.where(keep, k, zero)
            vh = jnp.where(keep, v, zero)
            strip = strip_ref[2 * p + h].astype(F32)
            strip_sum_ref[...] = jnp.zeros_like(strip_sum_ref)
            for i in range(length // STRIP):
                rows = slice(i * STRIP, (i + 1) * STRIP)
                start = length - STRIP - i * STRIP
                s = dot_nt(q[rows], kh) * scale + strip[:, start : start + length]
                s = jnp.where(block_row_ref[m] <= block_col_ref[rows, m : m + 1], s, masked_score)
                prob = jnp.exp(s - total_ref[2 * p + h, rows, :])
                grad_prob = dot_nt(g[rows], vh)
                row_inner = jnp.sum(prob * grad_prob, axis=1, keepdims=True)
                grad_score = prob * (grad_prob - row_inner)
                strip_sum_ref[:, start : start + length] += grad_score
                low = grad_score.astype(BF16)
                low_ref[rows, :] = low
                prob_ref[rows, :] = prob.astype(BF16)
                part = dot(low, kh)
                outs[i] = part if outs[i] is None else outs[i] + part
            half = slice(h * HEAD, (h + 1) * HEAD)
            keys.append(dot(q_turned[half], low_ref[...]))
            values.append(dot(g_turned[half], prob_ref[...]))
            gathered = jnp.zeros((8, 2 * length), F32)
            for a in range(STRIP // 8):
                piece = strip_sum_ref[8 * a : 8 * a + 8, :]
                gathered += pltpu.roll(piece, STRIP - 8 - 8 * a, 1) if a < STRIP // 8 - 1 else piece
            line = gathered[7:8]
            for b in range(7):
                line += pltpu.roll(gathered[b : b + 1], 7 - b, 1)
            diagonal_ref[pl.ds(2 * p + h, 1), :] = line
        for i, part in enumerate(outs):
            grad_proj_ref[i * STRIP : (i + 1) * STRIP, pl.ds(lanes, PAIR)] = (part * scale).astype(BF16)
        grad_key = jnp.concatenate(keys, axis=0).T
        grad_value = jnp.concatenate(values, axis=0).T
        grad_proj_ref[:, pl.ds(width + lanes, PAIR)] = (grad_key * scale).astype(BF16)
        grad_proj_ref[:, pl.ds(2 * width + lanes, PAIR)] = grad_value.astype(BF16)
        return carry

    lax.fori_loop(0, width // PAIR, pair, 0)
    x = x_ref[part].astype(F32)
    r1 = lax.rsqrt(jnp.mean(x * x, axis=1, keepdims=True) + epsilon)
    normed_ref[...] = (x * r1 * gains_ref[0:1, :]).astype(BF16)
    grad_normed = dot_nt(grad_proj_ref[...], weight_ref[:, : 3 * width])
    scaled = grad_normed * gains_ref[0:1, :]
    inner = jnp.mean(x * scaled, axis=1, keepdims=True)
    grad_gain_ref[0:1, :] = jnp.sum(grad_normed * x * r1, axis=0, keepdims=True)
    grad_x_ref[...] = (grad_hidden + r1 * scaled - x * (r1 * r1 * r1 * inner)).astype(BF16)


def expert_kernel(
    kind, near, alias, part, *refs,
):
    sent_ref, cots_ref, ids_ref, mine_ref, router_ref, router_turned_ref, first_ref, last_ref = refs[:8]
    refs = refs[8 + alias :]
    back_refs, refs = refs[: near if kind else 1], refs[near if kind else 1 :]
    all_ref, act_ref, grad_up_ref, scaled_ref, grad_router_ref = refs[:5]
    gate_ref, other_ref, out_acc, back_acc, slot_ref, partner_ref, out_ref, back_ref, sem = refs[5:]
    step = pl.program_id(0)
    total = scaled_ref.shape[0]
    _, sources, length = ids_ref.shape
    capacity = total // near
    mine = mine_ref[0, 0]
    base = mine // near * near
    tile = total

    @pl.when(step == 0)
    def _():
        first, second = ids_ref[0], ids_ref[1]
        named = (first == mine) | (second == mine)
        before = hot(iota((length, length), 0) < iota((length, length), 1))
        place = dot(hot(named), before).astype(jnp.int32)
        slot_ref[...] = jnp.where(named, place, -1)
        partner_ref[...] = jnp.where(first == mine, second, first).astype(F32)
        for d in range(near):
            at = slice(d * capacity, (d + 1) * capacity)
            source = pl.ds((base + d) ^ (kind * near), 1)
            here = iota((capacity, length), 0) == slot_ref[source, :]
            other_ref[at, :] = jnp.sum(
                jnp.where(here, partner_ref[source, :], 0.0), axis=1, keepdims=True
            ).astype(jnp.int32)
        lane = iota((total, LANES), 1)
        logits = dot(sent_ref[...].reshape(total, -1), router_ref[...])
        gap = jnp.sum(
            jnp.where(lane == mine, logits, 0.0) - jnp.where(lane == other_ref[...], logits, 0.0),
            axis=1, keepdims=True,
        )
        small = jnp.exp(-jnp.abs(gap))
        gate = jnp.where(gap >= 0, 1.0, small) / (1.0 + small)
        gate_ref[...] = gate
        scaled_ref[...] = (gate * cots_ref[...].reshape(total, -1).astype(F32)).astype(BF16)

    first_weight, last_weight = first_ref[...], last_ref[...]
    rows = sent_ref[...].reshape(total, -1)
    scaled = scaled_ref[...]
    up = dot(rows, first_weight)
    grad_act = dot_nt(scaled, last_weight)
    square = up * up
    half = 0.5 * jnp.tanh(up * (gelu_a + (gelu_a * gelu_b) * square)) + 0.5
    act = up * half
    slope = half + (act * (1.0 - half)) * (2 * gelu_a + (6 * gelu_a * gelu_b) * square)
    act_low = act.astype(BF16)
    grad_up = (grad_act * slope).astype(BF16)
    act_ref[...] = act_low
    grad_up_ref[...] = grad_up
    out_part = dot(act_low, last_weight)
    back_part = dot_nt(grad_up, first_weight)

    @pl.when(step == 0)
    def _():
        out_acc[...] = out_part
        back_acc[...] = back_part

    @pl.when(step > 0)
    def _():
        out_acc[...] += out_part
        back_acc[...] += back_part

    @pl.when(step == pl.num_programs(0) - 1)
    def _():
        grad_router = jnp.zeros(grad_router_ref.shape, F32)
        copies = []
        for d in range(near):
            at = slice(d * capacity, (d + 1) * capacity)
            produced = out_acc[at, :].astype(BF16).astype(F32)
            gate = gate_ref[at, :]
            here = pl.ds(part * capacity, capacity)
            out_ref[at, :] = (gate * produced).astype(BF16)
            copies.append(pltpu.make_async_copy(out_ref.at[at, :], all_ref.at[d, here, :], sem.at[0, d]))
            copies[-1].start()
            grad_gate = jnp.sum(cots_ref[d].astype(F32) * produced, axis=1, keepdims=True)
            share = gate * (1.0 - gate) * grad_gate
            lane = iota((capacity, LANES), 1)
            signed = jnp.where(lane == mine, share, 0.0) - jnp.where(lane == other_ref[at, :], share, 0.0)
            high = signed.astype(BF16)
            rest = (signed - high.astype(F32)).astype(BF16)
            routed = dot(high, router_turned_ref[...]) + dot(rest, router_turned_ref[...])
            back = (back_acc[at, :] + routed).astype(BF16)
            if kind:
                for e in range(near):
                    @pl.when((mine % near) ^ d == e)
                    def _():
                        back_refs[e][...] = back
            else:
                back_ref[at, :] = back
                copies.append(pltpu.make_async_copy(back_ref.at[at, :], back_refs[0].at[d, here, :], sem.at[1, d]))
                copies[-1].start()
            rows = sent_ref[d]
            grad_router = grad_router + dot_tn(rows, high) + dot_tn(rows, rest)
        grad_router_ref[...] = grad_router
        for copy in copies:
            copy.wait()


def expert_grad_kernel(parts, flat, half_ref, *refs):
    total = None
    for a_ref, b_ref in zip(refs[:parts], refs[parts : 2 * parts]):
        a, b = a_ref[...], b_ref[...]
        product = dot_tn(a.reshape(-1, a.shape[-1]), b)
        total = product if total is None else total + product
    if len(refs) > 2 * parts + 1:
        total = total + refs[2 * parts][...].astype(F32)
    refs[-1][...] = total.astype(BF16)


def join_kernel(odd_ref, mine_ref, other_ref, out_ref):
    own = pl.program_id(0) == odd_ref[0]
    out_ref[...] = jnp.where(own, mine_ref[...], other_ref[...]).astype(F32)


def dense_grad_kernel(n0, n1, g0, g1, m0, m1, b0, b1, small, left_ref, right_ref):
    width = n0.shape[1]
    left_ref[...] = (dot_tn(n0[...], g0[:, : 2 * width]) + dot_tn(n1[...], g1[:, : 2 * width])).astype(BF16)
    right_ref[:, :width] = (dot_tn(n0[...], g0[:, 2 * width :]) + dot_tn(n1[...], g1[:, 2 * width :])).astype(BF16)
    right_ref[:, width : 2 * width] = (dot_tn(m0[...], b0[...]) + dot_tn(m1[...], b1[...])).astype(BF16)
    right_ref[:, 2 * width :] = small[...]


def combine_kernel(out_ref, far_ref, mine_ref, col_ref, hidden_ref, result_ref, pick_ref):
    near, capacity, _ = out_ref.shape
    fill_pick(col_ref, pick_ref, mine_ref[0, 0] // near * near * capacity)
    rows = out_ref[...].reshape(near * capacity, -1)
    summed = dot(pick_ref[...], rows) + far_ref[...].astype(F32)
    result_ref[...] = (hidden_ref[...] + summed).astype(BF16)


def cost(flops, byte_count, transcendentals=0):
    return pl.CostEstimate(flops=int(SCALE * flops), bytes_accessed=int(byte_count), transcendentals=int(transcendentals))


def shaped(shape, dtype):
    return jax.ShapeDtypeStruct(shape, dtype)


def later(kernel, count, ties):
    if not ties:
        return kernel
    return lambda *refs: kernel(*refs[:count], *refs[count + ties :])


def make_strip(base, after):
    heads, width = base.shape
    return pl.pallas_call(
        later(strip_kernel, 1, len(after)),
        in_specs=[VECTOR] + [ANYWHERE] * len(after),
        out_shape=shaped((heads, STRIP, width - STRIP), BF16),
        compiler_params=params(),
        cost_estimate=cost(0, 0),
    )(base, *after)


def place(ids, far_ids, mine, experts, near, capacity):
    length = ids.shape[0]
    row, col = shaped((2, length), jnp.int32), shaped((length, 2), jnp.int32)
    return pl.pallas_call(
        functools.partial(slots_kernel, experts, near, capacity),
        out_shape=(row, row, col, col),
        in_specs=[VECTOR] * 4 + [SCALAR],
        compiler_params=params(),
        cost_estimate=cost(0, 0),
    )(ids.T, ids, far_ids, far_ids.T, mine)


def scatter(near, capacity, *parts, after=()):
    slots = [part[0] for part in parts]
    values = [value for part in parts for value, _ in part[1]]
    picks = [[pick for _, pick in part[1]] for part in parts]
    length, width = slots[0].shape[1], values[0].shape[-1]
    total = near * capacity * len(parts)
    return pl.pallas_call(
        later(functools.partial(scatter_kernel, picks), len(slots) + len(values), len(after)),
        in_specs=[VECTOR] * (len(slots) + len(values)) + [ANYWHERE] * len(after),
        out_shape=shaped((near, capacity * len(parts), width), BF16),
        compiler_params=params(),
        cost_estimate=cost(2 * total * length * width, 6e6),
    )(*slots, *values, *after)


def gather(col, base, blocks, after):
    length, width = col[0].shape[0], blocks.shape[2]
    near, capacity = blocks.shape[0], blocks.shape[1] // 2
    total = near * capacity
    return pl.pallas_call(
        later(gather_kernel, 4, len(after)),
        out_shape=(shaped((length, width), BF16), shaped((length, width), BF16)),
        in_specs=[VECTOR] * 2 + [SCALAR, VECTOR] + [ANYWHERE] * len(after),
        scratch_shapes=[pltpu.VMEM((length, total), BF16), pltpu.VMEM((total, width), BF16)],
        compiler_params=params(),
        cost_estimate=cost(4 * total * length * width, 6e6),
    )(*col, base, blocks, *after)


def forward(m, x, gains, weight, strip, block_row, block_col, row_slots, near, capacity, after):
    _, length, width = x.shape
    heads = width // HEAD
    return pl.pallas_call(
        later(functools.partial(forward_kernel, m), 7, len(after)),
        in_specs=[VECTOR] * 7 + [ANYWHERE] * len(after),
        out_shape=(
            shaped((length, 3 * width), BF16),
            shaped((length, width), BF16),
            shaped((heads, length, 1), F32),
            shaped((length, width), F32),
            shaped((length, width), BF16),
            shaped((near, capacity, width), BF16),
        ),
        compiler_params=params(),
        cost_estimate=cost(
            2 * length * width * 4 * width + 8 * heads * length * length * HEAD,
            24e6, heads * length * length,
        ),
    )(x, gains, weight, strip, block_row, block_col, row_slots, *after)


def backward(
    part, own, far, mine, col, cot, hidden, gains, weight, proj, totals, strip, block_row, block_col, x, after
):
    _, length, width = x.shape
    heads = width // HEAD
    near, capacity = own.shape[0], own.shape[1] // 2
    total = 2 * near * capacity
    return pl.pallas_call(
        later(functools.partial(backward_kernel, near, part), near + 13, len(after)),
        in_specs=[VECTOR] * (near + 1) + [SCALAR] + [VECTOR] * 11 + [ANYWHERE] * len(after),
        out_shape=(
            shaped((length, width), BF16),
            shaped((length, width), BF16),
            shaped((length, 3 * width), BF16),
            shaped((length, width), BF16),
            shaped((2, width), F32),
            shaped((heads, 2 * length), F32),
        ),
        scratch_shapes=[
            pltpu.VMEM((length, total), BF16),
            pltpu.VMEM((total, width), BF16),
            pltpu.VMEM((length, width), BF16),
            pltpu.VMEM((length, length), BF16),
            pltpu.VMEM((length, length), BF16),
            pltpu.VMEM((STRIP, 2 * length), F32),
        ],
        compiler_params=params(),
        cost_estimate=cost(
            2 * length * width * 4 * width + 20 * heads * length * length * HEAD + 2 * total * length * width,
            30e6, heads * length * length,
        ),
    )(*far, own, mine, col, cot, hidden, gains, weight, proj, totals, strip, block_row, block_col, x, *after)


def block_of(count, near, capacity, width, index):
    return pl.BlockSpec((near, capacity, width), lambda f: (0, index, 0), pipeline_mode=pl.Buffered(1))


def expert(kind, part, sent, cots, ids, mine, router, router_turned, first, last, earlier, after):
    (sent, sent_block), (cots, cot_block) = sent, cots
    near, _, width = sent.shape
    experts = ids.shape[1]
    capacity = 3 * ids.shape[2] // experts
    total = near * capacity
    inner = first.shape[1]
    step = 768

    def whole(shape):
        return pl.BlockSpec(shape, lambda f: (0,) * len(shape), pipeline_mode=pl.Buffered(1))

    anywhere = pl.BlockSpec(memory_space=pl.ANY)
    shared = shaped((near, 2 * capacity, width), BF16)
    if kind:
        back_specs = tuple(whole((capacity, width)) for _ in range(near))
        back_shapes = tuple(shaped((capacity, width), BF16) for _ in range(near))
    else:
        back_specs, back_shapes = (anywhere,), (shared,)
    count = len(back_specs)
    alias = len(earlier)
    targets = (count,) if kind else (0, 1)
    outs = pl.pallas_call(
        later(functools.partial(expert_kernel, kind, near, alias, part), 8 + alias, len(after)),
        grid=(inner // step,),
        in_specs=[
            block_of(0, near, capacity, width, sent_block), block_of(0, near, capacity, width, cot_block),
            whole(ids.shape), SCALAR, whole(router.shape), whole(router_turned.shape),
            pl.BlockSpec((width, step), lambda f: (0, f)),
            pl.BlockSpec((step, width), lambda f: (f, 0)),
        ] + [anywhere] * (alias + len(after)),
        out_specs=back_specs + (
            anywhere,
            pl.BlockSpec((total, step), lambda f: (0, f)),
            pl.BlockSpec((total, step), lambda f: (0, f)),
            whole((total, width)), whole((width, LANES)),
        ),
        out_shape=back_shapes + (
            shared,
            shaped((total, inner), BF16), shaped((total, inner), BF16),
            shaped((total, width), BF16), shaped((width, LANES), F32),
        ),
        scratch_shapes=[
            pltpu.VMEM((total, 1), F32),
            pltpu.VMEM((total, 1), jnp.int32),
            pltpu.VMEM((total, width), F32),
            pltpu.VMEM((total, width), F32),
            pltpu.VMEM(ids.shape[1:], jnp.int32),
            pltpu.VMEM(ids.shape[1:], F32),
            pltpu.VMEM((total, width), BF16),
            pltpu.VMEM((total, width), BF16),
            pltpu.SemaphoreType.DMA((2, near)),
        ],
        input_output_aliases={8 + n: target for n, target in enumerate(targets)} if alias else {},
        compiler_params=params(dimension_semantics=("arbitrary",)),
        cost_estimate=cost(8 * total * width * inner, 30e6, total * inner),
    )(sent, cots, ids, mine, router, router_turned, first, last, *earlier, *after)
    backs = list(outs[:count])
    return (backs if kind else backs[0]), outs[count], outs[count + 1 :]


def last_grad(half, acts, scaled, received, after):
    total, inner = acts[0].shape
    width = scaled[0].shape[1]
    step = 512
    count = inner // 2 // step
    out_spec = pl.BlockSpec((step, width), lambda f, half: (f, 0))
    specs = [pl.BlockSpec((total, step), lambda f, half: (0, half[0] * count + f))] * len(acts)
    specs += [pl.BlockSpec((total, width), lambda f, half: (0, 0))] * len(acts)
    extra = [] if received is None else [received]
    return pl.pallas_call(
        later(functools.partial(expert_grad_kernel, len(acts), True), 1 + 2 * len(acts) + len(extra), len(after)),
        grid_spec=pltpu.PrefetchScalarGridSpec(
            num_scalar_prefetch=1, grid=(count,), in_specs=specs + [out_spec] * len(extra) + [ANYWHERE] * len(after),
            out_specs=out_spec
        ),
        out_shape=shaped((inner // 2, width), BF16),
        compiler_params=params(dimension_semantics=("arbitrary",)),
        cost_estimate=cost(len(acts) * total * inner * width, 15e6),
    )(half, *acts, *scaled, *extra, *after)


def first_grad(half, rows, ups, received, after):
    total, inner = ups[0].shape
    near, _, width = rows[0][0].shape
    capacity = total // near
    step = 768
    out_spec = pl.BlockSpec((width // 2, step), lambda f, half: (0, f))

    def row_spec(block):
        return pl.BlockSpec((near, capacity, width // 2), lambda f, half: (0, block, half[0]))

    specs = [row_spec(block) for _, block in rows]
    specs += [pl.BlockSpec((total, step), lambda f, half: (0, f))] * len(ups)
    extra = [] if received is None else [received]
    return pl.pallas_call(
        later(functools.partial(expert_grad_kernel, len(ups), False), 1 + 2 * len(ups) + len(extra), len(after)),
        grid_spec=pltpu.PrefetchScalarGridSpec(
            num_scalar_prefetch=1, grid=(inner // step,), in_specs=specs + [out_spec] * len(extra) + [ANYWHERE] * len(after),
            out_specs=out_spec
        ),
        out_shape=shaped((width // 2, inner), BF16),
        compiler_params=params(dimension_semantics=("arbitrary",)),
        cost_estimate=cost(len(ups) * total * inner * width, 25e6),
    )(half, *[array for array, _ in rows], *ups, *extra, *after)


def join(odd, mine, other):
    rows, columns = mine.shape
    step = rows // 3
    spec = pl.BlockSpec((step, columns), lambda h, i, odd: (i, 0))
    return pl.pallas_call(
        join_kernel,
        grid_spec=pltpu.PrefetchScalarGridSpec(
            num_scalar_prefetch=1, grid=(2, 3), in_specs=[spec, spec],
            out_specs=pl.BlockSpec((step, columns), lambda h, i, odd: (h * 3 + i, 0)),
        ),
        out_shape=shaped((2 * rows, columns), F32),
        compiler_params=params(dimension_semantics=("arbitrary", "arbitrary")),
        cost_estimate=cost(rows * columns, 20e6),
    )(odd, mine, other)


def dense_grad(*arrays, after):
    small = arrays[-1]
    width = arrays[0].shape[1]
    length = arrays[0].shape[0]
    return pl.pallas_call(
        later(dense_grad_kernel, len(arrays), len(after)),
        in_specs=[VECTOR] * len(arrays) + [ANYWHERE] * len(after),
        out_shape=(shaped((width, 2 * width), BF16), shaped((width, 2 * width + small.shape[1]), BF16)),
        compiler_params=params(),
        cost_estimate=cost(4 * length * width * 4 * width, 20e6),
    )(*arrays, *after)


def combine(out_rows, part, far, mine, col, hidden):
    length, width = hidden.shape
    near, capacity = out_rows.shape[0], out_rows.shape[1] // 2
    total = near * capacity
    plain = pl.BlockSpec((length, width), lambda f: (0, 0))
    return pl.pallas_call(
        combine_kernel,
        grid=(1,),
        in_specs=[
            block_of(0, near, capacity, width, part), plain, SCALAR, pl.BlockSpec(col.shape, lambda f: (0, 0)), plain,
        ],
        out_specs=plain,
        out_shape=shaped((length, width), BF16),
        scratch_shapes=[pltpu.VMEM((length, total), BF16)],
        compiler_params=params(),
        cost_estimate=cost(2 * total * length * width, 6e6),
    )(out_rows, far, mine, col, hidden)


def swap(value, axis, size, bit):
    return lax.ppermute(value, axis, [(i, i ^ bit) for i in range(size)])


def pair_sum(a, b):
    return (a.astype(F32) + b.astype(F32)).astype(BF16)


def halve(value, axis, name, size, bit):
    odd = (lax.axis_index(name) & bit) > 0
    count = value.shape[axis] // 2
    low = lax.slice_in_dim(value, 0, count, axis=axis)
    high = lax.slice_in_dim(value, count, 2 * count, axis=axis)
    kept, sent = jnp.where(odd, high, low), jnp.where(odd, low, high)
    return pair_sum(kept, swap(sent, name, size, bit))


def unite(value, name, size, bit):
    odd = (lax.axis_index(name) & bit) > 0
    other = swap(value, name, size, bit)
    return jnp.concatenate([jnp.where(odd, other, value), jnp.where(odd, value, other)], axis=0)


def dense_sum(left, right, dp, experts, after):
    def split(value):
        return halve(value.reshape(dp // 2, 2, value.shape[0] // dp, value.shape[1]), 1, "dp", dp, 1)[:, 0]

    def along_dp(value):
        bit = 2
        while bit < dp:
            shape = value.shape
            value = halve(value.reshape(shape[0] // 2, 2, *shape[1:]), 1, "dp", dp, bit)[:, 0]
            bit *= 2
        return value

    left, right = split(left), split(right)
    left = after(0, along_dp(left))
    right = halve(right, 1, "expert", experts, 1)
    left = halve(left, 1, "expert", experts, 1)
    right = along_dp(right)
    rows = after(1, jnp.concatenate([left[0], right[0]], axis=1))
    step, bit = 2, 2
    while bit < experts:
        rows = after(step, halve(rows, 0, "expert", experts, bit))
        step, bit = step + 1, bit * 2
    while bit > 1:
        bit //= 2
        rows = unite(rows, "expert", experts, bit)
        if bit == 2:
            rows = after(9, rows)
    return rows.astype(F32)


def body(
    dp, experts, inputs, gain_one, w_qkv, w_out, rel_table, second_norm_gain, w_router, w_in, w_back,
    expert_ids, block_ids, cotangent,
):
    micro, length, width = inputs.shape
    capacity = 3 * length // experts
    near = experts // 2
    buckets, heads = rel_table.shape[0] * dp, rel_table.shape[1]
    shard = gain_one.shape[0]
    first_in, last_out = w_in[0], w_back[0]
    mine = lax.axis_index("expert").astype(jnp.int32).reshape(1, 1)

    groups = [list(range(near)), list(range(near, experts))]
    odd = (lax.axis_index("dp") & 1).astype(jnp.int32).reshape(1)

    def cross(value, bit):
        return swap(value, "expert", experts, bit)

    def around(blocks):
        return lax.all_to_all(
            blocks, "expert", split_axis=0, concat_axis=0, axis_index_groups=groups, tiled=True
        )

    def order(*values):
        return lax.optimization_barrier(values)

    middle = length // 2
    cot0_top, cot0_end = cross(cotangent[0, :middle], near), cross(cotangent[0, middle:], near)

    ids_row = jnp.transpose(expert_ids, (0, 2, 1))
    ids_all = lax.all_to_all(
        jnp.broadcast_to(ids_row[None], (experts,) + ids_row.shape), "expert", split_axis=0, concat_axis=0, tiled=True
    )
    ids_all = jnp.transpose(ids_all, (1, 2, 0, 3))
    ids_far = lax.dynamic_index_in_dim(ids_all, lax.axis_index("expert") ^ near, 2, keepdims=False)

    table_column = jnp.pad(rel_table.reshape(-1), (0, shard - rel_table.size))
    small = jnp.concatenate([gain_one[:, None], second_norm_gain[:, None], table_column[:, None], w_router], axis=1)
    extra = jnp.pad(small, ((0, 0), (0, LANES - small.shape[1])))
    bit = 1
    while bit < dp:
        other = swap(extra, "dp", dp, bit)
        high = (lax.axis_index("dp") & bit) > 0
        extra = jnp.concatenate([jnp.where(high, other, extra), jnp.where(high, extra, other)], axis=0)
        bit *= 2
    packed = lax.all_gather(jnp.concatenate([w_qkv, w_out], axis=1), "dp", axis=0, tiled=True)
    gains = extra[:, :2].astype(F32).T
    table = extra[:, 2].reshape(dp, shard)[:, : rel_table.size].reshape(buckets, heads)
    router = jnp.pad(extra[:, 3 : 3 + experts], ((0, 0), (0, LANES - experts)))
    router_turned = router.T
    levels = bucket_table(length, buckets)
    base = lax.dot_general(
        table, jnp.asarray(levels, BF16), (((0,), (0,)), ((), ())), preferred_element_type=F32
    )
    strip = make_strip(base, [])
    places = [place(expert_ids[m], ids_far[m], mine, experts, near, capacity) for m in range(micro)]

    kept = []
    block_cols = block_ids[:, 0, :].T

    def layer_front(m, after):
        block_row, block_col = block_ids, block_cols
        proj, mixed, totals, hidden, second, send = forward(
            m, inputs, gains, packed, strip, block_row, block_col, places[m][0], near, capacity, after
        )
        kept.append((proj, mixed, totals, hidden, block_row, block_col))
        return second, send

    cot_own = around(
        scatter(near, capacity, (places[0][0], [(cotangent, 0)]), (places[1][0], [(cotangent, 1)]), after=[cot0_top, strip])
    )
    second0, send0 = layer_front(0, [])
    second0_far = cross(second0, near)
    own0 = around(send0)
    second1, send1 = layer_front(1, [send0, cot0_end])
    own1 = around(send1)

    common = (mine, router, router_turned, first_in, last_out)
    cot1_far = cross(order(cotangent[1], second0_far, send1)[0], near)
    back_own, out_own, kept0_own = expert(
        0, 0, (own0, 0), (cot_own, 0), ids_all[0], *common, (), [second0_far, send1]
    )
    second1_far = cross(order(second1, second0_far)[0], near)
    far0_send = scatter(
        near, capacity, (places[0][1], [(cot0_top, None), (cot0_end, None)]), (places[0][1], [(second0_far, None)]),
        after=[out_own],
    )
    far0 = around(far0_send)
    back_own, out_own, kept1_own = expert(
        0, 1, (own1, 0), (cot_own, 1), ids_all[1], *common, (back_own, out_own), [far0_send]
    )
    far1_send = scatter(
        near, capacity, (places[1][1], [(cot1_far, None)]), (places[1][1], [(second1_far, None)]), after=[out_own],
    )
    far1 = around(far1_send)
    back0_far, out_far, kept0_far = expert(1, 0, (far0, 1), (far0, 0), ids_all[0], *common, (), [far1_send])
    back1_far, out_far, kept1_far = expert(1, 1, (far1, 1), (far1, 0), ids_all[1], *common, (out_far,), [])
    back_own, out_own, _ = order(back_own, out_own, back0_far[0])
    back_own, out_own, out_far = around(back_own), around(out_own), around(out_far)
    home = [
        [cross(block, near | d) for d, block in enumerate(back0_far)],
        [cross(block, near | d) for d, block in enumerate(back1_far)],
    ]
    quarter = max(1, near // 4)

    parts = (kept0_own, kept1_own, kept0_far, kept1_far)
    acts, ups, scaled, routers = zip(*parts)
    rows = ((own0, 0), (own1, 0), (far0, 1), (far1, 1))
    grad_router = sum(routers)[:, :experts]

    home0, home1 = home
    other = 1 - odd
    last_part = last_grad(other, acts, scaled, None, home0[: 2 * quarter] + [back_own])
    last_got = swap(last_part, "dp", dp, 1)
    first_part = first_grad(other, rows, ups, None, [last_part] + home0[2 * quarter : 3 * quarter])
    first_got = swap(first_part, "dp", dp, 1)
    last_sum = last_grad(odd, acts, scaled, last_got, [first_part] + home0[3 * quarter :])
    first_sum = first_grad(odd, rows, ups, first_got, [last_sum] + home1[:quarter])
    first_whole = first_sum

    def over_dp(value):
        bit = 2
        while bit < dp:
            other = swap(value, "dp", dp, bit)
            value = pair_sum(value, other)
            bit *= 2
        return value, other

    def pieces(value):
        count = value.shape[0] // 4
        return [value[n * count : (n + 1) * count] for n in range(4)]

    last_sum, last_came = zip(*[over_dp(piece) for piece in pieces(last_sum)])
    first_sum = pieces(first_sum)
    first_sum[0], first_came = over_dp(first_sum[0])

    def layer_back(m, after):
        proj, mixed, totals, hidden, block_row, block_col = kept[m]
        return backward(
            m, back_own, home[m], mine, places[m][2], cotangent, hidden, gains, packed, proj, totals, strip,
            block_row, block_col, inputs, after,
        )

    back_outs = [layer_back(0, [first_whole, last_came[0]] + home1[quarter : 2 * quarter])]
    out_sums = gather((places[0][3], places[1][3]), mine, out_far, [back_outs[0][1]])
    out0_far, out1_far = cross(out_sums[0], near), cross(out_sums[1], near)
    back_outs.append(layer_back(1, [last_came[1], last_came[2], out_sums[0]]))

    gain_grads = back_outs[0][4] + back_outs[1][4]
    diagonals = back_outs[0][5] + back_outs[1][5]
    table_grad = lax.dot_general(
        jnp.asarray(levels, F32), diagonals, (((1,), (1,)), ((), ())),
        precision=lax.Precision.HIGHEST, preferred_element_type=F32,
    )
    table_grad = jnp.pad(table_grad.reshape(dp, rel_table.size), ((0, 0), (0, shard - rel_table.size)))
    small_grad = jnp.concatenate([gain_grads.T, table_grad.reshape(width, 1), grad_router], axis=1).astype(BF16)
    small_grad = jnp.pad(small_grad, ((0, 0), (0, LANES - small_grad.shape[1])))
    left, right = dense_grad(
        back_outs[0][3], back_outs[1][3], back_outs[0][2], back_outs[1][2],
        kept[0][1], kept[1][1], back_outs[0][1], back_outs[1][1], small_grad,
        after=[last_came[3], first_came, out0_far, out_own],
    )
    results = [combine(out_own, 0, out0_far, mine, places[0][2], kept[0][3])]
    last_sum = jnp.concatenate(last_sum, axis=0)
    grad_last = join(odd, last_sum, swap(last_sum, "dp", dp, 1))
    grad_first = None

    def after(step, value):
        nonlocal grad_first, grad_last, first_sum, out1_far
        if step == 0:
            value, results[0] = order(value, results[0])
        if step == 1:
            value, grad_last, out1_far, *rest = order(value, grad_last, out1_far, *first_sum[1:])
            results.append(combine(out_own, 1, out1_far, mine, places[1][2], kept[1][3]))
            both = jnp.concatenate(first_sum[:1] + [over_dp(piece)[0] for piece in rest], axis=0)
            grad_first = join(odd, both, swap(both, "dp", dp, 1))
        if step == 3:
            value, results[1] = order(value, results[1])
        if step == 9:
            value, grad_first = order(value, grad_first)
        return value

    dense = dense_sum(left, right, dp, experts, after)
    tail = dense[:, 4 * width :]
    return (
        jnp.stack(results),
        jnp.stack([out[0] for out in back_outs]),
        tail[:, 0],
        dense[:, : 3 * width],
        dense[:, 3 * width : 4 * width],
        tail[: rel_table.size, 2].reshape(rel_table.shape),
        tail[:, 1],
        tail[:, 3 : 3 + experts],
        grad_first[None],
        grad_last[None],
    )


def solution(mesh):
    split = P(None, ("dp", "expert"), None)
    in_specs = (
        split, P("dp"), P("dp", None), P("dp", None), P("dp", None), P("dp"), P("dp", None),
        P("expert", None, None), P("expert", None, None), split, split, split,
    )
    out_specs = (
        split, split, P("dp"), P("dp", None), P("dp", None), P("dp", None), P("dp"), P("dp", None),
        P("expert", None, None), P("expert", None, None),
    )
    return jax.shard_map(
        functools.partial(body, mesh.shape["dp"], mesh.shape["expert"]), mesh=mesh, in_specs=in_specs, out_specs=out_specs, check_vma=False
    )
```

```python
import functools

import jax
import jax.numpy as jnp
import numpy as np
from jax import lax
from jax.experimental import pallas as pl
from jax.experimental.pallas import tpu as pltpu
from jax.sharding import PartitionSpec as P

HEAD = 64
PAIR = 2 * HEAD
STRIP = 128
LANES = 128
VMEM_BYTES = 60 * 1024 * 1024
SCALE = 5
VECTOR = pl.BlockSpec(memory_space=pltpu.VMEM)
SCALAR = pl.BlockSpec(memory_space=pltpu.SMEM)
ANYWHERE = pl.BlockSpec(memory_space=pl.ANY)

epsilon = 1e-06
bucket_edges = (12, 16, 23, 32, 46, 64, 91)
masked_score = -1e30
gelu_a = float(np.sqrt(2.0 / np.pi))
gelu_b = 0.044715

F32 = jnp.float32
BF16 = jnp.bfloat16


def dot(a, b):
    return jnp.dot(a, b, preferred_element_type=F32)


def dot_nt(a, b):
    return lax.dot_general(a, b, (((1,), (1,)), ((), ())), preferred_element_type=F32)


def dot_tn(a, b):
    return lax.dot_general(a, b, (((0,), (0,)), ((), ())), preferred_element_type=F32)


def iota(shape, dim):
    return lax.broadcasted_iota(jnp.int32, shape, dim)


def hot(mask):
    return jnp.where(mask, 1.0, 0.0).astype(BF16)


def params(**extra):
    return pltpu.CompilerParams(vmem_limit_bytes=VMEM_BYTES, **extra)


def bucket_table(length, buckets):
    offset = np.arange(2 * length) - (length - 1)
    distance = np.abs(offset)
    far = 8 + sum((distance >= edge).astype(np.int32) for edge in bucket_edges)
    bucket = np.where(distance < 8, distance, far) + 16 * (offset > 0)
    table = (bucket[None, :] == np.arange(buckets)[:, None]) & (offset < length)[None, :]
    return table.astype(np.float32)


def strip_kernel(base_ref, out_ref):
    heads, width = base_ref.shape
    for h in range(heads):
        row = jnp.broadcast_to(base_ref[h : h + 1, :], (STRIP, width))
        rolled = pltpu.roll(row, width - (STRIP - 1), 1, stride=1, stride_axis=0)
        out_ref[h] = rolled[:, : width - STRIP].astype(BF16)


def slots_kernel(experts, near, capacity, ids_row_ref, ids_col_ref, far_row_ref, far_col_ref, mine_ref, row_ref, row_far_ref, col_ref, col_far_ref):
    length = ids_row_ref.shape[1]
    base = mine_ref[0, 0] // near * near
    padded = max(16, experts)
    before = hot(iota((length, length), 0) < iota((length, length), 1))
    for ids_row, row_out in ((ids_row_ref, row_ref), (far_row_ref, row_far_ref)):
        level = iota((padded, length), 0)
        first, second = ids_row[0:1, :], ids_row[1:2, :]
        place = dot(hot((level == first) | (level == second)), before).astype(jnp.int32)
        block = level - base
        slot = jnp.where((block >= 0) & (block < near), place + block * capacity, -1)
        row_out[0:1, :] = jnp.sum(jnp.where(level == first, slot, 0), axis=0, keepdims=True)
        row_out[1:2, :] = jnp.sum(jnp.where(level == second, slot, 0), axis=0, keepdims=True)

    after = hot(iota((length, length), 1) < iota((length, length), 0))
    for ids_col, col_out in ((ids_col_ref, col_ref), (far_col_ref, col_far_ref)):
        level = iota((length, LANES), 1)
        first, second = ids_col[:, 0:1], ids_col[:, 1:2]
        slot = dot(after, hot((level == first) | (level == second))) + (level * capacity).astype(F32)
        col_out[:, 0:1] = jnp.sum(jnp.where(level == first, slot, 0.0), axis=1, keepdims=True).astype(jnp.int32)
        col_out[:, 1:2] = jnp.sum(jnp.where(level == second, slot, 0.0), axis=1, keepdims=True).astype(jnp.int32)


def scatter_kernel(picks, *refs):
    count = len(picks)
    slots, refs, send_ref = refs[:count], refs[count:-1], refs[-1]
    values = []
    for part in picks:
        values.append([ref if pick is None else ref.at[pick] for pick, ref in zip(part, refs)])
        refs = refs[len(part) :]
    scatter_parts(slots, values, send_ref)


def scatter_parts(slot_refs, value_refs, send_ref):
    near, length = send_ref.shape[0], slot_refs[0].shape[1]
    count = len(slot_refs)
    capacity = send_ref.shape[1] // count
    for n in range(count):
        first, second = slot_refs[n][0:1, :], slot_refs[n][1:2, :]
        values = [ref[...] for ref in value_refs[n]]
        for d in range(near):
            slots = iota((capacity, length), 0) + d * capacity
            pick = hot((slots == first) | (slots == second))
            total, start = None, 0
            for value in values:
                part = dot(pick[:, start : start + value.shape[0]], value)
                total = part if total is None else total + part
                start += value.shape[0]
            send_ref[d, n * capacity : (n + 1) * capacity, :] = total.astype(BF16)


def fill_pick(col_ref, pick_ref, offset=0):
    length, total = pick_ref.shape
    first, second = col_ref[:, 0:1] - offset, col_ref[:, 1:2] - offset
    step = 256
    for start in range(0, total, step):
        slots = iota((length, step), 1) + start
        pick_ref[:, start : start + step] = hot((slots == first) | (slots == second))


def gather_kernel(first_ref, second_ref, mine_ref, blocks_ref, first_sum_ref, second_sum_ref, pick_ref, near_ref):
    near, pair_rows, _ = blocks_ref.shape
    capacity = pair_rows // 2
    offset = mine_ref[0, 0] // near * near * capacity
    for part, (col_ref, sum_ref) in enumerate(((first_ref, first_sum_ref), (second_ref, second_sum_ref))):
        fill_pick(col_ref, pick_ref, offset)
        for d in range(near):
            near_ref[d * capacity : (d + 1) * capacity, :] = blocks_ref[d, part * capacity : (part + 1) * capacity, :]
        sum_ref[...] = dot(pick_ref[...], near_ref[...]).astype(BF16)


def head_mask(length):
    return iota((length, PAIR), 1) < HEAD


def forward_kernel(
    m, x_ref, gains_ref, weight_ref, strip_ref, block_row_ref, block_col_ref, row_ref,
    proj_ref, mixed_ref, total_ref, hidden_ref, second_ref, send_ref,
    score_ref, weight_part_ref, mask_ref,
):
    _, length, width = x_ref.shape
    scale = HEAD ** (-0.5)
    x = x_ref[m].astype(F32)
    r1 = lax.rsqrt(jnp.mean(x * x, axis=1, keepdims=True) + epsilon)
    normed = (x * r1 * gains_ref[0:1, :]).astype(BF16)
    proj_ref[...] = dot(normed, weight_ref[:, : 3 * width]).astype(BF16)
    total_ref[...] = jnp.zeros_like(total_ref)

    mask_ref[...] = jnp.where(block_row_ref[m] <= block_col_ref[:, m : m + 1], 0.0, masked_score)
    lane = iota((STRIP, LANES), 1)

    def pair(p, carry):
        lanes = pl.multiple_of(p * PAIR, PAIR)
        q = proj_ref[:, pl.ds(lanes, PAIR)] * scale
        k = proj_ref[:, pl.ds(width + lanes, PAIR)]
        v = proj_ref[:, pl.ds(2 * width + lanes, PAIR)]
        left = head_mask(length)
        zero = jnp.zeros_like(k)
        keeps = (left, jnp.logical_not(left))
        for h in range(2):
            score_ref[h] = dot_nt(q, jnp.where(keeps[h], k, zero))
        for h in range(2):
            strip = strip_ref[2 * p + h].astype(F32)
            for i in range(length // STRIP):
                rows = slice(i * STRIP, (i + 1) * STRIP)
                start = length - STRIP - i * STRIP
                s = (score_ref[h, rows, :] + strip[:, start : start + length]) + mask_ref[rows, :]
                top = jnp.max(s, axis=1, keepdims=True)
                e = jnp.exp(s - top)
                total = jnp.sum(e, axis=1, keepdims=True)
                weight_part_ref[h, rows, :] = (e * (1.0 / total)).astype(BF16)
                total_ref[rows, :] = jnp.where(lane == 2 * p + h, top + jnp.log(total), total_ref[rows, :])
        out = dot(weight_part_ref[0], jnp.where(keeps[0], v, zero)) + dot(weight_part_ref[1], jnp.where(keeps[1], v, zero))
        mixed_ref[:, pl.ds(lanes, PAIR)] = out.astype(BF16)
        return carry

    lax.fori_loop(0, width // PAIR, pair, 0)
    hidden = x + dot(mixed_ref[...], weight_ref[:, 3 * width : 4 * width])
    hidden_ref[...] = hidden
    r2 = lax.rsqrt(jnp.mean(hidden * hidden, axis=1, keepdims=True) + epsilon)
    second_ref[...] = (hidden * r2 * gains_ref[1:2, :]).astype(BF16)
    scatter_parts([row_ref], [[second_ref]], send_ref)


def backward_kernel(near, part, *refs):
    backward_main(part, refs[:near], *refs[near:])


def backward_main(
    part, far_refs, own_ref, mine_ref, col_ref, cot_ref, hidden_ref, gains_ref, weight_ref, proj_ref, total_ref, strip_ref,
    block_row_ref, block_col_ref, x_ref,
    grad_x_ref, branch_ref, grad_proj_ref, normed_ref, grad_gain_ref, diagonal_ref,
    pick_ref, back_ref, grad_mixed_ref, low_ref, prob_ref, strip_sum_ref, score_ref, grad_prob_ref, mask_ref,
):
    _, length, width = cot_ref.shape
    scale = HEAD ** (-0.5)
    near, capacity = own_ref.shape[0], own_ref.shape[1] // 2
    mine = mine_ref[0, 0]
    base = mine // near * near
    for d in range(near):
        own = own_ref[d, part * capacity : (part + 1) * capacity, :]
        back_ref[pl.ds(pl.multiple_of((base + d) * capacity, 16), capacity), :] = own
        back_ref[pl.ds(pl.multiple_of((mine ^ (near | d)) * capacity, 16), capacity), :] = far_refs[d][...]
    fill_pick(col_ref, pick_ref)
    grad_second = dot(pick_ref[...], back_ref[...])
    hidden = hidden_ref[...]
    r2 = lax.rsqrt(jnp.mean(hidden * hidden, axis=1, keepdims=True) + epsilon)
    scaled = grad_second * gains_ref[1:2, :]
    inner = jnp.mean(hidden * scaled, axis=1, keepdims=True)
    grad_hidden = cot_ref[part].astype(F32) + r2 * scaled - hidden * (r2 * r2 * r2 * inner)
    grad_gain_ref[1:2, :] = jnp.sum(grad_second * hidden * r2, axis=0, keepdims=True)
    branch = grad_hidden.astype(BF16)
    branch_ref[...] = branch
    grad_mixed_ref[...] = dot_nt(branch, weight_ref[:, 3 * width : 4 * width]).astype(BF16)

    mask_ref[...] = jnp.where(block_row_ref[part] <= block_col_ref[:, part : part + 1], 0.0, masked_score)
    lane = iota((STRIP, LANES), 1)

    def pair(p, carry):
        lanes = pl.multiple_of(p * PAIR, PAIR)
        q = proj_ref[:, pl.ds(lanes, PAIR)]
        k = proj_ref[:, pl.ds(width + lanes, PAIR)]
        v = proj_ref[:, pl.ds(2 * width + lanes, PAIR)]
        g = grad_mixed_ref[:, pl.ds(lanes, PAIR)]
        q_turned = q.astype(F32).T.astype(BF16)
        g_turned = g.astype(F32).T.astype(BF16)
        left = head_mask(length)
        zero = jnp.zeros_like(k)
        keeps = (left, jnp.logical_not(left))
        scaled_q = q * scale
        for h in range(2):
            score_ref[h] = dot_nt(scaled_q, jnp.where(keeps[h], k, zero))
            grad_prob_ref[h] = dot_nt(g, jnp.where(keeps[h], v, zero))
        keys, values = [], []
        for h in range(2):
            strip = strip_ref[2 * p + h].astype(F32)
            strip_sum_ref[...] = jnp.zeros_like(strip_sum_ref)
            for i in range(length // STRIP):
                rows = slice(i * STRIP, (i + 1) * STRIP)
                start = length - STRIP - i * STRIP
                s = (score_ref[h, rows, :] + strip[:, start : start + length]) + mask_ref[rows, :]
                row_total = jnp.sum(jnp.where(lane == 2 * p + h, total_ref[rows, :], 0.0), axis=1, keepdims=True)
                prob = jnp.exp(s - row_total)
                grad_prob = grad_prob_ref[h, rows, :]
                row_inner = jnp.sum(prob * grad_prob, axis=1, keepdims=True)
                grad_score = prob * (grad_prob - row_inner)
                strip_sum_ref[:, start : start + length] += grad_score
                low_ref[h, rows, :] = grad_score.astype(BF16)
                prob_ref[h, rows, :] = prob.astype(BF16)
            half = slice(h * HEAD, (h + 1) * HEAD)
            keys.append(dot(q_turned[half], low_ref[h]))
            values.append(dot(g_turned[half], prob_ref[h]))
            gathered = jnp.zeros((8, 2 * length), F32)
            for a in range(STRIP // 8):
                piece = strip_sum_ref[8 * a : 8 * a + 8, :]
                gathered += pltpu.roll(piece, STRIP - 8 - 8 * a, 1) if a < STRIP // 8 - 1 else piece
            line = gathered[7:8]
            for b in range(7):
                line += pltpu.roll(gathered[b : b + 1], 7 - b, 1)
            diagonal_ref[pl.ds(2 * p + h, 1), :] = line
        grad_query = dot(low_ref[0], jnp.where(keeps[0], k, zero)) + dot(low_ref[1], jnp.where(keeps[1], k, zero))
        grad_proj_ref[:, pl.ds(lanes, PAIR)] = (grad_query * scale).astype(BF16)
        grad_key = jnp.concatenate(keys, axis=0).T
        grad_value = jnp.concatenate(values, axis=0).T
        grad_proj_ref[:, pl.ds(width + lanes, PAIR)] = (grad_key * scale).astype(BF16)
        grad_proj_ref[:, pl.ds(2 * width + lanes, PAIR)] = grad_value.astype(BF16)
        return carry

    lax.fori_loop(0, width // PAIR, pair, 0)
    x = x_ref[part].astype(F32)
    r1 = lax.rsqrt(jnp.mean(x * x, axis=1, keepdims=True) + epsilon)
    normed_ref[...] = (x * r1 * gains_ref[0:1, :]).astype(BF16)
    grad_normed = dot_nt(grad_proj_ref[...], weight_ref[:, : 3 * width])
    scaled = grad_normed * gains_ref[0:1, :]
    inner = jnp.mean(x * scaled, axis=1, keepdims=True)
    grad_gain_ref[0:1, :] = jnp.sum(grad_normed * x * r1, axis=0, keepdims=True)
    grad_x_ref[...] = (grad_hidden + r1 * scaled - x * (r1 * r1 * r1 * inner)).astype(BF16)


def expert_kernel(
    kind, near, alias, part, *refs,
):
    sent_ref, cots_ref, ids_ref, mine_ref, router_ref, router_turned_ref, first_ref, last_ref = refs[:8]
    refs = refs[8 + alias :]
    back_refs, refs = refs[: near if kind else 1], refs[near if kind else 1 :]
    all_ref, act_ref, grad_up_ref, scaled_ref, grad_router_ref = refs[:5]
    gate_ref, other_ref, out_acc, back_acc, slot_ref, partner_ref, out_ref, back_ref, sem = refs[5:]
    step = pl.program_id(0)
    total = scaled_ref.shape[0]
    _, sources, length = ids_ref.shape
    capacity = total // near
    mine = mine_ref[0, 0]
    base = mine // near * near
    tile = total

    @pl.when(step == 0)
    def _():
        first, second = ids_ref[0], ids_ref[1]
        named = (first == mine) | (second == mine)
        before = hot(iota((length, length), 0) < iota((length, length), 1))
        place = dot(hot(named), before).astype(jnp.int32)
        slot_ref[...] = jnp.where(named, place, -1)
        partner_ref[...] = jnp.where(first == mine, second, first).astype(F32)
        for d in range(near):
            at = slice(d * capacity, (d + 1) * capacity)
            source = pl.ds((base + d) ^ (kind * near), 1)
            here = iota((capacity, length), 0) == slot_ref[source, :]
            other_ref[at, :] = jnp.sum(
                jnp.where(here, partner_ref[source, :], 0.0), axis=1, keepdims=True
            ).astype(jnp.int32)
        lane = iota((total, LANES), 1)
        logits = dot(sent_ref[...].reshape(total, -1), router_ref[...])
        gap = jnp.sum(
            jnp.where(lane == mine, logits, 0.0) - jnp.where(lane == other_ref[...], logits, 0.0),
            axis=1, keepdims=True,
        )
        small = jnp.exp(-jnp.abs(gap))
        gate = jnp.where(gap >= 0, 1.0, small) / (1.0 + small)
        gate_ref[...] = gate
        scaled_ref[...] = (gate * cots_ref[...].reshape(total, -1).astype(F32)).astype(BF16)

    first_weight, last_weight = first_ref[...], last_ref[...]
    rows = sent_ref[...].reshape(total, -1)
    scaled = scaled_ref[...]
    up = dot(rows, first_weight)
    grad_act = dot_nt(scaled, last_weight)
    square = up * up
    half = 0.5 * jnp.tanh(up * (gelu_a + (gelu_a * gelu_b) * square)) + 0.5
    act = up * half
    slope = half + (act * (1.0 - half)) * (2 * gelu_a + (6 * gelu_a * gelu_b) * square)
    act_low = act.astype(BF16)
    grad_up = (grad_act * slope).astype(BF16)
    act_ref[...] = act_low
    grad_up_ref[...] = grad_up
    out_part = dot(act_low, last_weight)
    back_part = dot_nt(grad_up, first_weight)

    @pl.when(step == 0)
    def _():
        out_acc[...] = out_part
        back_acc[...] = back_part

    @pl.when(step > 0)
    def _():
        out_acc[...] += out_part
        back_acc[...] += back_part

    @pl.when(step == pl.num_programs(0) - 1)
    def _():
        copies, parts = [], []
        lane = iota((capacity, LANES), 1)
        here = pl.ds(part * capacity, capacity)
        for d in range(near):
            at = slice(d * capacity, (d + 1) * capacity)
            produced = out_acc[at, :].astype(BF16).astype(F32)
            gate = gate_ref[at, :]
            out_ref[at, :] = (gate * produced).astype(BF16)
            copies.append(pltpu.make_async_copy(out_ref.at[at, :], all_ref.at[d, here, :], sem.at[0, d]))
            copies[-1].start()
            grad_gate = jnp.sum(cots_ref[d].astype(F32) * produced, axis=1, keepdims=True)
            share = gate * (1.0 - gate) * grad_gate
            signed = jnp.where(lane == mine, share, 0.0) - jnp.where(lane == other_ref[at, :], share, 0.0)
            high = signed.astype(BF16)
            rest = (signed - high.astype(F32)).astype(BF16)
            parts.append(jnp.concatenate([high, rest], axis=1))
            routed = dot(parts[-1], router_turned_ref[...])
            back = (back_acc[at, :] + routed).astype(BF16)
            if kind:
                for e in range(near):
                    @pl.when((mine % near) ^ d == e)
                    def _():
                        back_refs[e][...] = back
            else:
                back_ref[at, :] = back
                copies.append(pltpu.make_async_copy(back_ref.at[at, :], back_refs[0].at[d, here, :], sem.at[1, d]))
                copies[-1].start()
        both = dot_tn(jnp.concatenate(parts, axis=0), rows)
        grad_router_ref[...] = both[:LANES] + both[LANES:]
        for copy in copies:
            copy.wait()


def expert_grad_kernel(parts, flat, half_ref, *refs):
    total = None
    for a_ref, b_ref in zip(refs[:parts], refs[parts : 2 * parts]):
        a, b = a_ref[...], b_ref[...]
        product = dot_tn(a.reshape(-1, a.shape[-1]), b)
        total = product if total is None else total + product
    if len(refs) > 2 * parts + 1:
        total = total + refs[2 * parts][...].astype(F32)
    refs[-1][...] = total.astype(BF16)


def join_kernel(odd_ref, mine_ref, other_ref, out_ref):
    own = pl.program_id(0) == odd_ref[0]
    out_ref[...] = jnp.where(own, mine_ref[...], other_ref[...]).astype(F32)


def dense_grad_kernel(n0, n1, g0, g1, m0, m1, b0, b1, small, left_ref, right_ref):
    width = n0.shape[1]
    left_ref[...] = (dot_tn(n0[...], g0[:, : 2 * width]) + dot_tn(n1[...], g1[:, : 2 * width])).astype(BF16)
    right_ref[:, :width] = (dot_tn(n0[...], g0[:, 2 * width :]) + dot_tn(n1[...], g1[:, 2 * width :])).astype(BF16)
    right_ref[:, width : 2 * width] = (dot_tn(m0[...], b0[...]) + dot_tn(m1[...], b1[...])).astype(BF16)
    right_ref[:, 2 * width :] = small[...]


def combine_kernel(out_ref, far_ref, mine_ref, col_ref, hidden_ref, result_ref, pick_ref):
    near, capacity, _ = out_ref.shape
    fill_pick(col_ref, pick_ref, mine_ref[0, 0] // near * near * capacity)
    rows = out_ref[...].reshape(near * capacity, -1)
    summed = dot(pick_ref[...], rows) + far_ref[...].astype(F32)
    result_ref[...] = (hidden_ref[...] + summed).astype(BF16)


def cost(flops, byte_count, transcendentals=0):
    return pl.CostEstimate(flops=int(SCALE * flops), bytes_accessed=int(byte_count), transcendentals=int(transcendentals))


def shaped(shape, dtype):
    return jax.ShapeDtypeStruct(shape, dtype)


def later(kernel, count, ties):
    if not ties:
        return kernel
    return lambda *refs: kernel(*refs[:count], *refs[count + ties :])


def make_strip(base, after):
    heads, width = base.shape
    return pl.pallas_call(
        later(strip_kernel, 1, len(after)),
        in_specs=[VECTOR] + [ANYWHERE] * len(after),
        out_shape=shaped((heads, STRIP, width - STRIP), BF16),
        compiler_params=params(),
        cost_estimate=cost(0, 0),
    )(base, *after)


def place(ids, far_ids, mine, experts, near, capacity):
    length = ids.shape[0]
    row, col = shaped((2, length), jnp.int32), shaped((length, 2), jnp.int32)
    return pl.pallas_call(
        functools.partial(slots_kernel, experts, near, capacity),
        out_shape=(row, row, col, col),
        in_specs=[VECTOR] * 4 + [SCALAR],
        compiler_params=params(),
        cost_estimate=cost(0, 0),
    )(ids.T, ids, far_ids, far_ids.T, mine)


def scatter(near, capacity, *parts, after=()):
    slots = [part[0] for part in parts]
    values = [value for part in parts for value, _ in part[1]]
    picks = [[pick for _, pick in part[1]] for part in parts]
    length, width = slots[0].shape[1], values[0].shape[-1]
    total = near * capacity * len(parts)
    return pl.pallas_call(
        later(functools.partial(scatter_kernel, picks), len(slots) + len(values), len(after)),
        in_specs=[VECTOR] * (len(slots) + len(values)) + [ANYWHERE] * len(after),
        out_shape=shaped((near, capacity * len(parts), width), BF16),
        compiler_params=params(),
        cost_estimate=cost(2 * total * length * width, 6e6),
    )(*slots, *values, *after)


def gather(col, base, blocks, after):
    length, width = col[0].shape[0], blocks.shape[2]
    near, capacity = blocks.shape[0], blocks.shape[1] // 2
    total = near * capacity
    return pl.pallas_call(
        later(gather_kernel, 4, len(after)),
        out_shape=(shaped((length, width), BF16), shaped((length, width), BF16)),
        in_specs=[VECTOR] * 2 + [SCALAR, VECTOR] + [ANYWHERE] * len(after),
        scratch_shapes=[pltpu.VMEM((length, total), BF16), pltpu.VMEM((total, width), BF16)],
        compiler_params=params(),
        cost_estimate=cost(4 * total * length * width, 6e6),
    )(*col, base, blocks, *after)


def forward(m, x, gains, weight, strip, block_row, block_col, row_slots, near, capacity, after):
    _, length, width = x.shape
    heads = width // HEAD
    return pl.pallas_call(
        later(functools.partial(forward_kernel, m), 7, len(after)),
        in_specs=[VECTOR] * 7 + [ANYWHERE] * len(after),
        out_shape=(
            shaped((length, 3 * width), BF16),
            shaped((length, width), BF16),
            shaped((length, LANES), F32),
            shaped((length, width), F32),
            shaped((length, width), BF16),
            shaped((near, capacity, width), BF16),
        ),
        scratch_shapes=[
            pltpu.VMEM((2, length, length), F32), pltpu.VMEM((2, length, length), BF16), pltpu.VMEM((length, length), F32),
        ],
        compiler_params=params(),
        cost_estimate=cost(
            2 * length * width * 4 * width + 8 * heads * length * length * HEAD,
            24e6, heads * length * length,
        ),
    )(x, gains, weight, strip, block_row, block_col, row_slots, *after)


def backward(
    part, own, far, mine, col, cot, hidden, gains, weight, proj, totals, strip, block_row, block_col, x, after
):
    _, length, width = x.shape
    heads = width // HEAD
    near, capacity = own.shape[0], own.shape[1] // 2
    total = 2 * near * capacity
    return pl.pallas_call(
        later(functools.partial(backward_kernel, near, part), near + 13, len(after)),
        in_specs=[VECTOR] * (near + 1) + [SCALAR] + [VECTOR] * 11 + [ANYWHERE] * len(after),
        out_shape=(
            shaped((length, width), BF16),
            shaped((length, width), BF16),
            shaped((length, 3 * width), BF16),
            shaped((length, width), BF16),
            shaped((2, width), F32),
            shaped((heads, 2 * length), F32),
        ),
        scratch_shapes=[
            pltpu.VMEM((length, total), BF16),
            pltpu.VMEM((total, width), BF16),
            pltpu.VMEM((length, width), BF16),
            pltpu.VMEM((2, length, length), BF16),
            pltpu.VMEM((2, length, length), BF16),
            pltpu.VMEM((STRIP, 2 * length), F32),
            pltpu.VMEM((2, length, length), F32),
            pltpu.VMEM((2, length, length), F32),
            pltpu.VMEM((length, length), F32),
        ],
        compiler_params=params(),
        cost_estimate=cost(
            2 * length * width * 4 * width + 20 * heads * length * length * HEAD + 2 * total * length * width,
            30e6, heads * length * length,
        ),
    )(*far, own, mine, col, cot, hidden, gains, weight, proj, totals, strip, block_row, block_col, x, *after)


def block_of(count, near, capacity, width, index):
    return pl.BlockSpec((near, capacity, width), lambda f: (0, index, 0), pipeline_mode=pl.Buffered(1))


def expert(kind, part, sent, cots, ids, mine, router, router_turned, first, last, earlier, after):
    (sent, sent_block), (cots, cot_block) = sent, cots
    near, _, width = sent.shape
    experts = ids.shape[1]
    capacity = 3 * ids.shape[2] // experts
    total = near * capacity
    inner = first.shape[1]
    step = 768

    def whole(shape):
        return pl.BlockSpec(shape, lambda f: (0,) * len(shape), pipeline_mode=pl.Buffered(1))

    anywhere = pl.BlockSpec(memory_space=pl.ANY)
    shared = shaped((near, 2 * capacity, width), BF16)
    if kind:
        back_specs = tuple(whole((capacity, width)) for _ in range(near))
        back_shapes = tuple(shaped((capacity, width), BF16) for _ in range(near))
    else:
        back_specs, back_shapes = (anywhere,), (shared,)
    count = len(back_specs)
    alias = len(earlier)
    targets = (count,) if kind else (0, 1)
    outs = pl.pallas_call(
        later(functools.partial(expert_kernel, kind, near, alias, part), 8 + alias, len(after)),
        grid=(inner // step,),
        in_specs=[
            block_of(0, near, capacity, width, sent_block), block_of(0, near, capacity, width, cot_block),
            whole(ids.shape), SCALAR, whole(router.shape), whole(router_turned.shape),
            pl.BlockSpec((width, step), lambda f: (0, f)),
            pl.BlockSpec((step, width), lambda f: (f, 0)),
        ] + [anywhere] * (alias + len(after)),
        out_specs=back_specs + (
            anywhere,
            pl.BlockSpec((total, step), lambda f: (0, f)),
            pl.BlockSpec((total, step), lambda f: (0, f)),
            whole((total, width)), whole((LANES, width)),
        ),
        out_shape=back_shapes + (
            shared,
            shaped((total, inner), BF16), shaped((total, inner), BF16),
            shaped((total, width), BF16), shaped((LANES, width), F32),
        ),
        scratch_shapes=[
            pltpu.VMEM((total, 1), F32),
            pltpu.VMEM((total, 1), jnp.int32),
            pltpu.VMEM((total, width), F32),
            pltpu.VMEM((total, width), F32),
            pltpu.VMEM(ids.shape[1:], jnp.int32),
            pltpu.VMEM(ids.shape[1:], F32),
            pltpu.VMEM((total, width), BF16),
            pltpu.VMEM((total, width), BF16),
            pltpu.SemaphoreType.DMA((2, near)),
        ],
        input_output_aliases={8 + n: target for n, target in enumerate(targets)} if alias else {},
        compiler_params=params(dimension_semantics=("arbitrary",)),
        cost_estimate=cost(8 * total * width * inner, 30e6, total * inner),
    )(sent, cots, ids, mine, router, router_turned, first, last, *earlier, *after)
    backs = list(outs[:count])
    return (backs if kind else backs[0]), outs[count], outs[count + 1 :]


def last_grad(half, acts, scaled, received, after):
    total, inner = acts[0].shape
    width = scaled[0].shape[1]
    step = 512
    count = inner // 2 // step
    out_spec = pl.BlockSpec((step, width), lambda f, half: (f, 0))
    specs = [pl.BlockSpec((total, step), lambda f, half: (0, half[0] * count + f))] * len(acts)
    specs += [pl.BlockSpec((total, width), lambda f, half: (0, 0))] * len(acts)
    extra = [] if received is None else [received]
    return pl.pallas_call(
        later(functools.partial(expert_grad_kernel, len(acts), True), 1 + 2 * len(acts) + len(extra), len(after)),
        grid_spec=pltpu.PrefetchScalarGridSpec(
            num_scalar_prefetch=1, grid=(count,), in_specs=specs + [out_spec] * len(extra) + [ANYWHERE] * len(after),
            out_specs=out_spec
        ),
        out_shape=shaped((inner // 2, width), BF16),
        compiler_params=params(dimension_semantics=("arbitrary",)),
        cost_estimate=cost(len(acts) * total * inner * width, 15e6),
    )(half, *acts, *scaled, *extra, *after)


def first_grad(half, rows, ups, received, after):
    total, inner = ups[0].shape
    near, _, width = rows[0][0].shape
    capacity = total // near
    step = 768
    out_spec = pl.BlockSpec((width // 2, step), lambda f, half: (0, f))

    def row_spec(block):
        return pl.BlockSpec((near, capacity, width // 2), lambda f, half: (0, block, half[0]))

    specs = [row_spec(block) for _, block in rows]
    specs += [pl.BlockSpec((total, step), lambda f, half: (0, f))] * len(ups)
    extra = [] if received is None else [received]
    return pl.pallas_call(
        later(functools.partial(expert_grad_kernel, len(ups), False), 1 + 2 * len(ups) + len(extra), len(after)),
        grid_spec=pltpu.PrefetchScalarGridSpec(
            num_scalar_prefetch=1, grid=(inner // step,), in_specs=specs + [out_spec] * len(extra) + [ANYWHERE] * len(after),
            out_specs=out_spec
        ),
        out_shape=shaped((width // 2, inner), BF16),
        compiler_params=params(dimension_semantics=("arbitrary",)),
        cost_estimate=cost(len(ups) * total * inner * width, 25e6),
    )(half, *[array for array, _ in rows], *ups, *extra, *after)


def join(odd, mine, other, after):
    rows, columns = mine.shape
    step = rows // 3
    own = pl.BlockSpec((step, columns), lambda h, i, odd: (jnp.where(h == odd[0], i, 2 * (1 - h)), 0))
    far = pl.BlockSpec((step, columns), lambda h, i, odd: (jnp.where(h == odd[0], 2 * (1 - h), i), 0))
    return pl.pallas_call(
        later(join_kernel, 3, len(after)),
        grid_spec=pltpu.PrefetchScalarGridSpec(
            num_scalar_prefetch=1, grid=(2, 3), in_specs=[own, far] + [ANYWHERE] * len(after),
            out_specs=pl.BlockSpec((step, columns), lambda h, i, odd: (h * 3 + i, 0)),
        ),
        out_shape=shaped((2 * rows, columns), F32),
        compiler_params=params(dimension_semantics=("arbitrary", "arbitrary")),
        cost_estimate=cost(rows * columns, 20e6),
    )(odd, mine, other, *after)


def dense_grad(*arrays, after):
    small = arrays[-1]
    width = arrays[0].shape[1]
    length = arrays[0].shape[0]
    return pl.pallas_call(
        later(dense_grad_kernel, len(arrays), len(after)),
        in_specs=[VECTOR] * len(arrays) + [ANYWHERE] * len(after),
        out_shape=(shaped((width, 2 * width), BF16), shaped((width, 2 * width + small.shape[1]), BF16)),
        compiler_params=params(),
        cost_estimate=cost(4 * length * width * 4 * width, 20e6),
    )(*arrays, *after)


def combine(out_rows, part, far, mine, col, hidden, after):
    length, width = hidden.shape
    near, capacity = out_rows.shape[0], out_rows.shape[1] // 2
    total = near * capacity
    plain = pl.BlockSpec((length, width), lambda f: (0, 0))
    return pl.pallas_call(
        later(combine_kernel, 5, len(after)),
        grid=(1,),
        in_specs=[
            block_of(0, near, capacity, width, part), plain, SCALAR, pl.BlockSpec(col.shape, lambda f: (0, 0)), plain,
        ] + [ANYWHERE] * len(after),
        out_specs=plain,
        out_shape=shaped((length, width), BF16),
        scratch_shapes=[pltpu.VMEM((length, total), BF16)],
        compiler_params=params(),
        cost_estimate=cost(2 * total * length * width, 6e6),
    )(out_rows, far, mine, col, hidden, *after)


def swap(value, axis, size, bit):
    return lax.ppermute(value, axis, [(i, i ^ bit) for i in range(size)])


def pair_sum(a, b):
    return (a.astype(F32) + b.astype(F32)).astype(BF16)


def halve(value, axis, name, size, bit):
    odd = (lax.axis_index(name) & bit) > 0
    count = value.shape[axis] // 2
    low = lax.slice_in_dim(value, 0, count, axis=axis)
    high = lax.slice_in_dim(value, count, 2 * count, axis=axis)
    kept, sent = jnp.where(odd, high, low), jnp.where(odd, low, high)
    return pair_sum(kept, swap(sent, name, size, bit))


def unite(value, name, size, bit):
    odd = (lax.axis_index(name) & bit) > 0
    other = swap(value, name, size, bit)
    return jnp.concatenate([jnp.where(odd, other, value), jnp.where(odd, value, other)], axis=0)


def dense_sum(left, right, dp, experts, after):
    def split(value):
        return halve(value.reshape(dp // 2, 2, value.shape[0] // dp, value.shape[1]), 1, "dp", dp, 1)[:, 0]

    def along_dp(value):
        bit = 2
        while bit < dp:
            shape = value.shape
            value = halve(value.reshape(shape[0] // 2, 2, *shape[1:]), 1, "dp", dp, bit)[:, 0]
            bit *= 2
        return value

    left, right = split(left), split(right)
    left = after(0, along_dp(left))
    right = halve(right, 1, "expert", experts, 1)
    left = halve(left, 1, "expert", experts, 1)
    right = along_dp(right)
    rows = after(1, jnp.concatenate([left[0], right[0]], axis=1))
    step, bit = 2, 2
    while bit < experts:
        rows = after(step, halve(rows, 0, "expert", experts, bit))
        step, bit = step + 1, bit * 2
    while bit > 1:
        bit //= 2
        rows = unite(rows, "expert", experts, bit)
        rows = after({4: 8, 2: 9}.get(bit), rows)
    return rows.astype(F32)


def body(
    dp, experts, inputs, gain_one, w_qkv, w_out, rel_table, second_norm_gain, w_router, w_in, w_back,
    expert_ids, block_ids, cotangent,
):
    micro, length, width = inputs.shape
    capacity = 3 * length // experts
    near = experts // 2
    buckets, heads = rel_table.shape[0] * dp, rel_table.shape[1]
    shard = gain_one.shape[0]
    first_in, last_out = w_in[0], w_back[0]
    mine = lax.axis_index("expert").astype(jnp.int32).reshape(1, 1)

    groups = [list(range(near)), list(range(near, experts))]
    odd = (lax.axis_index("dp") & 1).astype(jnp.int32).reshape(1)

    def cross(value, bit):
        return swap(value, "expert", experts, bit)

    def around(blocks):
        return lax.all_to_all(
            blocks, "expert", split_axis=0, concat_axis=0, axis_index_groups=groups, tiled=True
        )

    def order(*values):
        return lax.optimization_barrier(values)

    middle = length // 2
    cot0_top, cot0_end = cross(cotangent[0, :middle], near), cross(cotangent[0, middle:], near)

    ids_row = jnp.transpose(expert_ids, (0, 2, 1))
    ids_all = lax.all_to_all(
        jnp.broadcast_to(ids_row[None], (experts,) + ids_row.shape), "expert", split_axis=0, concat_axis=0, tiled=True
    )
    ids_all = jnp.transpose(ids_all, (1, 2, 0, 3))
    ids_far = lax.dynamic_index_in_dim(ids_all, lax.axis_index("expert") ^ near, 2, keepdims=False)

    table_column = jnp.pad(rel_table.reshape(-1), (0, shard - rel_table.size))
    small = jnp.concatenate([gain_one[:, None], second_norm_gain[:, None], table_column[:, None], w_router], axis=1)
    extra = jnp.pad(small, ((0, 0), (0, LANES - small.shape[1])))
    bit = 1
    while bit < dp:
        other = swap(extra, "dp", dp, bit)
        high = (lax.axis_index("dp") & bit) > 0
        extra = jnp.concatenate([jnp.where(high, other, extra), jnp.where(high, extra, other)], axis=0)
        bit *= 2
    packed = lax.all_gather(jnp.concatenate([w_qkv, w_out], axis=1), "dp", axis=0, tiled=True)
    gains = extra[:, :2].astype(F32).T
    table = extra[:, 2].reshape(dp, shard)[:, : rel_table.size].reshape(buckets, heads)
    router = jnp.pad(extra[:, 3 : 3 + experts], ((0, 0), (0, LANES - experts)))
    router_turned = jnp.concatenate([router.T, router.T], axis=0)
    levels = bucket_table(length, buckets)
    base = lax.dot_general(
        table, jnp.asarray(levels, BF16), (((0,), (0,)), ((), ())), preferred_element_type=F32
    )
    strip = make_strip(base, [])
    places = [place(expert_ids[m], ids_far[m], mine, experts, near, capacity) for m in range(micro)]

    kept = []
    block_cols = block_ids[:, 0, :].T

    def layer_front(m, after):
        block_row, block_col = block_ids, block_cols
        proj, mixed, totals, hidden, second, send = forward(
            m, inputs, gains, packed, strip, block_row, block_col, places[m][0], near, capacity, after
        )
        kept.append((proj, mixed, totals, hidden, block_row, block_col))
        return second, send

    cot_own = around(
        scatter(near, capacity, (places[0][0], [(cotangent, 0)]), (places[1][0], [(cotangent, 1)]), after=[cot0_top, strip])
    )
    second0, send0 = layer_front(0, [])
    second0_far = cross(second0, near)
    own0 = around(send0)
    second1, send1 = layer_front(1, [send0, cot0_end])
    own1 = around(send1)

    common = (mine, router, router_turned, first_in, last_out)
    cot1_far = cross(order(cotangent[1], second0_far, send1)[0], near)
    second1_far = cross(order(second1, second0_far)[0], near)
    far0_send = scatter(
        near, capacity, (places[0][1], [(cot0_top, None), (cot0_end, None)]), (places[0][1], [(second0_far, None)]),
        after=[send1],
    )
    back_own, out_own, kept0_own = expert(
        0, 0, (own0, 0), (cot_own, 0), ids_all[0], *common, (), [far0_send]
    )
    far0 = around(order(far0_send, out_own)[0])
    back_own, out_own, kept1_own = expert(
        0, 1, (own1, 0), (cot_own, 1), ids_all[1], *common, (back_own, out_own), []
    )
    far1_send = scatter(
        near, capacity, (places[1][1], [(cot1_far, None)]), (places[1][1], [(second1_far, None)]), after=[out_own],
    )
    far1 = around(far1_send)
    back0_far, out_far, kept0_far = expert(1, 0, (far0, 1), (far0, 0), ids_all[0], *common, (), [far1_send])
    back1_far, out_far, kept1_far = expert(1, 1, (far1, 1), (far1, 0), ids_all[1], *common, (out_far,), [])
    back_own, out_own, _ = order(back_own, out_own, back0_far[0])
    back_own, out_own, out_far = around(back_own), around(out_own), around(out_far)
    home = [
        [cross(block, near | d) for d, block in enumerate(back0_far)],
        [cross(block, near | d) for d, block in enumerate(back1_far)],
    ]
    quarter = max(1, near // 4)

    parts = (kept0_own, kept1_own, kept0_far, kept1_far)
    acts, ups, scaled, routers = zip(*parts)
    rows = ((own0, 0), (own1, 0), (far0, 1), (far1, 1))
    grad_router = sum(routers)[:experts].T

    home0, home1 = home
    other = 1 - odd
    last_part = last_grad(other, acts, scaled, None, home0[: 2 * quarter] + [back_own])
    last_got = swap(last_part, "dp", dp, 1)
    first_part = first_grad(other, rows, ups, None, [last_part] + home0[2 * quarter : 3 * quarter])
    first_got = swap(first_part, "dp", dp, 1)
    last_sum = last_grad(odd, acts, scaled, last_got, [first_part] + home0[3 * quarter :])
    first_sum = first_grad(odd, rows, ups, first_got, [last_sum] + home1[:quarter])
    first_whole = first_sum

    def over_dp(value):
        bit = 2
        while bit < dp:
            other = swap(value, "dp", dp, bit)
            value = pair_sum(value, other)
            bit *= 2
        return value, other

    def pieces(value):
        count = value.shape[0] // 4
        return [value[n * count : (n + 1) * count] for n in range(4)]

    last_sum, last_came = zip(*[over_dp(piece) for piece in pieces(last_sum)])
    first_sum = pieces(first_sum)
    first_sum[:3], first_came = map(list, zip(*[over_dp(piece) for piece in first_sum[:3]]))

    def layer_back(m, after):
        proj, mixed, totals, hidden, block_row, block_col = kept[m]
        return backward(
            m, back_own, home[m], mine, places[m][2], cotangent, hidden, gains, packed, proj, totals, strip,
            block_row, block_col, inputs, after,
        )

    back_outs = [layer_back(0, [first_whole, last_came[0]] + home1[quarter : 2 * quarter])]
    out_sums = gather((places[0][3], places[1][3]), mine, out_far, [back_outs[0][1]])
    out0_far, out1_far = cross(out_sums[0], near), cross(out_sums[1], near)
    back_outs.append(layer_back(1, [last_came[1], last_came[2], out_sums[0]]))

    gain_grads = back_outs[0][4] + back_outs[1][4]
    diagonals = back_outs[0][5] + back_outs[1][5]
    table_grad = lax.dot_general(
        jnp.asarray(levels, F32), diagonals, (((1,), (1,)), ((), ())),
        precision=lax.Precision.HIGHEST, preferred_element_type=F32,
    )
    table_grad = jnp.pad(table_grad.reshape(dp, rel_table.size), ((0, 0), (0, shard - rel_table.size)))
    small_grad = jnp.concatenate([gain_grads.T, table_grad.reshape(width, 1), grad_router], axis=1).astype(BF16)
    small_grad = jnp.pad(small_grad, ((0, 0), (0, LANES - small_grad.shape[1])))
    left, right = dense_grad(
        back_outs[0][3], back_outs[1][3], back_outs[0][2], back_outs[1][2],
        kept[0][1], kept[1][1], back_outs[0][1], back_outs[1][1], small_grad,
        after=[last_came[3], *first_came, out0_far, out_own],
    )
    results = [combine(out_own, 0, out0_far, mine, places[0][2], kept[0][3], [left])]
    last_sum = jnp.concatenate(last_sum, axis=0)
    grad_last = join(odd, last_sum, swap(last_sum, "dp", dp, 1), [left])

    def after(step, value):
        nonlocal grad_last, out1_far
        if step == 1:
            value, grad_last, out1_far, *rest = order(value, grad_last, out1_far, *first_sum[3:])
            results.append(combine(out_own, 1, out1_far, mine, places[1][2], kept[1][3], [results[0], grad_last]))
            rest, came = zip(*[over_dp(piece) for piece in rest])
            first_sum[3:] = rest
            first_came.extend(came)
        if step == 2:
            value, results[0] = order(value, results[0])
        if step == 3:
            value, results[1] = order(value, results[1])
        if step == 8:
            value, first_came[3] = order(value, first_came[3])
        return value

    dense = dense_sum(left, right, dp, experts, after)
    first_sum = jnp.concatenate(first_sum, axis=0)
    grad_first = join(odd, first_sum, swap(first_sum, "dp", dp, 1), [results[1]])
    tail = dense[:, 4 * width :]
    return (
        jnp.stack(results),
        jnp.stack([out[0] for out in back_outs]),
        tail[:, 0],
        dense[:, : 3 * width],
        dense[:, 3 * width : 4 * width],
        tail[: rel_table.size, 2].reshape(rel_table.shape),
        tail[:, 1],
        tail[:, 3 : 3 + experts],
        grad_first[None],
        grad_last[None],
    )


def solution(mesh):
    split = P(None, ("dp", "expert"), None)
    in_specs = (
        split, P("dp"), P("dp", None), P("dp", None), P("dp", None), P("dp"), P("dp", None),
        P("expert", None, None), P("expert", None, None), split, split, split,
    )
    out_specs = (
        split, split, P("dp"), P("dp", None), P("dp", None), P("dp", None), P("dp"), P("dp", None),
        P("expert", None, None), P("expert", None, None),
    )
    return jax.shard_map(
        functools.partial(body, mesh.shape["dp"], mesh.shape["expert"]), mesh=mesh, in_specs=in_specs, out_specs=out_specs, check_vma=False
    )
```

```python
import functools

import jax
import jax.numpy as jnp
import numpy as np
from jax import lax
from jax.experimental import pallas as pl
from jax.experimental.pallas import tpu as pltpu
from jax.sharding import PartitionSpec as P

HEAD = 64
PAIR = 2 * HEAD
STRIP = 128
LANES = 128
VMEM_BYTES = 60 * 1024 * 1024
SCALE = 5
VECTOR = pl.BlockSpec(memory_space=pltpu.VMEM)
SCALAR = pl.BlockSpec(memory_space=pltpu.SMEM)
ANYWHERE = pl.BlockSpec(memory_space=pl.ANY)

epsilon = 1e-06
bucket_edges = (12, 16, 23, 32, 46, 64, 91)
masked_score = -1e30
gelu_a = float(np.sqrt(2.0 / np.pi))
gelu_b = 0.044715

F32 = jnp.float32
BF16 = jnp.bfloat16


def dot(a, b):
    return jnp.dot(a, b, preferred_element_type=F32)


def dot_nt(a, b):
    return lax.dot_general(a, b, (((1,), (1,)), ((), ())), preferred_element_type=F32)


def dot_tn(a, b):
    return lax.dot_general(a, b, (((0,), (0,)), ((), ())), preferred_element_type=F32)


def iota(shape, dim):
    return lax.broadcasted_iota(jnp.int32, shape, dim)


def hot(mask):
    return jnp.where(mask, 1.0, 0.0).astype(BF16)


def params(**extra):
    return pltpu.CompilerParams(vmem_limit_bytes=VMEM_BYTES, **extra)


def bucket_table(length, buckets):
    offset = np.arange(2 * length) - (length - 1)
    distance = np.abs(offset)
    far = 8 + sum((distance >= edge).astype(np.int32) for edge in bucket_edges)
    bucket = np.where(distance < 8, distance, far) + 16 * (offset > 0)
    table = (bucket[None, :] == np.arange(buckets)[:, None]) & (offset < length)[None, :]
    return table.astype(np.float32)


def strip_kernel(base_ref, out_ref):
    heads, width = base_ref.shape
    for h in range(heads):
        row = jnp.broadcast_to(base_ref[h : h + 1, :], (STRIP, width))
        rolled = pltpu.roll(row, width - (STRIP - 1), 1, stride=1, stride_axis=0)
        out_ref[h] = rolled[:, : width - STRIP].astype(BF16)


def slots_kernel(experts, near, capacity, ids_row_ref, ids_col_ref, far_row_ref, far_col_ref, mine_ref, row_ref, row_far_ref, col_ref, col_far_ref):
    length = ids_row_ref.shape[1]
    base = mine_ref[0, 0] // near * near
    padded = max(16, experts)
    before = hot(iota((length, length), 0) < iota((length, length), 1))
    for ids_row, row_out in ((ids_row_ref, row_ref), (far_row_ref, row_far_ref)):
        level = iota((padded, length), 0)
        first, second = ids_row[0:1, :], ids_row[1:2, :]
        place = dot(hot((level == first) | (level == second)), before).astype(jnp.int32)
        block = level - base
        slot = jnp.where((block >= 0) & (block < near), place + block * capacity, -1)
        row_out[0:1, :] = jnp.sum(jnp.where(level == first, slot, 0), axis=0, keepdims=True)
        row_out[1:2, :] = jnp.sum(jnp.where(level == second, slot, 0), axis=0, keepdims=True)

    after = hot(iota((length, length), 1) < iota((length, length), 0))
    for ids_col, col_out in ((ids_col_ref, col_ref), (far_col_ref, col_far_ref)):
        level = iota((length, LANES), 1)
        first, second = ids_col[:, 0:1], ids_col[:, 1:2]
        slot = dot(after, hot((level == first) | (level == second))) + (level * capacity).astype(F32)
        col_out[:, 0:1] = jnp.sum(jnp.where(level == first, slot, 0.0), axis=1, keepdims=True).astype(jnp.int32)
        col_out[:, 1:2] = jnp.sum(jnp.where(level == second, slot, 0.0), axis=1, keepdims=True).astype(jnp.int32)


def scatter_kernel(picks, *refs):
    count = len(picks)
    slots, refs, send_ref = refs[:count], refs[count:-1], refs[-1]
    values = []
    for part in picks:
        values.append([ref if pick is None else ref.at[pick] for pick, ref in zip(part, refs)])
        refs = refs[len(part) :]
    scatter_parts(slots, values, send_ref)


def scatter_parts(slot_refs, value_refs, send_ref):
    near, length = send_ref.shape[0], slot_refs[0].shape[1]
    count = len(slot_refs)
    capacity = send_ref.shape[1] // count
    for n in range(count):
        first, second = slot_refs[n][0:1, :], slot_refs[n][1:2, :]
        values = [ref[...] for ref in value_refs[n]]
        for d in range(near):
            slots = iota((capacity, length), 0) + d * capacity
            pick = hot((slots == first) | (slots == second))
            total, start = None, 0
            for value in values:
                part = dot(pick[:, start : start + value.shape[0]], value)
                total = part if total is None else total + part
                start += value.shape[0]
            send_ref[d, n * capacity : (n + 1) * capacity, :] = total.astype(BF16)


def fill_pick(col_ref, pick_ref, offset=0):
    length, total = pick_ref.shape
    first, second = col_ref[:, 0:1] - offset, col_ref[:, 1:2] - offset
    step = 256
    for start in range(0, total, step):
        slots = iota((length, step), 1) + start
        pick_ref[:, start : start + step] = hot((slots == first) | (slots == second))


def gather_kernel(first_ref, second_ref, mine_ref, blocks_ref, first_sum_ref, second_sum_ref, pick_ref, near_ref):
    near, pair_rows, _ = blocks_ref.shape
    capacity = pair_rows // 2
    offset = mine_ref[0, 0] // near * near * capacity
    for part, (col_ref, sum_ref) in enumerate(((first_ref, first_sum_ref), (second_ref, second_sum_ref))):
        fill_pick(col_ref, pick_ref, offset)
        for d in range(near):
            near_ref[d * capacity : (d + 1) * capacity, :] = blocks_ref[d, part * capacity : (part + 1) * capacity, :]
        sum_ref[...] = dot(pick_ref[...], near_ref[...]).astype(BF16)


def head_mask(length):
    return iota((length, PAIR), 1) < HEAD


def forward_kernel(
    m, x_ref, gains_ref, weight_ref, strip_ref, block_row_ref, block_col_ref, row_ref,
    proj_ref, mixed_ref, total_ref, hidden_ref, second_ref, send_ref,
    score_ref, weight_part_ref, mask_ref,
):
    _, length, width = x_ref.shape
    scale = HEAD ** (-0.5)
    x = x_ref[m].astype(F32)
    r1 = lax.rsqrt(jnp.mean(x * x, axis=1, keepdims=True) + epsilon)
    normed = (x * r1 * gains_ref[0:1, :]).astype(BF16)
    proj_ref[...] = dot(normed, weight_ref[:, : 3 * width]).astype(BF16)
    total_ref[...] = jnp.zeros_like(total_ref)

    mask_ref[...] = jnp.where(block_row_ref[m] <= block_col_ref[:, m : m + 1], 0.0, masked_score)
    lane = iota((STRIP, LANES), 1)

    def pair(p, carry):
        lanes = pl.multiple_of(p * PAIR, PAIR)
        q = proj_ref[:, pl.ds(lanes, PAIR)] * scale
        k = proj_ref[:, pl.ds(width + lanes, PAIR)]
        v = proj_ref[:, pl.ds(2 * width + lanes, PAIR)]
        left = head_mask(length)
        zero = jnp.zeros_like(k)
        keeps = (left, jnp.logical_not(left))
        for h in range(2):
            score_ref[h] = dot_nt(q, jnp.where(keeps[h], k, zero))
        for h in range(2):
            strip = strip_ref[2 * p + h].astype(F32)
            for i in range(length // STRIP):
                rows = slice(i * STRIP, (i + 1) * STRIP)
                start = length - STRIP - i * STRIP
                s = (score_ref[h, rows, :] + strip[:, start : start + length]) + mask_ref[rows, :]
                top = jnp.max(s, axis=1, keepdims=True)
                e = jnp.exp(s - top)
                total = jnp.sum(e, axis=1, keepdims=True)
                weight_part_ref[h, rows, :] = (e * (1.0 / total)).astype(BF16)
                total_ref[rows, :] = jnp.where(lane == 2 * p + h, top + jnp.log(total), total_ref[rows, :])
        out = dot(weight_part_ref[0], jnp.where(keeps[0], v, zero)) + dot(weight_part_ref[1], jnp.where(keeps[1], v, zero))
        mixed_ref[:, pl.ds(lanes, PAIR)] = out.astype(BF16)
        return carry

    lax.fori_loop(0, width // PAIR, pair, 0)
    hidden = x + dot(mixed_ref[...], weight_ref[:, 3 * width : 4 * width])
    hidden_ref[...] = hidden
    r2 = lax.rsqrt(jnp.mean(hidden * hidden, axis=1, keepdims=True) + epsilon)
    second_ref[...] = (hidden * r2 * gains_ref[1:2, :]).astype(BF16)
    scatter_parts([row_ref], [[second_ref]], send_ref)


def backward_kernel(near, part, *refs):
    backward_main(part, refs[:near], *refs[near:])


def backward_main(
    part, far_refs, own_ref, mine_ref, col_ref, cot_ref, hidden_ref, gains_ref, weight_ref, proj_ref, total_ref, strip_ref,
    block_row_ref, block_col_ref, x_ref,
    grad_x_ref, branch_ref, grad_proj_ref, normed_ref, grad_gain_ref, diagonal_ref,
    pick_ref, back_ref, grad_mixed_ref, low_ref, prob_ref, strip_sum_ref, score_ref, grad_prob_ref, mask_ref,
):
    _, length, width = cot_ref.shape
    scale = HEAD ** (-0.5)
    near, capacity, _ = own_ref.shape
    mine = mine_ref[0, 0]
    base = mine // near * near
    for d in range(near):
        own = own_ref[d]
        back_ref[pl.ds(pl.multiple_of((base + d) * capacity, 16), capacity), :] = own
        back_ref[pl.ds(pl.multiple_of((mine ^ (near | d)) * capacity, 16), capacity), :] = far_refs[d][...]
    fill_pick(col_ref, pick_ref)
    grad_second = dot(pick_ref[...], back_ref[...])
    hidden = hidden_ref[...]
    r2 = lax.rsqrt(jnp.mean(hidden * hidden, axis=1, keepdims=True) + epsilon)
    scaled = grad_second * gains_ref[1:2, :]
    inner = jnp.mean(hidden * scaled, axis=1, keepdims=True)
    grad_hidden = cot_ref[part].astype(F32) + r2 * scaled - hidden * (r2 * r2 * r2 * inner)
    grad_gain_ref[1:2, :] = jnp.sum(grad_second * hidden * r2, axis=0, keepdims=True)
    branch = grad_hidden.astype(BF16)
    branch_ref[...] = branch
    grad_mixed_ref[...] = dot_nt(branch, weight_ref[:, 3 * width : 4 * width]).astype(BF16)

    mask_ref[...] = jnp.where(block_row_ref[part] <= block_col_ref[:, part : part + 1], 0.0, masked_score)
    lane = iota((STRIP, LANES), 1)

    def pair(p, carry):
        lanes = pl.multiple_of(p * PAIR, PAIR)
        q = proj_ref[:, pl.ds(lanes, PAIR)]
        k = proj_ref[:, pl.ds(width + lanes, PAIR)]
        v = proj_ref[:, pl.ds(2 * width + lanes, PAIR)]
        g = grad_mixed_ref[:, pl.ds(lanes, PAIR)]
        q_turned = q.astype(F32).T.astype(BF16)
        g_turned = g.astype(F32).T.astype(BF16)
        left = head_mask(length)
        zero = jnp.zeros_like(k)
        keeps = (left, jnp.logical_not(left))
        scaled_q = q * scale
        for h in range(2):
            score_ref[h] = dot_nt(scaled_q, jnp.where(keeps[h], k, zero))
            grad_prob_ref[h] = dot_nt(g, jnp.where(keeps[h], v, zero))
        keys, values = [], []
        for h in range(2):
            strip = strip_ref[2 * p + h].astype(F32)
            strip_sum_ref[...] = jnp.zeros_like(strip_sum_ref)
            for i in range(length // STRIP):
                rows = slice(i * STRIP, (i + 1) * STRIP)
                start = length - STRIP - i * STRIP
                s = (score_ref[h, rows, :] + strip[:, start : start + length]) + mask_ref[rows, :]
                row_total = jnp.sum(jnp.where(lane == 2 * p + h, total_ref[rows, :], 0.0), axis=1, keepdims=True)
                prob = jnp.exp(s - row_total)
                grad_prob = grad_prob_ref[h, rows, :]
                row_inner = jnp.sum(prob * grad_prob, axis=1, keepdims=True)
                grad_score = prob * (grad_prob - row_inner)
                strip_sum_ref[:, start : start + length] += grad_score
                low_ref[h, rows, :] = grad_score.astype(BF16)
                prob_ref[h, rows, :] = prob.astype(BF16)
            half = slice(h * HEAD, (h + 1) * HEAD)
            keys.append(dot(q_turned[half], low_ref[h]))
            values.append(dot(g_turned[half], prob_ref[h]))
            gathered = jnp.zeros((8, 2 * length), F32)
            for a in range(STRIP // 8):
                piece = strip_sum_ref[8 * a : 8 * a + 8, :]
                gathered += pltpu.roll(piece, STRIP - 8 - 8 * a, 1) if a < STRIP // 8 - 1 else piece
            line = gathered[7:8]
            for b in range(7):
                line += pltpu.roll(gathered[b : b + 1], 7 - b, 1)
            diagonal_ref[pl.ds(2 * p + h, 1), :] = line
        grad_query = dot(low_ref[0], jnp.where(keeps[0], k, zero)) + dot(low_ref[1], jnp.where(keeps[1], k, zero))
        grad_proj_ref[:, pl.ds(lanes, PAIR)] = (grad_query * scale).astype(BF16)
        grad_key = jnp.concatenate(keys, axis=0).T
        grad_value = jnp.concatenate(values, axis=0).T
        grad_proj_ref[:, pl.ds(width + lanes, PAIR)] = (grad_key * scale).astype(BF16)
        grad_proj_ref[:, pl.ds(2 * width + lanes, PAIR)] = grad_value.astype(BF16)
        return carry

    lax.fori_loop(0, width // PAIR, pair, 0)
    x = x_ref[part].astype(F32)
    r1 = lax.rsqrt(jnp.mean(x * x, axis=1, keepdims=True) + epsilon)
    normed_ref[...] = (x * r1 * gains_ref[0:1, :]).astype(BF16)
    grad_normed = dot_nt(grad_proj_ref[...], weight_ref[:, : 3 * width])
    scaled = grad_normed * gains_ref[0:1, :]
    inner = jnp.mean(x * scaled, axis=1, keepdims=True)
    grad_gain_ref[0:1, :] = jnp.sum(grad_normed * x * r1, axis=0, keepdims=True)
    grad_x_ref[...] = (grad_hidden + r1 * scaled - x * (r1 * r1 * r1 * inner)).astype(BF16)


def expert_kernel(
    kind, near, alias, part, *refs,
):
    sent_ref, cots_ref, ids_ref, mine_ref, router_ref, router_turned_ref, first_ref, last_ref = refs[:8]
    refs = refs[8 + alias :]
    back_refs, refs = refs[: near if kind else 1], refs[near if kind else 1 :]
    all_ref, act_ref, grad_up_ref, scaled_ref, grad_router_ref = refs[:5]
    gate_ref, other_ref, out_acc, back_acc, slot_ref, partner_ref, out_ref, back_ref, sem = refs[5:]
    step = pl.program_id(0)
    total = scaled_ref.shape[0]
    _, sources, length = ids_ref.shape
    capacity = total // near
    mine = mine_ref[0, 0]
    base = mine // near * near
    tile = total

    @pl.when(step == 0)
    def _():
        first, second = ids_ref[0], ids_ref[1]
        named = (first == mine) | (second == mine)
        before = hot(iota((length, length), 0) < iota((length, length), 1))
        place = dot(hot(named), before).astype(jnp.int32)
        slot_ref[...] = jnp.where(named, place, -1)
        partner_ref[...] = jnp.where(first == mine, second, first).astype(F32)
        for d in range(near):
            at = slice(d * capacity, (d + 1) * capacity)
            source = pl.ds((base + d) ^ (kind * near), 1)
            here = iota((capacity, length), 0) == slot_ref[source, :]
            other_ref[at, :] = jnp.sum(
                jnp.where(here, partner_ref[source, :], 0.0), axis=1, keepdims=True
            ).astype(jnp.int32)
        lane = iota((total, LANES), 1)
        logits = dot(sent_ref[...].reshape(total, -1), router_ref[...])
        gap = jnp.sum(
            jnp.where(lane == mine, logits, 0.0) - jnp.where(lane == other_ref[...], logits, 0.0),
            axis=1, keepdims=True,
        )
        small = jnp.exp(-jnp.abs(gap))
        gate = jnp.where(gap >= 0, 1.0, small) / (1.0 + small)
        gate_ref[...] = gate
        scaled_ref[...] = (gate * cots_ref[...].reshape(total, -1).astype(F32)).astype(BF16)

    first_weight, last_weight = first_ref[...], last_ref[...]
    rows = sent_ref[...].reshape(total, -1)
    scaled = scaled_ref[...]
    up = dot(rows, first_weight)
    grad_act = dot_nt(scaled, last_weight)
    square = up * up
    half = 0.5 * jnp.tanh(up * (gelu_a + (gelu_a * gelu_b) * square)) + 0.5
    act = up * half
    slope = half + (act * (1.0 - half)) * (2 * gelu_a + (6 * gelu_a * gelu_b) * square)
    act_low = act.astype(BF16)
    grad_up = (grad_act * slope).astype(BF16)
    act_ref[...] = act_low
    grad_up_ref[...] = grad_up
    out_part = dot(act_low, last_weight)
    back_part = dot_nt(grad_up, first_weight)

    @pl.when(step == 0)
    def _():
        out_acc[...] = out_part
        back_acc[...] = back_part

    @pl.when(step > 0)
    def _():
        out_acc[...] += out_part
        back_acc[...] += back_part

    @pl.when(step == pl.num_programs(0) - 1)
    def _():
        copies, parts = [], []
        lane = iota((capacity, LANES), 1)
        here = pl.ds(part * capacity, capacity)
        for d in range(near):
            at = slice(d * capacity, (d + 1) * capacity)
            produced = out_acc[at, :].astype(BF16).astype(F32)
            gate = gate_ref[at, :]
            out_ref[at, :] = (gate * produced).astype(BF16)
            copies.append(pltpu.make_async_copy(out_ref.at[at, :], all_ref.at[d, here, :], sem.at[0, d]))
            copies[-1].start()
            grad_gate = jnp.sum(cots_ref[d].astype(F32) * produced, axis=1, keepdims=True)
            share = gate * (1.0 - gate) * grad_gate
            signed = jnp.where(lane == mine, share, 0.0) - jnp.where(lane == other_ref[at, :], share, 0.0)
            high = signed.astype(BF16)
            rest = (signed - high.astype(F32)).astype(BF16)
            parts.append(jnp.concatenate([high, rest], axis=1))
            routed = dot(parts[-1], router_turned_ref[...])
            back = (back_acc[at, :] + routed).astype(BF16)
            if kind:
                for e in range(near):
                    @pl.when((mine % near) ^ d == e)
                    def _():
                        back_refs[e][...] = back
            else:
                back_ref[at, :] = back
                copies.append(pltpu.make_async_copy(back_ref.at[at, :], back_refs[0].at[d], sem.at[1, d]))
                copies[-1].start()
        both = dot_tn(jnp.concatenate(parts, axis=0), rows)
        grad_router_ref[...] = both[:LANES] + both[LANES:]
        for copy in copies:
            copy.wait()


def expert_grad_kernel(parts, flat, half_ref, *refs):
    total = None
    for a_ref, b_ref in zip(refs[:parts], refs[parts : 2 * parts]):
        a, b = a_ref[...], b_ref[...]
        product = dot_tn(a.reshape(-1, a.shape[-1]), b)
        total = product if total is None else total + product
    if len(refs) > 2 * parts + 1:
        total = total + refs[2 * parts][...].astype(F32)
    refs[-1][...] = total.astype(BF16)


def join_kernel(odd_ref, mine_ref, other_ref, out_ref):
    own = pl.program_id(0) == odd_ref[0]
    out_ref[...] = jnp.where(own, mine_ref[...], other_ref[...]).astype(F32)


def dense_grad_kernel(n0, n1, g0, g1, m0, m1, b0, b1, small, left_ref, right_ref):
    width = n0.shape[1]
    left_ref[...] = (dot_tn(n0[...], g0[:, : 2 * width]) + dot_tn(n1[...], g1[:, : 2 * width])).astype(BF16)
    right_ref[:, :width] = (dot_tn(n0[...], g0[:, 2 * width :]) + dot_tn(n1[...], g1[:, 2 * width :])).astype(BF16)
    right_ref[:, width : 2 * width] = (dot_tn(m0[...], b0[...]) + dot_tn(m1[...], b1[...])).astype(BF16)
    right_ref[:, 2 * width :] = small[...]


def combine_kernel(out_ref, far_ref, mine_ref, col_ref, hidden_ref, result_ref, pick_ref):
    near, capacity, _ = out_ref.shape
    fill_pick(col_ref, pick_ref, mine_ref[0, 0] // near * near * capacity)
    rows = out_ref[...].reshape(near * capacity, -1)
    summed = dot(pick_ref[...], rows) + far_ref[...].astype(F32)
    result_ref[...] = (hidden_ref[...] + summed).astype(BF16)


def cost(flops, byte_count, transcendentals=0):
    return pl.CostEstimate(flops=int(SCALE * flops), bytes_accessed=int(byte_count), transcendentals=int(transcendentals))


def shaped(shape, dtype):
    return jax.ShapeDtypeStruct(shape, dtype)


def later(kernel, count, ties):
    if not ties:
        return kernel
    return lambda *refs: kernel(*refs[:count], *refs[count + ties :])


def make_strip(base, after):
    heads, width = base.shape
    return pl.pallas_call(
        later(strip_kernel, 1, len(after)),
        in_specs=[VECTOR] + [ANYWHERE] * len(after),
        out_shape=shaped((heads, STRIP, width - STRIP), BF16),
        compiler_params=params(),
        cost_estimate=cost(0, 0),
    )(base, *after)


def place(ids, far_ids, mine, experts, near, capacity):
    length = ids.shape[0]
    row, col = shaped((2, length), jnp.int32), shaped((length, 2), jnp.int32)
    return pl.pallas_call(
        functools.partial(slots_kernel, experts, near, capacity),
        out_shape=(row, row, col, col),
        in_specs=[VECTOR] * 4 + [SCALAR],
        compiler_params=params(),
        cost_estimate=cost(0, 0),
    )(ids.T, ids, far_ids, far_ids.T, mine)


def scatter(near, capacity, *parts, after=()):
    slots = [part[0] for part in parts]
    values = [value for part in parts for value, _ in part[1]]
    picks = [[pick for _, pick in part[1]] for part in parts]
    length, width = slots[0].shape[1], values[0].shape[-1]
    total = near * capacity * len(parts)
    return pl.pallas_call(
        later(functools.partial(scatter_kernel, picks), len(slots) + len(values), len(after)),
        in_specs=[VECTOR] * (len(slots) + len(values)) + [ANYWHERE] * len(after),
        out_shape=shaped((near, capacity * len(parts), width), BF16),
        compiler_params=params(),
        cost_estimate=cost(2 * total * length * width, 6e6),
    )(*slots, *values, *after)


def gather(col, base, blocks, after):
    length, width = col[0].shape[0], blocks.shape[2]
    near, capacity = blocks.shape[0], blocks.shape[1] // 2
    total = near * capacity
    return pl.pallas_call(
        later(gather_kernel, 4, len(after)),
        out_shape=(shaped((length, width), BF16), shaped((length, width), BF16)),
        in_specs=[VECTOR] * 2 + [SCALAR, VECTOR] + [ANYWHERE] * len(after),
        scratch_shapes=[pltpu.VMEM((length, total), BF16), pltpu.VMEM((total, width), BF16)],
        compiler_params=params(),
        cost_estimate=cost(4 * total * length * width, 6e6),
    )(*col, base, blocks, *after)


def forward(m, x, gains, weight, strip, block_row, block_col, row_slots, near, capacity, after):
    _, length, width = x.shape
    heads = width // HEAD
    return pl.pallas_call(
        later(functools.partial(forward_kernel, m), 7, len(after)),
        in_specs=[VECTOR] * 7 + [ANYWHERE] * len(after),
        out_shape=(
            shaped((length, 3 * width), BF16),
            shaped((length, width), BF16),
            shaped((length, LANES), F32),
            shaped((length, width), F32),
            shaped((length, width), BF16),
            shaped((near, capacity, width), BF16),
        ),
        scratch_shapes=[
            pltpu.VMEM((2, length, length), F32), pltpu.VMEM((2, length, length), BF16), pltpu.VMEM((length, length), F32),
        ],
        compiler_params=params(),
        cost_estimate=cost(
            2 * length * width * 4 * width + 8 * heads * length * length * HEAD,
            24e6, heads * length * length,
        ),
    )(x, gains, weight, strip, block_row, block_col, row_slots, *after)


def backward(
    part, own, far, mine, col, cot, hidden, gains, weight, proj, totals, strip, block_row, block_col, x, after
):
    _, length, width = x.shape
    heads = width // HEAD
    near, capacity, _ = own.shape
    total = 2 * near * capacity
    return pl.pallas_call(
        later(functools.partial(backward_kernel, near, part), near + 13, len(after)),
        in_specs=[VECTOR] * (near + 1) + [SCALAR] + [VECTOR] * 11 + [ANYWHERE] * len(after),
        out_shape=(
            shaped((length, width), BF16),
            shaped((length, width), BF16),
            shaped((length, 3 * width), BF16),
            shaped((length, width), BF16),
            shaped((2, width), F32),
            shaped((heads, 2 * length), F32),
        ),
        scratch_shapes=[
            pltpu.VMEM((length, total), BF16),
            pltpu.VMEM((total, width), BF16),
            pltpu.VMEM((length, width), BF16),
            pltpu.VMEM((2, length, length), BF16),
            pltpu.VMEM((2, length, length), BF16),
            pltpu.VMEM((STRIP, 2 * length), F32),
            pltpu.VMEM((2, length, length), F32),
            pltpu.VMEM((2, length, length), F32),
            pltpu.VMEM((length, length), F32),
        ],
        compiler_params=params(),
        cost_estimate=cost(
            2 * length * width * 4 * width + 20 * heads * length * length * HEAD + 2 * total * length * width,
            30e6, heads * length * length,
        ),
    )(*far, own, mine, col, cot, hidden, gains, weight, proj, totals, strip, block_row, block_col, x, *after)


def block_of(count, near, capacity, width, index):
    return pl.BlockSpec((near, capacity, width), lambda f: (0, index, 0), pipeline_mode=pl.Buffered(1))


def expert(kind, part, sent, cots, ids, mine, router, router_turned, first, last, earlier, after):
    (sent, sent_block), (cots, cot_block) = sent, cots
    near, _, width = sent.shape
    experts = ids.shape[1]
    capacity = 3 * ids.shape[2] // experts
    total = near * capacity
    inner = first.shape[1]
    step = 768

    def whole(shape):
        return pl.BlockSpec(shape, lambda f: (0,) * len(shape), pipeline_mode=pl.Buffered(1))

    anywhere = pl.BlockSpec(memory_space=pl.ANY)
    shared = shaped((near, 2 * capacity, width), BF16)
    if kind:
        back_specs = tuple(whole((capacity, width)) for _ in range(near))
        back_shapes = tuple(shaped((capacity, width), BF16) for _ in range(near))
    else:
        back_specs, back_shapes = (anywhere,), (shaped((near, capacity, width), BF16),)
    count = len(back_specs)
    alias = len(earlier)
    targets = (count,)
    outs = pl.pallas_call(
        later(functools.partial(expert_kernel, kind, near, alias, part), 8 + alias, len(after)),
        grid=(inner // step,),
        in_specs=[
            block_of(0, near, capacity, width, sent_block), block_of(0, near, capacity, width, cot_block),
            whole(ids.shape), SCALAR, whole(router.shape), whole(router_turned.shape),
            pl.BlockSpec((width, step), lambda f: (0, f)),
            pl.BlockSpec((step, width), lambda f: (f, 0)),
        ] + [anywhere] * (alias + len(after)),
        out_specs=back_specs + (
            anywhere,
            pl.BlockSpec((total, step), lambda f: (0, f)),
            pl.BlockSpec((total, step), lambda f: (0, f)),
            whole((total, width)), whole((LANES, width)),
        ),
        out_shape=back_shapes + (
            shared,
            shaped((total, inner), BF16), shaped((total, inner), BF16),
            shaped((total, width), BF16), shaped((LANES, width), F32),
        ),
        scratch_shapes=[
            pltpu.VMEM((total, 1), F32),
            pltpu.VMEM((total, 1), jnp.int32),
            pltpu.VMEM((total, width), F32),
            pltpu.VMEM((total, width), F32),
            pltpu.VMEM(ids.shape[1:], jnp.int32),
            pltpu.VMEM(ids.shape[1:], F32),
            pltpu.VMEM((total, width), BF16),
            pltpu.VMEM((total, width), BF16),
            pltpu.SemaphoreType.DMA((2, near)),
        ],
        input_output_aliases={8 + n: target for n, target in enumerate(targets)} if alias else {},
        compiler_params=params(dimension_semantics=("arbitrary",)),
        cost_estimate=cost(8 * total * width * inner, 30e6, total * inner),
    )(sent, cots, ids, mine, router, router_turned, first, last, *earlier, *after)
    backs = list(outs[:count])
    return (backs if kind else backs[0]), outs[count], outs[count + 1 :]


def last_grad(half, acts, scaled, received, after):
    total, inner = acts[0].shape
    width = scaled[0].shape[1]
    step = 512
    count = inner // 2 // step
    out_spec = pl.BlockSpec((step, width), lambda f, half: (f, 0))
    specs = [pl.BlockSpec((total, step), lambda f, half: (0, half[0] * count + f))] * len(acts)
    specs += [pl.BlockSpec((total, width), lambda f, half: (0, 0))] * len(acts)
    extra = [] if received is None else [received]
    return pl.pallas_call(
        later(functools.partial(expert_grad_kernel, len(acts), True), 1 + 2 * len(acts) + len(extra), len(after)),
        grid_spec=pltpu.PrefetchScalarGridSpec(
            num_scalar_prefetch=1, grid=(count,), in_specs=specs + [out_spec] * len(extra) + [ANYWHERE] * len(after),
            out_specs=out_spec
        ),
        out_shape=shaped((inner // 2, width), BF16),
        compiler_params=params(dimension_semantics=("arbitrary",)),
        cost_estimate=cost(len(acts) * total * inner * width, 15e6),
    )(half, *acts, *scaled, *extra, *after)


def first_grad(half, rows, ups, received, after):
    total, inner = ups[0].shape
    near, _, width = rows[0][0].shape
    capacity = total // near
    step = 768
    out_spec = pl.BlockSpec((width // 2, step), lambda f, half: (0, f))

    def row_spec(block):
        return pl.BlockSpec((near, capacity, width // 2), lambda f, half: (0, block, half[0]))

    specs = [row_spec(block) for _, block in rows]
    specs += [pl.BlockSpec((total, step), lambda f, half: (0, f))] * len(ups)
    extra = [] if received is None else [received]
    return pl.pallas_call(
        later(functools.partial(expert_grad_kernel, len(ups), False), 1 + 2 * len(ups) + len(extra), len(after)),
        grid_spec=pltpu.PrefetchScalarGridSpec(
            num_scalar_prefetch=1, grid=(inner // step,), in_specs=specs + [out_spec] * len(extra) + [ANYWHERE] * len(after),
            out_specs=out_spec
        ),
        out_shape=shaped((width // 2, inner), BF16),
        compiler_params=params(dimension_semantics=("arbitrary",)),
        cost_estimate=cost(len(ups) * total * inner * width, 25e6),
    )(half, *[array for array, _ in rows], *ups, *extra, *after)


def join(odd, mine, other, after):
    rows, columns = mine.shape
    step = rows // 3
    own = pl.BlockSpec((step, columns), lambda h, i, odd: (jnp.where(h == odd[0], i, 2 * (1 - h)), 0))
    far = pl.BlockSpec((step, columns), lambda h, i, odd: (jnp.where(h == odd[0], 2 * (1 - h), i), 0))
    return pl.pallas_call(
        later(join_kernel, 3, len(after)),
        grid_spec=pltpu.PrefetchScalarGridSpec(
            num_scalar_prefetch=1, grid=(2, 3), in_specs=[own, far] + [ANYWHERE] * len(after),
            out_specs=pl.BlockSpec((step, columns), lambda h, i, odd: (h * 3 + i, 0)),
        ),
        out_shape=shaped((2 * rows, columns), F32),
        compiler_params=params(dimension_semantics=("arbitrary", "arbitrary")),
        cost_estimate=cost(rows * columns, 20e6),
    )(odd, mine, other, *after)


def dense_grad(*arrays, after):
    small = arrays[-1]
    width = arrays[0].shape[1]
    length = arrays[0].shape[0]
    return pl.pallas_call(
        later(dense_grad_kernel, len(arrays), len(after)),
        in_specs=[VECTOR] * len(arrays) + [ANYWHERE] * len(after),
        out_shape=(shaped((width, 2 * width), BF16), shaped((width, 2 * width + small.shape[1]), BF16)),
        compiler_params=params(),
        cost_estimate=cost(4 * length * width * 4 * width, 20e6),
    )(*arrays, *after)


def combine(out_rows, part, far, mine, col, hidden, after):
    length, width = hidden.shape
    near, capacity = out_rows.shape[0], out_rows.shape[1] // 2
    total = near * capacity
    plain = pl.BlockSpec((length, width), lambda f: (0, 0))
    return pl.pallas_call(
        later(combine_kernel, 5, len(after)),
        grid=(1,),
        in_specs=[
            block_of(0, near, capacity, width, part), plain, SCALAR, pl.BlockSpec(col.shape, lambda f: (0, 0)), plain,
        ] + [ANYWHERE] * len(after),
        out_specs=plain,
        out_shape=shaped((length, width), BF16),
        scratch_shapes=[pltpu.VMEM((length, total), BF16)],
        compiler_params=params(),
        cost_estimate=cost(2 * total * length * width, 6e6),
    )(out_rows, far, mine, col, hidden, *after)


def swap(value, axis, size, bit):
    return lax.ppermute(value, axis, [(i, i ^ bit) for i in range(size)])


def pair_sum(a, b):
    return (a.astype(F32) + b.astype(F32)).astype(BF16)


def halve(value, axis, name, size, bit):
    odd = (lax.axis_index(name) & bit) > 0
    count = value.shape[axis] // 2
    low = lax.slice_in_dim(value, 0, count, axis=axis)
    high = lax.slice_in_dim(value, count, 2 * count, axis=axis)
    kept, sent = jnp.where(odd, high, low), jnp.where(odd, low, high)
    return pair_sum(kept, swap(sent, name, size, bit))


def unite(value, name, size, bit, after=lambda step, value: value):
    odd = (lax.axis_index(name) & bit) > 0
    other = after(20, swap(value, name, size, bit))
    return jnp.concatenate([jnp.where(odd, other, value), jnp.where(odd, value, other)], axis=0)


def dense_sum(left, right, dp, experts, after):
    def split(value):
        return halve(value.reshape(dp // 2, 2, value.shape[0] // dp, value.shape[1]), 1, "dp", dp, 1)[:, 0]

    def along_dp(value):
        bit = 2
        while bit < dp:
            shape = value.shape
            value = halve(value.reshape(shape[0] // 2, 2, *shape[1:]), 1, "dp", dp, bit)[:, 0]
            bit *= 2
        return value

    left, right = split(left), split(right)
    after(-1, left)
    left = after(0, along_dp(left))
    right = halve(right, 1, "expert", experts, 1)
    left = halve(left, 1, "expert", experts, 1)
    right = along_dp(right)
    rows = after(1, jnp.concatenate([left[0], right[0]], axis=1))
    step, bit = 2, 2
    while bit < experts:
        rows = after(step, halve(rows, 0, "expert", experts, bit))
        step, bit = step + 1, bit * 2
    while bit > 1:
        bit //= 2
        rows = unite(rows, "expert", experts, bit, *([after] if bit == 1 else []))
        rows = after({4: 8, 2: 9}.get(bit), rows)
    return rows.astype(F32)


def body(
    dp, experts, inputs, gain_one, w_qkv, w_out, rel_table, second_norm_gain, w_router, w_in, w_back,
    expert_ids, block_ids, cotangent,
):
    micro, length, width = inputs.shape
    capacity = 3 * length // experts
    near = experts // 2
    buckets, heads = rel_table.shape[0] * dp, rel_table.shape[1]
    shard = gain_one.shape[0]
    first_in, last_out = w_in[0], w_back[0]
    mine = lax.axis_index("expert").astype(jnp.int32).reshape(1, 1)

    groups = [list(range(near)), list(range(near, experts))]
    odd = (lax.axis_index("dp") & 1).astype(jnp.int32).reshape(1)

    def cross(value, bit):
        return swap(value, "expert", experts, bit)

    def around(blocks):
        return lax.all_to_all(
            blocks, "expert", split_axis=0, concat_axis=0, axis_index_groups=groups, tiled=True
        )

    def order(*values):
        return lax.optimization_barrier(values)

    middle = length // 2
    cot0_top, cot0_end = cross(cotangent[0, :middle], near), cross(cotangent[0, middle:], near)

    ids_row = jnp.transpose(expert_ids, (0, 2, 1))
    ids_all = lax.all_to_all(
        jnp.broadcast_to(ids_row[None], (experts,) + ids_row.shape), "expert", split_axis=0, concat_axis=0, tiled=True
    )
    ids_all = jnp.transpose(ids_all, (1, 2, 0, 3))
    ids_far = lax.dynamic_index_in_dim(ids_all, lax.axis_index("expert") ^ near, 2, keepdims=False)

    table_column = jnp.pad(rel_table.reshape(-1), (0, shard - rel_table.size))
    small = jnp.concatenate([gain_one[:, None], second_norm_gain[:, None], table_column[:, None], w_router], axis=1)
    extra = jnp.pad(small, ((0, 0), (0, LANES - small.shape[1])))
    bit = 1
    while bit < dp:
        other = swap(extra, "dp", dp, bit)
        high = (lax.axis_index("dp") & bit) > 0
        extra = jnp.concatenate([jnp.where(high, other, extra), jnp.where(high, extra, other)], axis=0)
        bit *= 2
    packed = lax.all_gather(jnp.concatenate([w_qkv, w_out], axis=1), "dp", axis=0, tiled=True)
    gains = extra[:, :2].astype(F32).T
    table = extra[:, 2].reshape(dp, shard)[:, : rel_table.size].reshape(buckets, heads)
    router = jnp.pad(extra[:, 3 : 3 + experts], ((0, 0), (0, LANES - experts)))
    router_turned = jnp.concatenate([router.T, router.T], axis=0)
    levels = bucket_table(length, buckets)
    base = lax.dot_general(
        table, jnp.asarray(levels, BF16), (((0,), (0,)), ((), ())), preferred_element_type=F32
    )
    strip = make_strip(base, [])
    places = [place(expert_ids[m], ids_far[m], mine, experts, near, capacity) for m in range(micro)]

    kept = []
    block_cols = block_ids[:, 0, :].T

    def layer_front(m, after):
        block_row, block_col = block_ids, block_cols
        proj, mixed, totals, hidden, second, send = forward(
            m, inputs, gains, packed, strip, block_row, block_col, places[m][0], near, capacity, after
        )
        kept.append((proj, mixed, totals, hidden, block_row, block_col))
        return second, send

    cot_own = around(
        scatter(near, capacity, (places[0][0], [(cotangent, 0)]), (places[1][0], [(cotangent, 1)]), after=[cot0_top, strip])
    )
    second0, send0 = layer_front(0, [])
    second0_far = cross(second0, near)
    own0 = around(send0)
    second1, send1 = layer_front(1, [send0, cot0_end])
    own1 = around(send1)

    common = (mine, router, router_turned, first_in, last_out)
    cot1_far = cross(order(cotangent[1], second0_far, send1)[0], near)
    second1_far = cross(order(second1, second0_far)[0], near)
    far0_send = scatter(
        near, capacity, (places[0][1], [(cot0_top, None), (cot0_end, None)]), (places[0][1], [(second0_far, None)]),
        after=[send1],
    )
    back0_own, out_own, kept0_own = expert(
        0, 0, (own0, 0), (cot_own, 0), ids_all[0], *common, (), [far0_send]
    )
    far0 = around(order(far0_send, out_own)[0])
    back1_own, out_own, kept1_own = expert(
        0, 1, (own1, 0), (cot_own, 1), ids_all[1], *common, (out_own,), []
    )
    far1_send = scatter(
        near, capacity, (places[1][1], [(cot1_far, None)]), (places[1][1], [(second1_far, None)]), after=[out_own],
    )
    far1 = around(far1_send)
    back0_far, out_far, kept0_far = expert(1, 0, (far0, 1), (far0, 0), ids_all[0], *common, (), [far1_send])
    back1_far, out_far, kept1_far = expert(1, 1, (far1, 1), (far1, 0), ids_all[1], *common, (out_far,), [])
    back0_own, _ = order(back0_own, back0_far[0])
    back0_own, out_far = around(back0_own), around(out_far)
    home = [
        [cross(block, near | d) for d, block in enumerate(back0_far)],
        [cross(block, near | d) for d, block in enumerate(back1_far)],
    ]
    quarter = max(1, near // 4)

    parts = (kept0_own, kept1_own, kept0_far, kept1_far)
    acts, ups, scaled, routers = zip(*parts)
    rows = ((own0, 0), (own1, 0), (far0, 1), (far1, 1))
    grad_router = sum(routers)[:experts].T

    home0, home1 = home
    other = 1 - odd
    last_part = last_grad(other, acts, scaled, None, home0[: 2 * quarter] + [back0_own])
    last_got = swap(last_part, "dp", dp, 1)
    first_part = first_grad(other, rows, ups, None, [last_part] + home0[2 * quarter : 3 * quarter])
    first_got = swap(first_part, "dp", dp, 1)
    last_sum = last_grad(odd, acts, scaled, last_got, [first_part] + home0[3 * quarter :])
    first_sum = first_grad(odd, rows, ups, first_got, [last_sum] + home1[:quarter])
    first_whole = first_sum
    back1_own = around(order(back1_own, first_sum)[0])
    out_own = around(order(out_own, back1_own)[0])
    back_own = [back0_own, back1_own]

    def over_dp(value):
        bit = 2
        while bit < dp:
            other = swap(value, "dp", dp, bit)
            value = pair_sum(value, other)
            bit *= 2
        return value, other

    def pieces(value):
        count = value.shape[0] // 4
        return [value[n * count : (n + 1) * count] for n in range(4)]

    last_sum, last_came = zip(*[over_dp(piece) for piece in pieces(last_sum)])
    first_sum = pieces(first_sum)
    first_sum[:3], first_came = map(list, zip(*[over_dp(piece) for piece in first_sum[:3]]))

    def layer_back(m, after):
        proj, mixed, totals, hidden, block_row, block_col = kept[m]
        return backward(
            m, back_own[m], home[m], mine, places[m][2], cotangent, hidden, gains, packed, proj, totals, strip,
            block_row, block_col, inputs, after,
        )

    back_outs = [layer_back(0, [first_whole, last_came[0]] + home1[quarter : 2 * quarter])]
    out_sums = gather((places[0][3], places[1][3]), mine, out_far, [back_outs[0][1]])
    out0_top, out0_end = cross(out_sums[0][:middle], near), cross(out_sums[0][middle:], near)
    out1_far = cross(out_sums[1], near)
    back_outs.append(layer_back(1, [last_came[1], last_came[2], out_sums[0]]))

    gain_grads = back_outs[0][4] + back_outs[1][4]
    diagonals = back_outs[0][5] + back_outs[1][5]
    table_grad = lax.dot_general(
        jnp.asarray(levels, F32), diagonals, (((1,), (1,)), ((), ())),
        precision=lax.Precision.HIGHEST, preferred_element_type=F32,
    )
    table_grad = jnp.pad(table_grad.reshape(dp, rel_table.size), ((0, 0), (0, shard - rel_table.size)))
    small_grad = jnp.concatenate([gain_grads.T, table_grad.reshape(width, 1), grad_router], axis=1).astype(BF16)
    small_grad = jnp.pad(small_grad, ((0, 0), (0, LANES - small_grad.shape[1])))
    left, right = dense_grad(
        back_outs[0][3], back_outs[1][3], back_outs[0][2], back_outs[1][2],
        kept[0][1], kept[1][1], back_outs[0][1], back_outs[1][1], small_grad,
        after=[last_came[3], *first_came, out0_top, out_own],
    )
    last_sum = jnp.concatenate(last_sum, axis=0)
    grad_last = None

    results, grad_first = [], None

    def after(step, value):
        nonlocal grad_first, grad_last, out0_end, out1_far
        if step == -1:
            grad_last = join(odd, last_sum, swap(last_sum, "dp", dp, 1), [value])
        if step == 1:
            value, grad_last, out0_end, out1_far, *rest = order(value, grad_last, out0_end, out1_far, *first_sum[3:])
            out0_far = jnp.concatenate([out0_top, out0_end], axis=0)
            results.append(combine(out_own, 0, out0_far, mine, places[0][2], kept[0][3], [grad_last]))
            results.append(combine(out_own, 1, out1_far, mine, places[1][2], kept[1][3], [results[0], grad_last]))
            rest, came = zip(*[over_dp(piece) for piece in rest])
            first_sum[3:] = rest
            first_came.extend(came)
        if step == 20:
            whole = jnp.concatenate(first_sum, axis=0)
            grad_first = join(odd, whole, swap(whole, "dp", dp, 1), [results[1]])
            value, grad_first = order(value, grad_first)
        if step == 2:
            value, results[0] = order(value, results[0])
        if step == 3:
            value, results[1] = order(value, results[1])
        if step == 8:
            value, first_came[3] = order(value, first_came[3])
        return value

    dense = dense_sum(left, right, dp, experts, after)
    tail = dense[:, 4 * width :]
    return (
        jnp.stack(results),
        jnp.stack([out[0] for out in back_outs]),
        tail[:, 0],
        dense[:, : 3 * width],
        dense[:, 3 * width : 4 * width],
        tail[: rel_table.size, 2].reshape(rel_table.shape),
        tail[:, 1],
        tail[:, 3 : 3 + experts],
        grad_first[None],
        grad_last[None],
    )


def solution(mesh):
    split = P(None, ("dp", "expert"), None)
    in_specs = (
        split, P("dp"), P("dp", None), P("dp", None), P("dp", None), P("dp"), P("dp", None),
        P("expert", None, None), P("expert", None, None), split, split, split,
    )
    out_specs = (
        split, split, P("dp"), P("dp", None), P("dp", None), P("dp", None), P("dp"), P("dp", None),
        P("expert", None, None), P("expert", None, None),
    )
    return jax.shard_map(
        functools.partial(body, mesh.shape["dp"], mesh.shape["expert"]), mesh=mesh, in_specs=in_specs, out_specs=out_specs, check_vma=False
    )
```

```python
import functools

import jax
import jax.numpy as jnp
import numpy as np
from jax import lax
from jax.experimental import pallas as pl
from jax.experimental.pallas import tpu as pltpu
from jax.sharding import PartitionSpec as P

HEAD = 64
PAIR = 2 * HEAD
STRIP = 128
LANES = 128
VMEM_BYTES = 60 * 1024 * 1024
SCALE = 5
VECTOR = pl.BlockSpec(memory_space=pltpu.VMEM)
SCALAR = pl.BlockSpec(memory_space=pltpu.SMEM)
ANYWHERE = pl.BlockSpec(memory_space=pl.ANY)

epsilon = 1e-06
bucket_edges = (12, 16, 23, 32, 46, 64, 91)
masked_score = -1e30
gelu_a = float(np.sqrt(2.0 / np.pi))
gelu_b = 0.044715

F32 = jnp.float32
BF16 = jnp.bfloat16


def dot(a, b):
    return jnp.dot(a, b, preferred_element_type=F32)


def dot_nt(a, b):
    return lax.dot_general(a, b, (((1,), (1,)), ((), ())), preferred_element_type=F32)


def dot_tn(a, b):
    return lax.dot_general(a, b, (((0,), (0,)), ((), ())), preferred_element_type=F32)


def iota(shape, dim):
    return lax.broadcasted_iota(jnp.int32, shape, dim)


def hot(mask):
    return jnp.where(mask, 1.0, 0.0).astype(BF16)


def params(**extra):
    return pltpu.CompilerParams(vmem_limit_bytes=VMEM_BYTES, **extra)


def bucket_table(length, buckets):
    offset = np.arange(2 * length) - (length - 1)
    distance = np.abs(offset)
    far = 8 + sum((distance >= edge).astype(np.int32) for edge in bucket_edges)
    bucket = np.where(distance < 8, distance, far) + 16 * (offset > 0)
    table = (bucket[None, :] == np.arange(buckets)[:, None]) & (offset < length)[None, :]
    return table.astype(np.float32)


def strip_kernel(base_ref, out_ref):
    heads, width = base_ref.shape
    for h in range(heads):
        row = jnp.broadcast_to(base_ref[h : h + 1, :], (STRIP, width))
        rolled = pltpu.roll(row, width - (STRIP - 1), 1, stride=1, stride_axis=0)
        out_ref[h] = rolled[:, : width - STRIP].astype(BF16)


def slots_kernel(experts, near, capacity, ids_row_ref, ids_col_ref, far_row_ref, far_col_ref, mine_ref, row_ref, row_far_ref, col_ref, col_far_ref):
    length = ids_row_ref.shape[1]
    base = mine_ref[0, 0] // near * near
    padded = max(16, experts)
    before = hot(iota((length, length), 0) < iota((length, length), 1))
    for ids_row, row_out in ((ids_row_ref, row_ref), (far_row_ref, row_far_ref)):
        level = iota((padded, length), 0)
        first, second = ids_row[0:1, :], ids_row[1:2, :]
        place = dot(hot((level == first) | (level == second)), before).astype(jnp.int32)
        block = level - base
        slot = jnp.where((block >= 0) & (block < near), place + block * capacity, -1)
        row_out[0:1, :] = jnp.sum(jnp.where(level == first, slot, 0), axis=0, keepdims=True)
        row_out[1:2, :] = jnp.sum(jnp.where(level == second, slot, 0), axis=0, keepdims=True)

    after = hot(iota((length, length), 1) < iota((length, length), 0))
    for ids_col, col_out in ((ids_col_ref, col_ref), (far_col_ref, col_far_ref)):
        level = iota((length, LANES), 1)
        first, second = ids_col[:, 0:1], ids_col[:, 1:2]
        slot = dot(after, hot((level == first) | (level == second))) + (level * capacity).astype(F32)
        col_out[:, 0:1] = jnp.sum(jnp.where(level == first, slot, 0.0), axis=1, keepdims=True).astype(jnp.int32)
        col_out[:, 1:2] = jnp.sum(jnp.where(level == second, slot, 0.0), axis=1, keepdims=True).astype(jnp.int32)


def scatter_kernel(picks, *refs):
    count = len(picks)
    slots, refs, send_ref = refs[:count], refs[count:-1], refs[-1]
    values = []
    for part in picks:
        values.append([ref if pick is None else ref.at[pick] for pick, ref in zip(part, refs)])
        refs = refs[len(part) :]
    scatter_parts(slots, values, send_ref)


def scatter_parts(slot_refs, value_refs, send_ref):
    near, length = send_ref.shape[0], slot_refs[0].shape[1]
    count = len(slot_refs)
    capacity = send_ref.shape[1] // count
    for n in range(count):
        first, second = slot_refs[n][0:1, :], slot_refs[n][1:2, :]
        values = [ref[...] for ref in value_refs[n]]
        for d in range(near):
            slots = iota((capacity, length), 0) + d * capacity
            pick = hot((slots == first) | (slots == second))
            total, start = None, 0
            for value in values:
                part = dot(pick[:, start : start + value.shape[0]], value)
                total = part if total is None else total + part
                start += value.shape[0]
            send_ref[d, n * capacity : (n + 1) * capacity, :] = total.astype(BF16)


def fill_pick(col_ref, pick_ref, offset=0):
    length, total = pick_ref.shape
    first, second = col_ref[:, 0:1] - offset, col_ref[:, 1:2] - offset
    step = 256
    for start in range(0, total, step):
        slots = iota((length, step), 1) + start
        pick_ref[:, start : start + step] = hot((slots == first) | (slots == second))


def gather_kernel(first_ref, second_ref, mine_ref, blocks_ref, first_sum_ref, second_sum_ref, pick_ref, near_ref):
    near, pair_rows, _ = blocks_ref.shape
    capacity = pair_rows // 2
    offset = mine_ref[0, 0] // near * near * capacity
    for part, (col_ref, sum_ref) in enumerate(((first_ref, first_sum_ref), (second_ref, second_sum_ref))):
        fill_pick(col_ref, pick_ref, offset)
        for d in range(near):
            near_ref[d * capacity : (d + 1) * capacity, :] = blocks_ref[d, part * capacity : (part + 1) * capacity, :]
        sum_ref[...] = dot(pick_ref[...], near_ref[...]).astype(BF16)


def head_mask(length):
    return iota((length, PAIR), 1) < HEAD


def forward_kernel(
    m, x_ref, gains_ref, weight_ref, strip_ref, block_row_ref, block_col_ref, row_ref,
    proj_ref, mixed_ref, total_ref, hidden_ref, second_ref, send_ref,
    score_ref, weight_part_ref, mask_ref,
):
    _, length, width = x_ref.shape
    scale = HEAD ** (-0.5)
    x = x_ref[m].astype(F32)
    r1 = lax.rsqrt(jnp.mean(x * x, axis=1, keepdims=True) + epsilon)
    normed = (x * r1 * gains_ref[0:1, :]).astype(BF16)
    proj_ref[...] = dot(normed, weight_ref[:, : 3 * width]).astype(BF16)
    total_ref[...] = jnp.zeros_like(total_ref)

    mask_ref[...] = jnp.where(block_row_ref[m] <= block_col_ref[:, m : m + 1], 0.0, masked_score)
    lane = iota((STRIP, LANES), 1)

    def pair(p, carry):
        lanes = pl.multiple_of(p * PAIR, PAIR)
        q = proj_ref[:, pl.ds(lanes, PAIR)] * scale
        k = proj_ref[:, pl.ds(width + lanes, PAIR)]
        v = proj_ref[:, pl.ds(2 * width + lanes, PAIR)]
        left = head_mask(length)
        zero = jnp.zeros_like(k)
        keeps = (left, jnp.logical_not(left))
        for h in range(2):
            score_ref[h] = dot_nt(q, jnp.where(keeps[h], k, zero))
        for h in range(2):
            strip = strip_ref[2 * p + h].astype(F32)
            for i in range(length // STRIP):
                rows = slice(i * STRIP, (i + 1) * STRIP)
                start = length - STRIP - i * STRIP
                s = (score_ref[h, rows, :] + strip[:, start : start + length]) + mask_ref[rows, :]
                top = jnp.max(s, axis=1, keepdims=True)
                e = jnp.exp(s - top)
                total = jnp.sum(e, axis=1, keepdims=True)
                weight_part_ref[h, rows, :] = (e * (1.0 / total)).astype(BF16)
                total_ref[rows, :] = jnp.where(lane == 2 * p + h, top + jnp.log(total), total_ref[rows, :])
        out = dot(weight_part_ref[0], jnp.where(keeps[0], v, zero)) + dot(weight_part_ref[1], jnp.where(keeps[1], v, zero))
        mixed_ref[:, pl.ds(lanes, PAIR)] = out.astype(BF16)
        return carry

    lax.fori_loop(0, width // PAIR, pair, 0)
    hidden = x + dot(mixed_ref[...], weight_ref[:, 3 * width : 4 * width])
    hidden_ref[...] = hidden
    r2 = lax.rsqrt(jnp.mean(hidden * hidden, axis=1, keepdims=True) + epsilon)
    second_ref[...] = (hidden * r2 * gains_ref[1:2, :]).astype(BF16)
    scatter_parts([row_ref], [[second_ref]], send_ref)


def backward_kernel(near, part, *refs):
    backward_main(part, refs[:near], *refs[near:])


def backward_main(
    part, far_refs, own_ref, mine_ref, col_ref, cot_ref, hidden_ref, gains_ref, weight_ref, proj_ref, total_ref, strip_ref,
    block_row_ref, block_col_ref, x_ref,
    grad_x_ref, branch_ref, grad_proj_ref, normed_ref, grad_gain_ref, diagonal_ref,
    pick_ref, back_ref, grad_mixed_ref, low_ref, prob_ref, strip_sum_ref, score_ref, grad_prob_ref, mask_ref,
):
    _, length, width = cot_ref.shape
    scale = HEAD ** (-0.5)
    near, capacity, _ = own_ref.shape
    mine = mine_ref[0, 0]
    base = mine // near * near
    for d in range(near):
        own = own_ref[d]
        back_ref[pl.ds(pl.multiple_of((base + d) * capacity, 16), capacity), :] = own
        back_ref[pl.ds(pl.multiple_of((mine ^ (near | d)) * capacity, 16), capacity), :] = far_refs[d][...]
    fill_pick(col_ref, pick_ref)
    grad_second = dot(pick_ref[...], back_ref[...])
    hidden = hidden_ref[...]
    r2 = lax.rsqrt(jnp.mean(hidden * hidden, axis=1, keepdims=True) + epsilon)
    scaled = grad_second * gains_ref[1:2, :]
    inner = jnp.mean(hidden * scaled, axis=1, keepdims=True)
    grad_hidden = cot_ref[part].astype(F32) + r2 * scaled - hidden * (r2 * r2 * r2 * inner)
    grad_gain_ref[1:2, :] = jnp.sum(grad_second * hidden * r2, axis=0, keepdims=True)
    branch = grad_hidden.astype(BF16)
    branch_ref[...] = branch
    grad_mixed_ref[...] = dot_nt(branch, weight_ref[:, 3 * width : 4 * width]).astype(BF16)

    mask_ref[...] = jnp.where(block_row_ref[part] <= block_col_ref[:, part : part + 1], 0.0, masked_score)
    lane = iota((STRIP, LANES), 1)

    def pair(p, carry):
        lanes = pl.multiple_of(p * PAIR, PAIR)
        q = proj_ref[:, pl.ds(lanes, PAIR)]
        k = proj_ref[:, pl.ds(width + lanes, PAIR)]
        v = proj_ref[:, pl.ds(2 * width + lanes, PAIR)]
        g = grad_mixed_ref[:, pl.ds(lanes, PAIR)]
        q_turned = q.astype(F32).T.astype(BF16)
        g_turned = g.astype(F32).T.astype(BF16)
        left = head_mask(length)
        zero = jnp.zeros_like(k)
        keeps = (left, jnp.logical_not(left))
        scaled_q = q * scale
        for h in range(2):
            score_ref[h] = dot_nt(scaled_q, jnp.where(keeps[h], k, zero))
            grad_prob_ref[h] = dot_nt(g, jnp.where(keeps[h], v, zero))
        keys, values = [], []
        for h in range(2):
            strip = strip_ref[2 * p + h].astype(F32)
            strip_sum_ref[...] = jnp.zeros_like(strip_sum_ref)
            for i in range(length // STRIP):
                rows = slice(i * STRIP, (i + 1) * STRIP)
                start = length - STRIP - i * STRIP
                s = (score_ref[h, rows, :] + strip[:, start : start + length]) + mask_ref[rows, :]
                row_total = jnp.sum(jnp.where(lane == 2 * p + h, total_ref[rows, :], 0.0), axis=1, keepdims=True)
                prob = jnp.exp(s - row_total)
                grad_prob = grad_prob_ref[h, rows, :]
                row_inner = jnp.sum(prob * grad_prob, axis=1, keepdims=True)
                grad_score = prob * (grad_prob - row_inner)
                strip_sum_ref[:, start : start + length] += grad_score
                low_ref[h, rows, :] = grad_score.astype(BF16)
                prob_ref[h, rows, :] = prob.astype(BF16)
            half = slice(h * HEAD, (h + 1) * HEAD)
            keys.append(dot(q_turned[half], low_ref[h]))
            values.append(dot(g_turned[half], prob_ref[h]))
            gathered = jnp.zeros((8, 2 * length), F32)
            for a in range(STRIP // 8):
                piece = strip_sum_ref[8 * a : 8 * a + 8, :]
                gathered += pltpu.roll(piece, STRIP - 8 - 8 * a, 1) if a < STRIP // 8 - 1 else piece
            line = gathered[7:8]
            for b in range(7):
                line += pltpu.roll(gathered[b : b + 1], 7 - b, 1)
            diagonal_ref[pl.ds(2 * p + h, 1), :] = line
        grad_query = dot(low_ref[0], jnp.where(keeps[0], k, zero)) + dot(low_ref[1], jnp.where(keeps[1], k, zero))
        grad_proj_ref[:, pl.ds(lanes, PAIR)] = (grad_query * scale).astype(BF16)
        grad_key = jnp.concatenate(keys, axis=0).T
        grad_value = jnp.concatenate(values, axis=0).T
        grad_proj_ref[:, pl.ds(width + lanes, PAIR)] = (grad_key * scale).astype(BF16)
        grad_proj_ref[:, pl.ds(2 * width + lanes, PAIR)] = grad_value.astype(BF16)
        return carry

    lax.fori_loop(0, width // PAIR, pair, 0)
    x = x_ref[part].astype(F32)
    r1 = lax.rsqrt(jnp.mean(x * x, axis=1, keepdims=True) + epsilon)
    normed_ref[...] = (x * r1 * gains_ref[0:1, :]).astype(BF16)
    grad_normed = dot_nt(grad_proj_ref[...], weight_ref[:, : 3 * width])
    scaled = grad_normed * gains_ref[0:1, :]
    inner = jnp.mean(x * scaled, axis=1, keepdims=True)
    grad_gain_ref[0:1, :] = jnp.sum(grad_normed * x * r1, axis=0, keepdims=True)
    grad_x_ref[...] = (grad_hidden + r1 * scaled - x * (r1 * r1 * r1 * inner)).astype(BF16)


def expert_kernel(
    kind, near, alias, part, *refs,
):
    sent_ref, cots_ref, ids_ref, mine_ref, router_ref, router_turned_ref, first_ref, last_ref = refs[:8]
    refs = refs[8 + alias :]
    back_refs, refs = refs[: near if kind else 1], refs[near if kind else 1 :]
    all_ref, act_ref, grad_up_ref, scaled_ref, grad_router_ref = refs[:5]
    gate_ref, other_ref, out_acc, back_acc, slot_ref, partner_ref, out_ref, back_ref, sem = refs[5:]
    step = pl.program_id(0)
    total = scaled_ref.shape[0]
    _, sources, length = ids_ref.shape
    capacity = total // near
    mine = mine_ref[0, 0]
    base = mine // near * near
    tile = total

    @pl.when(step == 0)
    def _():
        first, second = ids_ref[0], ids_ref[1]
        named = (first == mine) | (second == mine)
        before = hot(iota((length, length), 0) < iota((length, length), 1))
        place = dot(hot(named), before).astype(jnp.int32)
        slot_ref[...] = jnp.where(named, place, -1)
        partner_ref[...] = jnp.where(first == mine, second, first).astype(F32)
        for d in range(near):
            at = slice(d * capacity, (d + 1) * capacity)
            source = pl.ds((base + d) ^ (kind * near), 1)
            here = iota((capacity, length), 0) == slot_ref[source, :]
            other_ref[at, :] = jnp.sum(
                jnp.where(here, partner_ref[source, :], 0.0), axis=1, keepdims=True
            ).astype(jnp.int32)
        lane = iota((total, LANES), 1)
        logits = dot(sent_ref[...].reshape(total, -1), router_ref[...])
        gap = jnp.sum(
            jnp.where(lane == mine, logits, 0.0) - jnp.where(lane == other_ref[...], logits, 0.0),
            axis=1, keepdims=True,
        )
        small = jnp.exp(-jnp.abs(gap))
        gate = jnp.where(gap >= 0, 1.0, small) / (1.0 + small)
        gate_ref[...] = gate
        scaled_ref[...] = (gate * cots_ref[...].reshape(total, -1).astype(F32)).astype(BF16)

    first_weight, last_weight = first_ref[...], last_ref[...]
    rows = sent_ref[...].reshape(total, -1)
    scaled = scaled_ref[...]
    up = dot(rows, first_weight)
    grad_act = dot_nt(scaled, last_weight)
    square = up * up
    half = 0.5 * jnp.tanh(up * (gelu_a + (gelu_a * gelu_b) * square)) + 0.5
    act = up * half
    slope = half + (act * (1.0 - half)) * (2 * gelu_a + (6 * gelu_a * gelu_b) * square)
    act_low = act.astype(BF16)
    grad_up = (grad_act * slope).astype(BF16)
    act_ref[...] = act_low
    grad_up_ref[...] = grad_up
    out_part = dot(act_low, last_weight)
    back_part = dot_nt(grad_up, first_weight)

    @pl.when(step == 0)
    def _():
        out_acc[...] = out_part
        back_acc[...] = back_part

    @pl.when(step > 0)
    def _():
        out_acc[...] += out_part
        back_acc[...] += back_part

    @pl.when(step == pl.num_programs(0) - 1)
    def _():
        copies, parts = [], []
        lane = iota((capacity, LANES), 1)
        here = pl.ds(part * capacity, capacity)
        for d in range(near):
            at = slice(d * capacity, (d + 1) * capacity)
            produced = out_acc[at, :].astype(BF16).astype(F32)
            gate = gate_ref[at, :]
            out_ref[at, :] = (gate * produced).astype(BF16)
            copies.append(pltpu.make_async_copy(out_ref.at[at, :], all_ref.at[d, here, :], sem.at[0, d]))
            copies[-1].start()
            grad_gate = jnp.sum(cots_ref[d].astype(F32) * produced, axis=1, keepdims=True)
            share = gate * (1.0 - gate) * grad_gate
            signed = jnp.where(lane == mine, share, 0.0) - jnp.where(lane == other_ref[at, :], share, 0.0)
            high = signed.astype(BF16)
            rest = (signed - high.astype(F32)).astype(BF16)
            parts.append(jnp.concatenate([high, rest], axis=1))
            routed = dot(parts[-1], router_turned_ref[...])
            back = (back_acc[at, :] + routed).astype(BF16)
            if kind:
                for e in range(near):
                    @pl.when((mine % near) ^ d == e)
                    def _():
                        back_refs[e][...] = back
            else:
                back_ref[at, :] = back
                copies.append(pltpu.make_async_copy(back_ref.at[at, :], back_refs[0].at[d], sem.at[1, d]))
                copies[-1].start()
        both = dot_tn(jnp.concatenate(parts, axis=0), rows)
        grad_router_ref[...] = both[:LANES] + both[LANES:]
        for copy in copies:
            copy.wait()


def expert_grad_kernel(parts, flat, half_ref, *refs):
    total = None
    for a_ref, b_ref in zip(refs[:parts], refs[parts : 2 * parts]):
        a, b = a_ref[...], b_ref[...]
        product = dot_tn(a.reshape(-1, a.shape[-1]), b)
        total = product if total is None else total + product
    if len(refs) > 2 * parts + 1:
        total = total + refs[2 * parts][...].astype(F32)
    refs[-1][...] = total.astype(BF16)


def join_kernel(odd_ref, mine_ref, other_ref, out_ref):
    own = pl.program_id(0) == odd_ref[0]
    out_ref[...] = jnp.where(own, mine_ref[...], other_ref[...]).astype(F32)


def left_grad_kernel(n0, n1, g0, g1, left_ref):
    columns = left_ref.shape[1]
    left_ref[...] = (dot_tn(n0[...], g0[:, :columns]) + dot_tn(n1[...], g1[:, :columns])).astype(BF16)


def right_grad_kernel(n0, n1, g0, g1, m0, m1, b0, b1, small, right_ref):
    width = n0.shape[1]
    right_ref[:, :width] = (dot_tn(n0[...], g0[:, 2 * width :]) + dot_tn(n1[...], g1[:, 2 * width :])).astype(BF16)
    right_ref[:, width : 2 * width] = (dot_tn(m0[...], b0[...]) + dot_tn(m1[...], b1[...])).astype(BF16)
    right_ref[:, 2 * width :] = small[...]


def combine_kernel(out_ref, far_ref, mine_ref, col_ref, hidden_ref, result_ref, pick_ref):
    near, capacity, _ = out_ref.shape
    fill_pick(col_ref, pick_ref, mine_ref[0, 0] // near * near * capacity)
    rows = out_ref[...].reshape(near * capacity, -1)
    summed = dot(pick_ref[...], rows) + far_ref[...].astype(F32)
    result_ref[...] = (hidden_ref[...] + summed).astype(BF16)


def cost(flops, byte_count, transcendentals=0):
    return pl.CostEstimate(flops=int(SCALE * flops), bytes_accessed=int(byte_count), transcendentals=int(transcendentals))


def shaped(shape, dtype):
    return jax.ShapeDtypeStruct(shape, dtype)


def later(kernel, count, ties):
    if not ties:
        return kernel
    return lambda *refs: kernel(*refs[:count], *refs[count + ties :])


def make_strip(base, after):
    heads, width = base.shape
    return pl.pallas_call(
        later(strip_kernel, 1, len(after)),
        in_specs=[VECTOR] + [ANYWHERE] * len(after),
        out_shape=shaped((heads, STRIP, width - STRIP), BF16),
        compiler_params=params(),
        cost_estimate=cost(0, 0),
    )(base, *after)


def place(ids, far_ids, mine, experts, near, capacity):
    length = ids.shape[0]
    row, col = shaped((2, length), jnp.int32), shaped((length, 2), jnp.int32)
    return pl.pallas_call(
        functools.partial(slots_kernel, experts, near, capacity),
        out_shape=(row, row, col, col),
        in_specs=[VECTOR] * 4 + [SCALAR],
        compiler_params=params(),
        cost_estimate=cost(0, 0),
    )(ids.T, ids, far_ids, far_ids.T, mine)


def scatter(near, capacity, *parts, after=()):
    slots = [part[0] for part in parts]
    values = [value for part in parts for value, _ in part[1]]
    picks = [[pick for _, pick in part[1]] for part in parts]
    length, width = slots[0].shape[1], values[0].shape[-1]
    total = near * capacity * len(parts)
    return pl.pallas_call(
        later(functools.partial(scatter_kernel, picks), len(slots) + len(values), len(after)),
        in_specs=[VECTOR] * (len(slots) + len(values)) + [ANYWHERE] * len(after),
        out_shape=shaped((near, capacity * len(parts), width), BF16),
        compiler_params=params(),
        cost_estimate=cost(2 * total * length * width, 6e6),
    )(*slots, *values, *after)


def gather(col, base, blocks, after):
    length, width = col[0].shape[0], blocks.shape[2]
    near, capacity = blocks.shape[0], blocks.shape[1] // 2
    total = near * capacity
    return pl.pallas_call(
        later(gather_kernel, 4, len(after)),
        out_shape=(shaped((length, width), BF16), shaped((length, width), BF16)),
        in_specs=[VECTOR] * 2 + [SCALAR, VECTOR] + [ANYWHERE] * len(after),
        scratch_shapes=[pltpu.VMEM((length, total), BF16), pltpu.VMEM((total, width), BF16)],
        compiler_params=params(),
        cost_estimate=cost(4 * total * length * width, 6e6),
    )(*col, base, blocks, *after)


def forward(m, x, gains, weight, strip, block_row, block_col, row_slots, near, capacity, after):
    _, length, width = x.shape
    heads = width // HEAD
    return pl.pallas_call(
        later(functools.partial(forward_kernel, m), 7, len(after)),
        in_specs=[VECTOR] * 7 + [ANYWHERE] * len(after),
        out_shape=(
            shaped((length, 3 * width), BF16),
            shaped((length, width), BF16),
            shaped((length, LANES), F32),
            shaped((length, width), F32),
            shaped((length, width), BF16),
            shaped((near, capacity, width), BF16),
        ),
        scratch_shapes=[
            pltpu.VMEM((2, length, length), F32), pltpu.VMEM((2, length, length), BF16), pltpu.VMEM((length, length), F32),
        ],
        compiler_params=params(),
        cost_estimate=cost(
            2 * length * width * 4 * width + 8 * heads * length * length * HEAD,
            24e6, heads * length * length,
        ),
    )(x, gains, weight, strip, block_row, block_col, row_slots, *after)


def backward(
    part, own, far, mine, col, cot, hidden, gains, weight, proj, totals, strip, block_row, block_col, x, after
):
    _, length, width = x.shape
    heads = width // HEAD
    near, capacity, _ = own.shape
    total = 2 * near * capacity
    return pl.pallas_call(
        later(functools.partial(backward_kernel, near, part), near + 13, len(after)),
        in_specs=[VECTOR] * (near + 1) + [SCALAR] + [VECTOR] * 11 + [ANYWHERE] * len(after),
        out_shape=(
            shaped((length, width), BF16),
            shaped((length, width), BF16),
            shaped((length, 3 * width), BF16),
            shaped((length, width), BF16),
            shaped((2, width), F32),
            shaped((heads, 2 * length), F32),
        ),
        scratch_shapes=[
            pltpu.VMEM((length, total), BF16),
            pltpu.VMEM((total, width), BF16),
            pltpu.VMEM((length, width), BF16),
            pltpu.VMEM((2, length, length), BF16),
            pltpu.VMEM((2, length, length), BF16),
            pltpu.VMEM((STRIP, 2 * length), F32),
            pltpu.VMEM((2, length, length), F32),
            pltpu.VMEM((2, length, length), F32),
            pltpu.VMEM((length, length), F32),
        ],
        compiler_params=params(),
        cost_estimate=cost(
            2 * length * width * 4 * width + 20 * heads * length * length * HEAD + 2 * total * length * width,
            30e6, heads * length * length,
        ),
    )(*far, own, mine, col, cot, hidden, gains, weight, proj, totals, strip, block_row, block_col, x, *after)


def block_of(count, near, capacity, width, index):
    return pl.BlockSpec((near, capacity, width), lambda f: (0, index, 0), pipeline_mode=pl.Buffered(1))


def expert(kind, part, sent, cots, ids, mine, router, router_turned, first, last, earlier, after):
    (sent, sent_block), (cots, cot_block) = sent, cots
    near, _, width = sent.shape
    experts = ids.shape[1]
    capacity = 3 * ids.shape[2] // experts
    total = near * capacity
    inner = first.shape[1]
    step = 768

    def whole(shape):
        return pl.BlockSpec(shape, lambda f: (0,) * len(shape), pipeline_mode=pl.Buffered(1))

    anywhere = pl.BlockSpec(memory_space=pl.ANY)
    shared = shaped((near, 2 * capacity, width), BF16)
    if kind:
        back_specs = tuple(whole((capacity, width)) for _ in range(near))
        back_shapes = tuple(shaped((capacity, width), BF16) for _ in range(near))
    else:
        back_specs, back_shapes = (anywhere,), (shaped((near, capacity, width), BF16),)
    count = len(back_specs)
    alias = len(earlier)
    targets = (count,)
    outs = pl.pallas_call(
        later(functools.partial(expert_kernel, kind, near, alias, part), 8 + alias, len(after)),
        grid=(inner // step,),
        in_specs=[
            block_of(0, near, capacity, width, sent_block), block_of(0, near, capacity, width, cot_block),
            whole(ids.shape), SCALAR, whole(router.shape), whole(router_turned.shape),
            pl.BlockSpec((width, step), lambda f: (0, f)),
            pl.BlockSpec((step, width), lambda f: (f, 0)),
        ] + [anywhere] * (alias + len(after)),
        out_specs=back_specs + (
            anywhere,
            pl.BlockSpec((total, step), lambda f: (0, f)),
            pl.BlockSpec((total, step), lambda f: (0, f)),
            whole((total, width)), whole((LANES, width)),
        ),
        out_shape=back_shapes + (
            shared,
            shaped((total, inner), BF16), shaped((total, inner), BF16),
            shaped((total, width), BF16), shaped((LANES, width), F32),
        ),
        scratch_shapes=[
            pltpu.VMEM((total, 1), F32),
            pltpu.VMEM((total, 1), jnp.int32),
            pltpu.VMEM((total, width), F32),
            pltpu.VMEM((total, width), F32),
            pltpu.VMEM(ids.shape[1:], jnp.int32),
            pltpu.VMEM(ids.shape[1:], F32),
            pltpu.VMEM((total, width), BF16),
            pltpu.VMEM((total, width), BF16),
            pltpu.SemaphoreType.DMA((2, near)),
        ],
        input_output_aliases={8 + n: target for n, target in enumerate(targets)} if alias else {},
        compiler_params=params(dimension_semantics=("arbitrary",)),
        cost_estimate=cost(8 * total * width * inner, 30e6, total * inner),
    )(sent, cots, ids, mine, router, router_turned, first, last, *earlier, *after)
    backs = list(outs[:count])
    return (backs if kind else backs[0]), outs[count], outs[count + 1 :]


def last_grad(half, acts, scaled, received, after):
    total, inner = acts[0].shape
    width = scaled[0].shape[1]
    step = 512
    count = inner // 2 // step
    out_spec = pl.BlockSpec((step, width), lambda f, half: (f, 0))
    specs = [pl.BlockSpec((total, step), lambda f, half: (0, half[0] * count + f))] * len(acts)
    specs += [pl.BlockSpec((total, width), lambda f, half: (0, 0))] * len(acts)
    extra = [] if received is None else [received]
    return pl.pallas_call(
        later(functools.partial(expert_grad_kernel, len(acts), True), 1 + 2 * len(acts) + len(extra), len(after)),
        grid_spec=pltpu.PrefetchScalarGridSpec(
            num_scalar_prefetch=1, grid=(count,), in_specs=specs + [out_spec] * len(extra) + [ANYWHERE] * len(after),
            out_specs=out_spec
        ),
        out_shape=shaped((inner // 2, width), BF16),
        compiler_params=params(dimension_semantics=("arbitrary",)),
        cost_estimate=cost(len(acts) * total * inner * width, 15e6),
    )(half, *acts, *scaled, *extra, *after)


def first_grad(half, rows, ups, received, after):
    total, inner = ups[0].shape
    near, _, width = rows[0][0].shape
    capacity = total // near
    step = 768
    out_spec = pl.BlockSpec((width // 2, step), lambda f, half: (0, f))

    def row_spec(block):
        return pl.BlockSpec((near, capacity, width // 2), lambda f, half: (0, block, half[0]))

    specs = [row_spec(block) for _, block in rows]
    specs += [pl.BlockSpec((total, step), lambda f, half: (0, f))] * len(ups)
    extra = [] if received is None else [received]
    return pl.pallas_call(
        later(functools.partial(expert_grad_kernel, len(ups), False), 1 + 2 * len(ups) + len(extra), len(after)),
        grid_spec=pltpu.PrefetchScalarGridSpec(
            num_scalar_prefetch=1, grid=(inner // step,), in_specs=specs + [out_spec] * len(extra) + [ANYWHERE] * len(after),
            out_specs=out_spec
        ),
        out_shape=shaped((width // 2, inner), BF16),
        compiler_params=params(dimension_semantics=("arbitrary",)),
        cost_estimate=cost(len(ups) * total * inner * width, 25e6),
    )(half, *[array for array, _ in rows], *ups, *extra, *after)


def join(odd, mine, other, after):
    rows, columns = mine.shape
    step = rows // 3
    own = pl.BlockSpec((step, columns), lambda h, i, odd: (jnp.where(h == odd[0], i, 2 * (1 - h)), 0))
    far = pl.BlockSpec((step, columns), lambda h, i, odd: (jnp.where(h == odd[0], 2 * (1 - h), i), 0))
    return pl.pallas_call(
        later(join_kernel, 3, len(after)),
        grid_spec=pltpu.PrefetchScalarGridSpec(
            num_scalar_prefetch=1, grid=(2, 3), in_specs=[own, far] + [ANYWHERE] * len(after),
            out_specs=pl.BlockSpec((step, columns), lambda h, i, odd: (h * 3 + i, 0)),
        ),
        out_shape=shaped((2 * rows, columns), F32),
        compiler_params=params(dimension_semantics=("arbitrary", "arbitrary")),
        cost_estimate=cost(rows * columns, 20e6),
    )(odd, mine, other, *after)


def dense_grad(*arrays, after):
    small = arrays[-1]
    length, width = arrays[0].shape

    def call(kernel, inputs, columns, ties):
        return pl.pallas_call(
            later(kernel, len(inputs), len(ties)),
            in_specs=[VECTOR] * len(inputs) + [ANYWHERE] * len(ties),
            out_shape=shaped((width, columns), BF16),
            compiler_params=params(),
            cost_estimate=cost(4 * length * width * columns, 10e6),
        )(*inputs, *ties)

    left = call(left_grad_kernel, arrays[:4], 2 * width, after)
    return left, call(right_grad_kernel, arrays, 2 * width + small.shape[1], [left])


def combine(out_rows, part, far, mine, col, hidden, after):
    length, width = hidden.shape
    near, capacity = out_rows.shape[0], out_rows.shape[1] // 2
    total = near * capacity
    plain = pl.BlockSpec((length, width), lambda f: (0, 0))
    return pl.pallas_call(
        later(combine_kernel, 5, len(after)),
        grid=(1,),
        in_specs=[
            block_of(0, near, capacity, width, part), plain, SCALAR, pl.BlockSpec(col.shape, lambda f: (0, 0)), plain,
        ] + [ANYWHERE] * len(after),
        out_specs=plain,
        out_shape=shaped((length, width), BF16),
        scratch_shapes=[pltpu.VMEM((length, total), BF16)],
        compiler_params=params(),
        cost_estimate=cost(2 * total * length * width, 6e6),
    )(out_rows, far, mine, col, hidden, *after)


def swap(value, axis, size, bit):
    return lax.ppermute(value, axis, [(i, i ^ bit) for i in range(size)])


def pair_sum(a, b):
    return (a.astype(F32) + b.astype(F32)).astype(BF16)


def halve(value, axis, name, size, bit):
    odd = (lax.axis_index(name) & bit) > 0
    count = value.shape[axis] // 2
    low = lax.slice_in_dim(value, 0, count, axis=axis)
    high = lax.slice_in_dim(value, count, 2 * count, axis=axis)
    kept, sent = jnp.where(odd, high, low), jnp.where(odd, low, high)
    return pair_sum(kept, swap(sent, name, size, bit))


def unite(value, name, size, bit, after=lambda step, value: value):
    odd = (lax.axis_index(name) & bit) > 0
    other = after(20, swap(value, name, size, bit))
    return jnp.concatenate([jnp.where(odd, other, value), jnp.where(odd, value, other)], axis=0)


def dense_sum(left, right, dp, experts, after):
    def split(value):
        return halve(value.reshape(dp // 2, 2, value.shape[0] // dp, value.shape[1]), 1, "dp", dp, 1)[:, 0]

    def along_dp(value):
        bit = 2
        while bit < dp:
            shape = value.shape
            value = halve(value.reshape(shape[0] // 2, 2, *shape[1:]), 1, "dp", dp, bit)[:, 0]
            bit *= 2
        return value

    left, right = split(left), split(right)
    after(-1, left)
    left = after(0, along_dp(left))
    right = halve(right, 1, "expert", experts, 1)
    left = halve(left, 1, "expert", experts, 1)
    right = along_dp(right)
    rows = after(1, jnp.concatenate([left[0], right[0]], axis=1))
    step, bit = 2, 2
    while bit < experts:
        rows = after(step, halve(rows, 0, "expert", experts, bit))
        step, bit = step + 1, bit * 2
    while bit > 1:
        bit //= 2
        rows = unite(rows, "expert", experts, bit, *([after] if bit == 1 else []))
        rows = after({4: 8, 2: 9}.get(bit), rows)
    return rows.astype(F32)


def body(
    dp, experts, inputs, gain_one, w_qkv, w_out, rel_table, second_norm_gain, w_router, w_in, w_back,
    expert_ids, block_ids, cotangent,
):
    micro, length, width = inputs.shape
    capacity = 3 * length // experts
    near = experts // 2
    buckets, heads = rel_table.shape[0] * dp, rel_table.shape[1]
    shard = gain_one.shape[0]
    first_in, last_out = w_in[0], w_back[0]
    mine = lax.axis_index("expert").astype(jnp.int32).reshape(1, 1)

    groups = [list(range(near)), list(range(near, experts))]
    odd = (lax.axis_index("dp") & 1).astype(jnp.int32).reshape(1)

    def cross(value, bit):
        return swap(value, "expert", experts, bit)

    def around(blocks):
        return lax.all_to_all(
            blocks, "expert", split_axis=0, concat_axis=0, axis_index_groups=groups, tiled=True
        )

    def order(*values):
        return lax.optimization_barrier(values)

    middle = length // 2
    cot0_top, cot0_end = cross(cotangent[0, :middle], near), cross(cotangent[0, middle:], near)

    ids_row = jnp.transpose(expert_ids, (0, 2, 1))
    ids_all = lax.all_to_all(
        jnp.broadcast_to(ids_row[None], (experts,) + ids_row.shape), "expert", split_axis=0, concat_axis=0, tiled=True
    )
    ids_all = jnp.transpose(ids_all, (1, 2, 0, 3))
    ids_far = lax.dynamic_index_in_dim(ids_all, lax.axis_index("expert") ^ near, 2, keepdims=False)

    table_column = jnp.pad(rel_table.reshape(-1), (0, shard - rel_table.size))
    small = jnp.concatenate([gain_one[:, None], second_norm_gain[:, None], table_column[:, None], w_router], axis=1)
    extra = jnp.pad(small, ((0, 0), (0, LANES - small.shape[1])))
    bit = 1
    while bit < dp:
        other = swap(extra, "dp", dp, bit)
        high = (lax.axis_index("dp") & bit) > 0
        extra = jnp.concatenate([jnp.where(high, other, extra), jnp.where(high, extra, other)], axis=0)
        bit *= 2
    packed = lax.all_gather(jnp.concatenate([w_qkv, w_out], axis=1), "dp", axis=0, tiled=True)
    gains = extra[:, :2].astype(F32).T
    table = extra[:, 2].reshape(dp, shard)[:, : rel_table.size].reshape(buckets, heads)
    router = jnp.pad(extra[:, 3 : 3 + experts], ((0, 0), (0, LANES - experts)))
    router_turned = jnp.concatenate([router.T, router.T], axis=0)
    levels = bucket_table(length, buckets)
    base = lax.dot_general(
        table, jnp.asarray(levels, BF16), (((0,), (0,)), ((), ())), preferred_element_type=F32
    )
    strip = make_strip(base, [])
    places = [place(expert_ids[m], ids_far[m], mine, experts, near, capacity) for m in range(micro)]

    kept = []
    block_cols = block_ids[:, 0, :].T

    def layer_front(m, after):
        block_row, block_col = block_ids, block_cols
        proj, mixed, totals, hidden, second, send = forward(
            m, inputs, gains, packed, strip, block_row, block_col, places[m][0], near, capacity, after
        )
        kept.append((proj, mixed, totals, hidden, block_row, block_col))
        return second, send

    cot_own = around(
        scatter(near, capacity, (places[0][0], [(cotangent, 0)]), (places[1][0], [(cotangent, 1)]), after=[cot0_top, strip])
    )
    second0, send0 = layer_front(0, [])
    second0_far = cross(second0, near)
    own0 = around(send0)
    second1, send1 = layer_front(1, [send0, cot0_end])
    own1 = around(send1)

    common = (mine, router, router_turned, first_in, last_out)
    cot1_far = cross(order(cotangent[1], second0_far, send1)[0], near)
    second1_far = cross(order(second1, second0_far)[0], near)
    far0_send = scatter(
        near, capacity, (places[0][1], [(cot0_top, None), (cot0_end, None)]), (places[0][1], [(second0_far, None)]),
        after=[send1],
    )
    back0_own, out_own, kept0_own = expert(
        0, 0, (own0, 0), (cot_own, 0), ids_all[0], *common, (), [far0_send]
    )
    far0 = around(order(far0_send, out_own)[0])
    back1_own, out_own, kept1_own = expert(
        0, 1, (own1, 0), (cot_own, 1), ids_all[1], *common, (out_own,), []
    )
    far1_send = scatter(
        near, capacity, (places[1][1], [(cot1_far, None)]), (places[1][1], [(second1_far, None)]), after=[out_own],
    )
    far1 = around(far1_send)
    back0_far, out_far, kept0_far = expert(1, 0, (far0, 1), (far0, 0), ids_all[0], *common, (), [far1_send])
    back1_far, out_far, kept1_far = expert(1, 1, (far1, 1), (far1, 0), ids_all[1], *common, (out_far,), [])
    back0_own, _ = order(back0_own, back0_far[0])
    back0_own, out_far = around(back0_own), around(out_far)
    home = [
        [cross(block, near | d) for d, block in enumerate(back0_far)],
        [cross(block, near | d) for d, block in enumerate(back1_far)],
    ]
    quarter = max(1, near // 4)

    parts = (kept0_own, kept1_own, kept0_far, kept1_far)
    acts, ups, scaled, routers = zip(*parts)
    rows = ((own0, 0), (own1, 0), (far0, 1), (far1, 1))
    grad_router = sum(routers)[:experts].T

    home0, home1 = home
    other = 1 - odd
    last_part = last_grad(other, acts, scaled, None, home0[: 2 * quarter] + [back0_own])
    last_got = swap(last_part, "dp", dp, 1)
    first_part = first_grad(other, rows, ups, None, [last_part] + home0[2 * quarter : 3 * quarter])
    first_got = swap(first_part, "dp", dp, 1)
    last_sum = last_grad(odd, acts, scaled, last_got, [first_part] + home0[3 * quarter :])
    first_sum = first_grad(odd, rows, ups, first_got, [last_sum] + home1[:quarter])
    first_whole = first_sum
    back1_own = around(order(back1_own, first_sum)[0])
    out_own = around(order(out_own, back1_own)[0])
    back_own = [back0_own, back1_own]

    def over_dp(value):
        bit = 2
        while bit < dp:
            other = swap(value, "dp", dp, bit)
            value = pair_sum(value, other)
            bit *= 2
        return value, other

    def pieces(value):
        count = value.shape[0] // 4
        return [value[n * count : (n + 1) * count] for n in range(4)]

    last_sum, last_came = zip(*[over_dp(piece) for piece in pieces(last_sum)])
    first_sum = pieces(first_sum)
    first_sum[:3], first_came = map(list, zip(*[over_dp(piece) for piece in first_sum[:3]]))

    def layer_back(m, after):
        proj, mixed, totals, hidden, block_row, block_col = kept[m]
        return backward(
            m, back_own[m], home[m], mine, places[m][2], cotangent, hidden, gains, packed, proj, totals, strip,
            block_row, block_col, inputs, after,
        )

    back_outs = [layer_back(0, [first_whole, last_came[0]] + home1[quarter : 2 * quarter])]
    out_sums = gather((places[0][3], places[1][3]), mine, out_far, [back_outs[0][1]])
    out0_top, out0_end = cross(out_sums[0][:middle], near), cross(out_sums[0][middle:], near)
    out1_far = cross(out_sums[1], near)
    back_outs.append(layer_back(1, [last_came[1], last_came[2], out_sums[0]]))

    gain_grads = back_outs[0][4] + back_outs[1][4]
    diagonals = back_outs[0][5] + back_outs[1][5]
    table_grad = lax.dot_general(
        jnp.asarray(levels, F32), diagonals, (((1,), (1,)), ((), ())),
        precision=lax.Precision.HIGHEST, preferred_element_type=F32,
    )
    table_grad = jnp.pad(table_grad.reshape(dp, rel_table.size), ((0, 0), (0, shard - rel_table.size)))
    small_grad = jnp.concatenate([gain_grads.T, table_grad.reshape(width, 1), grad_router], axis=1).astype(BF16)
    small_grad = jnp.pad(small_grad, ((0, 0), (0, LANES - small_grad.shape[1])))
    left, right = dense_grad(
        back_outs[0][3], back_outs[1][3], back_outs[0][2], back_outs[1][2],
        kept[0][1], kept[1][1], back_outs[0][1], back_outs[1][1], small_grad,
        after=[last_came[3], *first_came, out0_top, out_own],
    )
    last_sum = jnp.concatenate(last_sum, axis=0)
    grad_last = None

    results, grad_first = [], None

    def after(step, value):
        nonlocal grad_first, grad_last, out0_end, out1_far
        if step == -1:
            grad_last = join(odd, last_sum, swap(last_sum, "dp", dp, 1), [value])
        if step == 1:
            value, grad_last, out0_end, out1_far, *rest = order(value, grad_last, out0_end, out1_far, *first_sum[3:])
            out0_far = jnp.concatenate([out0_top, out0_end], axis=0)
            results.append(combine(out_own, 0, out0_far, mine, places[0][2], kept[0][3], [grad_last]))
            results.append(combine(out_own, 1, out1_far, mine, places[1][2], kept[1][3], [results[0], grad_last]))
            rest, came = zip(*[over_dp(piece) for piece in rest])
            first_sum[3:] = rest
            first_came.extend(came)
        if step == 20:
            whole = jnp.concatenate(first_sum, axis=0)
            grad_first = join(odd, whole, swap(whole, "dp", dp, 1), [results[1]])
            value, grad_first = order(value, grad_first)
        if step == 2:
            value, results[0] = order(value, results[0])
        if step == 3:
            value, results[1] = order(value, results[1])
        if step == 8:
            value, first_came[3] = order(value, first_came[3])
        return value

    dense = dense_sum(left, right, dp, experts, after)
    tail = dense[:, 4 * width :]
    return (
        jnp.stack(results),
        jnp.stack([out[0] for out in back_outs]),
        tail[:, 0],
        dense[:, : 3 * width],
        dense[:, 3 * width : 4 * width],
        tail[: rel_table.size, 2].reshape(rel_table.shape),
        tail[:, 1],
        tail[:, 3 : 3 + experts],
        grad_first[None],
        grad_last[None],
    )


def solution(mesh):
    split = P(None, ("dp", "expert"), None)
    in_specs = (
        split, P("dp"), P("dp", None), P("dp", None), P("dp", None), P("dp"), P("dp", None),
        P("expert", None, None), P("expert", None, None), split, split, split,
    )
    out_specs = (
        split, split, P("dp"), P("dp", None), P("dp", None), P("dp", None), P("dp"), P("dp", None),
        P("expert", None, None), P("expert", None, None),
    )
    return jax.shard_map(
        functools.partial(body, mesh.shape["dp"], mesh.shape["expert"]), mesh=mesh, in_specs=in_specs, out_specs=out_specs, check_vma=False
    )
```
